128 devices in a mesh: pipe: 2 (over core), dp: 16 (over x, z), head: 4 (over y).
Axes of the slice: x: 4, y: 4, z: 4, core: 2. Of those that a mesh axis runs over, the one named last changes fastest.
Arguments:
- clips_in: bfloat16 [4, 16, 400, 384], P(None, 'dp'), may hold values from -6 to 6
- cotangent: bfloat16 [4, 16, 100, 768], P(None, 'dp'), may hold values from -6 to 6
- token_mask: int32 [4, 16, 400], P(None, 'dp'), may hold values from 0 to 1, as said below
- memory_valid: int32 [4, 16, 2], P(None, 'dp'), may hold values 0 or 1
- memory_one: bfloat16 [4, 16, 2, 50, 384], P(None, 'dp', None, None, 'head'), may hold values from -6 to 6
- memory_two: bfloat16 [4, 16, 2, 50, 768], P(None, 'dp', None, None, 'head'), may hold values from -6 to 6
- qkv_one: bfloat16 [384, 4, 288], P('dp', 'head'), may hold values from -0.3125 to 0.3125
- out_one: bfloat16 [384, 384], P('head', 'dp'), may hold values from -0.3125 to 0.3125
- up_one: bfloat16 [384, 1536], P('dp', 'head'), may hold values from -0.3125 to 0.3125
- down_one: bfloat16 [1536, 384], P('head', 'dp'), may hold values from -0.15625 to 0.15625
- up_bias_one: float32 [1536], P('head'), may hold values from -3 to 3
- gains_one: float32 [2, 384], replicated, may hold values from 0.1 to 1.9
- shifts_one: float32 [4, 384], replicated, may hold values from -1.5 to 1.5
- qkv_two: bfloat16 [384, 8, 288], P('dp', 'head'), may hold values from -0.3125 to 0.3125
- out_two: bfloat16 [768, 768], P('head', 'dp'), may hold values from -0.21875 to 0.21875
- res_two: bfloat16 [384, 768], P('head', 'dp'), may hold values from -0.3125 to 0.3125
- up_two: bfloat16 [768, 3072], P('dp', 'head'), may hold values from -0.21875 to 0.21875
- down_two: bfloat16 [3072, 768], P('head', 'dp'), may hold values from -0.109375 to 0.109375
- up_bias_two: float32 [3072], P('head'), may hold values from -3 to 3
- gain_two_in: float32 [384], replicated, may hold values from 0.1 to 1.9
- shift_two_in: float32 [384], replicated, may hold values from -1.5 to 1.5
- gains_two: float32 [768], replicated, may hold values from 0.1 to 1.9
- shifts_two: float32 [3, 768], replicated, may hold values from -1.5 to 1.5
Outputs:
- activations: bfloat16 [4, 16, 100, 768], P('pipe', 'dp')
- input_grad: bfloat16 [4, 16, 400, 384], P('pipe', 'dp')
- grad_qkv_one: float32 [384, 4, 288], P(('pipe', 'dp'), 'head')
- grad_out_one: float32 [384, 384], P('head', ('pipe', 'dp'))
- grad_up_one: float32 [384, 1536], P(('pipe', 'dp'), 'head')
- grad_down_one: float32 [1536, 384], P('head', ('pipe', 'dp'))
- grad_up_bias_one: float32 [1536], P('head')
- grad_gains_one: float32 [2, 384], replicated
- grad_shifts_one: float32 [4, 384], replicated
- grad_qkv_two: float32 [384, 8, 288], P(('pipe', 'dp'), 'head')
- grad_out_two: float32 [768, 768], P('head', ('pipe', 'dp'))
- grad_res_two: float32 [384, 768], P('head', ('pipe', 'dp'))
- grad_up_two: float32 [768, 3072], P(('pipe', 'dp'), 'head')
- grad_down_two: float32 [3072, 768], P('head', ('pipe', 'dp'))
- grad_up_bias_two: float32 [3072], P('head')
- grad_gain_two_in: float32 [384], replicated
- grad_shift_two_in: float32 [384], replicated
- grad_gains_two: float32 [768], replicated
- grad_shifts_two: float32 [3, 768], replicated
The draws below stay inside these ranges and needn't reach their ends.
Inputs may be any that keep to these rules, and one draw needn't show every extreme that they name: `token_mask`: in every clip the ones form the same top-left square of side 14 or 20 in each frame (tokens ordered frame, row, column on a 20 by 20 grid); both sides occur in every draw.
All inputs are finite; a program needn't handle non-finite values. No bound on the sum of `memory_valid` on one device may be relied on, other than what follows from the above.
Results may differ from the reference program's by a relative error of at most 0.029.
Values may be sent and summed in bfloat16 or wider, within the bound.
No kernel may reach another device: no remote copies, remote signals or barrier semaphores. Data moves between devices by JAX's collectives and lax.ppermute only.
A program may use at most 192 MiB of HBM per device.

```python
import jax
import jax.numpy as jnp
from jax import lax

WIDTH = 384
HEADS_ONE = 4
HEAD_DIM = 96
HIDDEN_ONE = 1536
WIDTH_TWO = 768
HEADS_TWO = 8
HIDDEN_TWO = 3072
GRID = 20
SMALL_SIDE = 14
MICRO = 4
TOK = 400
POOLED = 100
MEMKEYS = 50
CLIPS = 16


def draw_token_mask(key, part):
    key = jax.random.fold_in(key, 7)
    larger = jax.random.randint(key, (MICRO, CLIPS), 0, 2)
    larger = larger.at[0, 0].set(1)
    larger = larger.at[MICRO - 1, CLIPS - 1].set(0)
    side_size = SMALL_SIDE + (GRID - SMALL_SIDE) * larger
    places = jnp.arange(TOK, dtype=jnp.int32)
    row_index = places // GRID % GRID
    col_index = places % GRID
    inside = (row_index[None, None, :] < side_size[:, :, None]) & (col_index[None, None, :] < side_size[:, :, None])
    return inside.astype(jnp.int32)


def with_ends(drawn, stream_key, smallest, top_value):
    longest = drawn.shape.index(max(drawn.shape))
    spots = []
    for shift in (0, 1):
        where = [jax.random.randint(jax.random.fold_in(stream_key, axis), (), 0, length) for axis, length in enumerate(drawn.shape)]
        where[longest] = (where[longest] + shift) % drawn.shape[longest]
        spots.append(tuple(where))
    return drawn.at[spots[0]].set(smallest).at[spots[1]].set(top_value)


def block_levels(key, shape, shards, least, high):
    def one(axis_at, parts):
        draws = jax.random.uniform(jax.random.fold_in(jax.random.fold_in(key, 6), axis_at), (parts,), jnp.float32, least / len(shards), high / len(shards))
        return jnp.repeat(jnp.exp(draws), shape[axis_at] // parts).reshape((-1,) + (1,) * (len(shape) - axis_at - 1))

    level = one(*shards[0])
    for cut in shards[1:]:
        level = level * one(*cut)
    return level


def normal_values(key, shape, width, bound, pieces=(), kind=jnp.bfloat16):
    level = block_levels(key, shape, pieces, -0.22, 0.18) if pieces else 1.0
    drawn = jax.random.normal(key, shape, jnp.float32) * width * level
    return jnp.minimum(jnp.maximum(drawn, -bound), bound).astype(kind)


def setup_inputs(seed: int = 0) -> dict:
    keys = jax.random.split(jax.random.key(seed), 24)
    clips_in = normal_values(keys[0], (MICRO, CLIPS, TOK, WIDTH), 1.0, 6.0, ((1, 16),))
    cotangent = normal_values(keys[1], (MICRO, CLIPS, POOLED, WIDTH_TWO), 1.0, 6.0, ((1, 16),))
    token_mask = draw_token_mask(jax.random.fold_in(keys[23], 71), 0)
    memory_valid = with_ends((jax.random.randint(keys[3], (MICRO, CLIPS, 2), 0, 4) < 3).astype(jnp.int32), jax.random.fold_in(keys[3], 1), 0, 1)
    memory_one = normal_values(keys[4], (MICRO, CLIPS, 2, MEMKEYS, WIDTH), 1.0, 6.0, ((1, 16), (4, 4)))
    memory_two = normal_values(keys[5], (MICRO, CLIPS, 2, MEMKEYS, WIDTH_TWO), 1.0, 6.0, ((1, 16), (4, 4)))
    qkv_one = normal_values(keys[6], (WIDTH, HEADS_ONE, 3 * HEAD_DIM), WIDTH ** -0.5, 0.3125, ((0, 16), (1, 4)))
    out_one = normal_values(keys[7], (WIDTH, WIDTH), WIDTH ** -0.5, 0.3125, ((0, 4), (1, 16)))
    up_one = normal_values(keys[8], (WIDTH, HIDDEN_ONE), WIDTH ** -0.5, 0.3125, ((0, 16), (1, 4)))
    down_one = normal_values(keys[9], (HIDDEN_ONE, WIDTH), HIDDEN_ONE ** -0.5, 0.15625, ((0, 4), (1, 16)))
    up_bias_one = normal_values(keys[10], (HIDDEN_ONE,), 0.5, 3.0, ((0, 4),), jnp.float32)
    gains_one = jnp.clip(1.0 + 0.18 * jax.random.normal(keys[11], (2, WIDTH), jnp.float32), 0.1, 1.9)
    shifts_one = normal_values(keys[12], (4, WIDTH), 0.3, 1.5, (), jnp.float32)
    qkv_two = normal_values(keys[13], (WIDTH, HEADS_TWO, 3 * HEAD_DIM), WIDTH ** -0.5, 0.3125, ((0, 16), (1, 4)))
    out_two = normal_values(keys[14], (WIDTH_TWO, WIDTH_TWO), WIDTH_TWO ** -0.5, 0.21875, ((0, 4), (1, 16)))
    res_two = normal_values(keys[15], (WIDTH, WIDTH_TWO), WIDTH ** -0.5, 0.3125, ((0, 4), (1, 16)))
    up_two = normal_values(keys[16], (WIDTH_TWO, HIDDEN_TWO), WIDTH_TWO ** -0.5, 0.21875, ((0, 16), (1, 4)))
    down_two = normal_values(keys[17], (HIDDEN_TWO, WIDTH_TWO), HIDDEN_TWO ** -0.5, 0.109375, ((0, 4), (1, 16)))
    up_bias_two = normal_values(keys[18], (HIDDEN_TWO,), 0.5, 3.0, ((0, 4),), jnp.float32)
    gain_two_in = jnp.clip(1.0 + 0.18 * jax.random.normal(keys[19], (WIDTH,), jnp.float32), 0.1, 1.9)
    shift_two_in = normal_values(keys[20], (WIDTH,), 0.3, 1.5, (), jnp.float32)
    gains_two = jnp.clip(1.0 + 0.18 * jax.random.normal(keys[21], (WIDTH_TWO,), jnp.float32), 0.1, 1.9)
    shifts_two = normal_values(keys[22], (3, WIDTH_TWO), 0.3, 1.5, (), jnp.float32)
    return {"clips_in": clips_in, "cotangent": cotangent, "token_mask": token_mask, "memory_valid": memory_valid, "memory_one": memory_one, "memory_two": memory_two, "qkv_one": qkv_one, "out_one": out_one, "up_one": up_one, "down_one": down_one, "up_bias_one": up_bias_one, "gains_one": gains_one, "shifts_one": shifts_one, "qkv_two": qkv_two, "out_two": out_two, "res_two": res_two, "up_two": up_two, "down_two": down_two, "up_bias_two": up_bias_two, "gain_two_in": gain_two_in, "shift_two_in": shift_two_in, "gains_two": gains_two, "shifts_two": shifts_two}


@jax.custom_vjp
def low(v):
    return lax.optimization_barrier(v.astype(jnp.bfloat16)).astype(jnp.float32)

@jax.custom_vjp
def low_back(v):
    return v

def low_keep(v):
    return (low(v), None)

def low_pass(kept, grad):
    return (grad,)

def back_keep(v):
    return (v, None)

def back_low(kept, grad):
    return (low(grad),)
low.defvjp(low_keep, low_pass)
low_back.defvjp(back_keep, back_low)
exact = lax.Precision.HIGHEST
small_eps = 1e-06

def layer_norm(values, gain, shift):
    average = lax.optimization_barrier(jnp.mean(values, axis=-1, keepdims=True))
    centred = values - average
    variance = lax.optimization_barrier(jnp.mean(centred * centred, axis=-1, keepdims=True))
    return centred * lax.rsqrt(variance + small_eps) * gain + shift

def pool_grid(values):
    half_side = GRID // 2
    frame_count = values.shape[0] // (GRID * GRID)
    shaped = values.reshape(frame_count, half_side, 2, half_side, 2, values.shape[-1])
    return lax.optimization_barrier(jnp.mean(shaped, axis=(2, 4))).reshape(frame_count * half_side * half_side, values.shape[-1])

def pool_valid(flags):
    half_side = GRID // 2
    frame_count = flags.shape[-1] // (GRID * GRID)
    shaped = flags.reshape(frame_count, half_side, 2, half_side, 2)
    return shaped[:, :, 0, :, 0].reshape(frame_count * half_side * half_side) > 0

def block(inputs, weights, params, key_ok, memory, memory_ok, second):
    w_qkv, w_out, w_res, w_up, w_down = weights
    gain_in, shift_in, gain_mid, shift_mid, bias_out, bias_down, bias_up = params
    normed = layer_norm(inputs, gain_in, shift_in)
    joined = low_back(jnp.einsum('nc,chd->nhd', low(normed), w_qkv, precision=exact))
    token_count, head_count, triple = joined.shape
    head_width = triple // 3

    def squeeze(member):
        return pool_grid(member.reshape(token_count, head_count * head_width)).reshape(-1, head_count, head_width)
    queries = joined[..., :head_width]
    if second:
        queries = squeeze(queries)
    queries = low(queries)
    key_rows = low(squeeze(joined[..., head_width:2 * head_width]))
    value_rows = low(squeeze(joined[..., 2 * head_width:]))
    key_all = jnp.concatenate([key_rows, memory[0]], axis=0)
    value_all = jnp.concatenate([value_rows, memory[1]], axis=0)
    ok_all = jnp.concatenate([key_ok, memory_ok])
    scores = low_back(jnp.einsum('qhd,khd->hqk', queries, key_all, precision=exact) * head_width ** (-0.5))
    scores = jnp.where(ok_all[None, None, :], scores, -1000000000.0)
    shares = low(jax.nn.softmax(scores, axis=-1))
    mixture = jnp.einsum('hqk,khd->qhd', shares, value_all, precision=exact) + queries
    mixture = low(low_back(mixture))
    branch = jnp.dot(mixture.reshape(mixture.shape[0], -1), w_out, precision=exact)
    if second:
        branch = branch + jnp.dot(low(pool_grid(normed)), w_res, precision=exact)
        middle = bias_out + low_back(branch)
    else:
        middle = inputs + bias_out + low_back(branch)
    normed_mid = low(layer_norm(middle, gain_mid, shift_mid))
    hidden = low_back(jnp.dot(normed_mid, w_up, precision=exact) + bias_up)
    active = low(jax.nn.gelu(hidden, approximate=False))
    return middle + bias_down + jnp.dot(active, w_down, precision=exact)

def add_pair(left_tree, right_tree):
    return left_tree + right_tree

def reference(clips_in, cotangent, token_mask, memory_valid, memory_one, memory_two, qkv_one, out_one, up_one, down_one, up_bias_one, gains_one, shifts_one, qkv_two, out_two, res_two, up_two, down_two, up_bias_two, gain_two_in, shift_two_in, gains_two, shifts_two):
    pack = tuple((array.astype(jnp.float32) for array in (qkv_one, out_one, up_one, down_one, up_bias_one, gains_one, shifts_one, qkv_two, out_two, res_two, up_two, down_two, up_bias_two, gain_two_in, shift_two_in, gains_two, shifts_two)))
    item_count = MICRO * CLIPS
    sources = clips_in.astype(jnp.float32).reshape(item_count, TOK, WIDTH)
    cotangents = cotangent.astype(jnp.float32).reshape(item_count, POOLED, WIDTH_TWO)
    flags = token_mask.reshape(item_count, TOK)
    valids = memory_valid.reshape(item_count, 2)
    memories_one = memory_one.astype(jnp.float32).reshape(item_count, 2, MEMKEYS, HEADS_ONE, HEAD_DIM)
    memories_two = memory_two.astype(jnp.float32).reshape(item_count, 2, MEMKEYS, HEADS_TWO, HEAD_DIM)

    def step(totals, entry):
        source, cot_rows, flag_rows, valid_rows, memory_first, memory_second = entry
        key_ok = pool_valid(flag_rows)
        memory_ok = jnp.repeat(valid_rows > 0, MEMKEYS // 2)

        def forward(params, inputs):
            first_out = block(inputs, (params[0], params[1], None, params[2], params[3]), (params[5][0], params[6][0], params[5][1], params[6][1], params[6][2], params[6][3], params[4]), key_ok, memory_first, memory_ok, False)
            passed = low(low_back(first_out))
            return block(passed, (params[7], params[8], params[9], params[10], params[11]), (params[13], params[14], params[15], params[16][0], params[16][1], params[16][2], params[12]), key_ok, memory_second, memory_ok, True)
        output, pull = jax.vjp(forward, pack, source)
        grad_params, grad_source = pull(cot_rows * key_ok[:, None].astype(jnp.float32))
        totals = jax.tree.map(add_pair, totals, grad_params)
        return (totals, (output, grad_source))
    totals, (outputs, grad_sources) = lax.scan(step, jax.tree.map(jnp.zeros_like, pack), (sources, cotangents, flags, valids, memories_one, memories_two))
    return (outputs.reshape(MICRO, CLIPS, POOLED, WIDTH_TWO).astype(jnp.bfloat16), grad_sources.reshape(MICRO, CLIPS, TOK, WIDTH).astype(jnp.bfloat16), totals[0], totals[1], totals[2], totals[3], totals[4], totals[5], totals[6], totals[7], totals[8], totals[9], totals[10], totals[11], totals[12], totals[13], totals[14], totals[15], totals[16])
```

```python
import functools

import jax
import jax.numpy as jnp
import numpy as np
from jax import lax
from jax.experimental import pallas as pl
from jax.experimental.pallas import tpu as pltpu
from jax.sharding import PartitionSpec as P

F32 = jnp.float32
BF16 = jnp.bfloat16
GRID = 20
TOK = 400
WIN = 100
PW = 104
PT = 4 * PW
KEYS = 256
MEM0 = 112
MEMROWS = 50
HEAD = 96
EPS = 1e-06
MASKED = -1000000000.0
ABSENT = -3e38
SCALE = HEAD ** (-0.5)
VMEM_LIMIT = 56 * 1024 * 1024


def nn(a, b):
    return lax.dot_general(a, b, (((1,), (0,)), ((), ())), preferred_element_type=F32)


def nt(a, b):
    return lax.dot_general(a, b, (((1,), (1,)), ((), ())), preferred_element_type=F32)


def tn(a, b):
    return lax.dot_general(a, b, (((0,), (0,)), ((), ())), preferred_element_type=F32)


def thirds(v):
    high = v.astype(BF16)
    rest = v - high.astype(F32)
    mid = rest.astype(BF16)
    low = (rest - mid.astype(F32)).astype(BF16)
    return high, mid, low


def exact_nn(v, m):
    a, b, c = thirds(v)
    return nn(a, m) + nn(b, m) + nn(c, m)


def exact_nt(v, m):
    a, b, c = thirds(v)
    return nt(a, m) + nt(b, m) + nt(c, m)


def normalise(v):
    average = jnp.mean(v, axis=-1, keepdims=True)
    centred = v - average
    variance = jnp.mean(centred * centred, axis=-1, keepdims=True)
    inverse = lax.rsqrt(variance + EPS)
    return centred * inverse, inverse


def normalise_back(grad, unit, inverse, gain):
    scaled = grad * gain
    mean_one = jnp.mean(scaled, axis=-1, keepdims=True)
    mean_two = jnp.mean(scaled * unit, axis=-1, keepdims=True)
    return inverse * (scaled - mean_one - unit * mean_two)


def column_sum(v):
    return jnp.sum(v, axis=0, keepdims=True)


def gelu_both(h):
    cdf = 0.5 + 0.5 * lax.erf(h * 0.7071067811865476)
    density = 0.3989422804014327 * jnp.exp(-0.5 * h * h)
    return h * cdf, cdf + h * density


def pool_rows(v):
    return 0.25 * (v[0:PW] + v[PW : 2 * PW] + v[2 * PW : 3 * PW] + v[3 * PW : 4 * PW])


def softmax_rows(scores, ok, fill):
    scores = jnp.where(ok > 0, scores * SCALE, fill)
    peak = jnp.max(scores, axis=-1, keepdims=True)
    expos = jnp.exp(scores - peak)
    return expos / jnp.sum(expos, axis=-1, keepdims=True)


def attend_back(q, keys, values, ok, fill, dmix):
    shares = softmax_rows(nt(q, keys), ok, fill)
    dvalues = tn(shares.astype(BF16), dmix)
    dshares = nt(dmix, values)
    inner = jnp.sum(shares * dshares, axis=-1, keepdims=True)
    dscores = (shares * (dshares - inner)).astype(BF16)
    dq = nn(dscores, keys) * SCALE + dmix.astype(F32)
    dkeys = tn(dscores, q) * SCALE
    return dq, dkeys, dvalues


def start_all(copies):
    for copy in copies:
        copy.start()


def wait_all(copies):
    for copy in copies:
        copy.wait()


def weight_copies(flag, wanted, mine, other, dst, cols, sem):
    first_cols = mine[0].shape[1]

    def copies(group):
        out = []
        for r in range(4):
            out.append(pltpu.make_async_copy(group[r], dst.at[r, :, pl.ds(0, first_cols)], sem))
        for r in range(4):
            out.append(
                pltpu.make_async_copy(
                    group[4 + r],
                    dst.at[:, pl.ds(r * 96, 96), pl.ds(first_cols, cols - first_cols)],
                    sem,
                )
            )
        return out

    @pl.when(flag == wanted)
    def _():
        start_all(copies(mine))

    @pl.when(flag != wanted)
    def _():
        start_all(copies(other))

    return copies(mine)


def put_grad(outs_a, outs_b, r, lo, value):
    width = outs_a[0].shape[1]
    cols = value.shape[1]
    value = value.astype(BF16)
    if lo + cols <= width:
        outs_a[r][:, lo : lo + cols] = value
    elif lo >= width:
        for k in range(4):
            outs_b[k][r, :, lo - width : lo - width + cols] = value[k * 48 : (k + 1) * 48]
    else:
        put_grad(outs_a, outs_b, r, lo, value[:, : width - lo])
        put_grad(outs_a, outs_b, r, width, value[:, width - lo :])


def first_forward(
    place, x, token_perm, p1, vec384, ok, fill, mem, bias_up, *rest
):
    mine, other = rest[0:8], rest[8:16]
    passed, x_out, q_out, k_out, v_out, mix_out, mid_out, act_out, slope_out = rest[16:25]
    weights, gains, sem = rest[25:28]
    waits = weight_copies(place[0], 0, mine, other, weights, 1152, sem)
    gains[...] = exact_nn(vec384[...], p1[...])
    xb = nn(x[...], p1[...]).astype(BF16)
    xb = nn(token_perm[...], xb).astype(BF16)
    x_out[...] = xb
    xf = xb.astype(F32)
    unit, _ = normalise(xf)
    normed = unit * gains[0:1, :] + gains[2:3, :]
    nb = normed.astype(BF16)
    pn = pool_rows(normed).astype(BF16)
    k_out[...] = jnp.zeros_like(k_out)
    v_out[...] = jnp.zeros_like(v_out)
    wait_all(waits)
    branch = jnp.zeros((PT, 384), F32)
    for r in range(4):
        w = weights[r, :, 0:384]
        q = nn(nb, w[:, 0:256])[:, 96:192].astype(BF16)
        kv = nn(pn, w)
        q_out[r] = q
        k_out[r, 0:PW, :] = kv[:, 192:288].astype(BF16)
        v_out[r, 0:PW, :] = kv[:, 288:384].astype(BF16)
        k_out[r, MEM0 : MEM0 + MEMROWS, :] = mem[r, 0]
        v_out[r, MEM0 : MEM0 + MEMROWS, :] = mem[r, 1]
        shares = softmax_rows(nt(q, k_out[r]), ok[...], fill[...])
        mixed = (nn(shares.astype(BF16), v_out[r]) + q.astype(F32)).astype(BF16)
        mix_out[r] = mixed
        branch = branch + nt(mixed, w[:, 0:96])
    middle = xf + gains[4:5, :] + branch
    mid_out[...] = middle
    unit, _ = normalise(middle)
    nm = (unit * gains[1:2, :] + gains[3:4, :]).astype(BF16)
    total = middle + gains[5:6, :]
    for r in range(4):
        hidden = nn(nm, weights[r, :, 384:768]) + bias_up[r : r + 1, :]
        active, slope = gelu_both(hidden)
        active = active.astype(BF16)
        act_out[r] = active
        slope_out[r] = slope
        total = total + nt(active, weights[r, :, 768:1152])
    passed[...] = total.astype(BF16)


def first_backward(
    place, dpassed, x, q_in, k_in, v_in, mix_in, mid_in, act_in, slope_in,
    token_back, p1, s1, vec384, ok, fill, *rest
):
    mine, other = rest[0:8], rest[8:16]
    xgrad, vec_out, bias_out = rest[16:19]
    outs_a = rest[19:23]
    outs_b = rest[23:27]
    weights, gains, part, sem = rest[27:31]
    waits = weight_copies(place[0], 0, mine, other, weights, 1152, sem)
    gains[...] = exact_nn(vec384[...], p1[...])
    xf = x[...].astype(F32)
    unit_in, inv_in = normalise(xf)
    normed = unit_in * gains[0:1, :] + gains[2:3, :]
    nb = normed.astype(BF16)
    pn = pool_rows(normed).astype(BF16)
    middle = mid_in[...]
    unit_mid, inv_mid = normalise(middle)
    nm = (unit_mid * gains[1:2, :] + gains[3:4, :]).astype(BF16)
    sel = s1[...]
    dyb = dpassed[...]
    dy = dyb.astype(F32)
    dy_sel = nt(sel, dyb).astype(BF16)
    nm_sel = nt(sel, nm).astype(BF16)
    nb_sel = nt(sel, nb).astype(BF16)
    pn_sel = nt(sel, pn).astype(BF16)
    wait_all(waits)

    put = functools.partial(put_grad, outs_a, outs_b)
    dnm = jnp.zeros((PT, 384), F32)
    for r in range(4):
        dact = nn(dyb, weights[r, :, 768:1152])
        dh = (dact * slope_in[r]).astype(BF16)
        bias_out[r : r + 1, :] = column_sum(dh.astype(F32))
        put(r, 768, nn(dy_sel, act_in[r]))
        put(r, 384, nn(nm_sel, dh))
        dnm = dnm + nt(dh, weights[r, :, 384:768])
    dmid = dy + normalise_back(dnm, unit_mid, inv_mid, gains[1:2, :])
    dbr = dmid.astype(BF16)
    dbr_sel = nt(sel, dbr).astype(BF16)
    dnormed = jnp.zeros((PT, 384), F32)
    dpooled = jnp.zeros((PW, 384), F32)
    for r in range(4):
        w = weights[r, :, 0:384]
        dmix = nn(dbr, w[:, 0:96]).astype(BF16)
        q = q_in[r]
        dq, dk, dv = attend_back(q, k_in[r], v_in[r], ok[...], fill[...], dmix)
        dqb = dq.astype(BF16)
        dkb = (dk[0:PW] * 0.25).astype(BF16)
        dvb = (dv[0:PW] * 0.25).astype(BF16)
        zero = jnp.zeros((PT, HEAD), BF16)
        part[...] = jnp.zeros_like(part)
        part[:, 0:96] = mix_in[r]
        first = nn(dbr_sel, part[...])
        part[:, 0:96] = zero
        part[:, 96:192] = dqb
        first = first + nn(nb_sel, part[...])
        dnormed = dnormed + nt(part[:, 0:256], w[:, 0:256])
        part[:, 96:192] = zero
        part[0:PW, 192:288] = dkb
        part[0:PW, 288:384] = dvb
        first = first + 4.0 * nn(pn_sel, part[0:PW, :])
        dpooled = dpooled + nt(part[0:PW, 128:384], w[:, 128:384])
        put(r, 0, first)
    dnormed = dnormed + jnp.concatenate([dpooled, dpooled, dpooled, dpooled], axis=0)
    dx = normalise_back(dnormed, unit_in, inv_in, gains[0:1, :]) + dmid
    vec = jnp.concatenate(
        [
            column_sum(dnormed * unit_in),
            column_sum(dnm * unit_mid),
            column_sum(dnormed),
            column_sum(dnm),
            column_sum(dmid),
            column_sum(dy),
            jnp.zeros((2, 384), F32),
        ],
        axis=0,
    )
    vec_out[...] = exact_nt(vec, p1[...])
    dxb = nt(dx.astype(BF16), p1[...]).astype(BF16)
    xgrad[...] = nn(token_back[...], dxb).astype(BF16)


def second_block(
    place, passed, cot, key_ok, ok, fill, mem, bias_up, p1, p2, pr, s1, s2, vec384, vec768, *rest
):
    mine_a, other_a, mine_f, other_f = rest[0:8], rest[8:16], rest[16:24], rest[24:32]
    act_out, dpassed, vec1_out, vec2_out, bias_out = rest[32:37]
    outs_a, outs_b = rest[37:41], rest[41:45]
    (wa, wu, wd, gains, gains2, keys, values, queries, mixes, acts, slopes, part, sem_a, sem_u, sem_d) = rest[45:60]
    waits_a = weight_copies(place[0], 1, mine_a, other_a, wa, 1152, sem_a)
    waits_u = weight_copies(place[0], 0, mine_f, other_f, wu, 1536, sem_u)
    waits_d = weight_copies(place[0], 1, mine_f, other_f, wd, 1536, sem_d)
    gains[...] = exact_nn(vec384[...], p1[...])
    gains2[...] = exact_nn(vec768[...], p2[...])
    xf = passed[...].astype(F32)
    unit_in, inv_in = normalise(xf)
    normed = unit_in * gains[6:7, :] + gains[7:8, :]
    pn = pool_rows(normed).astype(BF16)
    pnr = nn(pn, pr[...]).astype(BF16)
    dyb = nn(cot[...], p2[...]).astype(BF16)
    dyb = jnp.concatenate([dyb, jnp.zeros((PW - WIN, 768), BF16)], axis=0)
    dy = dyb.astype(F32) * key_ok[...]
    dyb = dy.astype(BF16)
    keys[...] = jnp.zeros_like(keys)
    values[...] = jnp.zeros_like(values)
    mixes[...] = jnp.zeros_like(mixes)
    wait_all(waits_a)
    branch = [jnp.zeros((PW, 384), F32), jnp.zeros((PW, 384), F32)]
    for r in range(4):
        kv = nn(pn, wa[r, :, 768:1152])
        mixes[r, :, 192:288] = pnr[:, r * 96 : (r + 1) * 96]
        for h in range(2):
            q = nn(pn, wa[r, :, 384 * h + 256 : 384 * h + 384])[:, 32:128].astype(BF16)
            n = 2 * r + h
            queries[n] = q
            keys[n, 0:PW, :] = kv[:, 192 * h : 192 * h + 96].astype(BF16)
            values[n, 0:PW, :] = kv[:, 192 * h + 96 : 192 * h + 192].astype(BF16)
            keys[n, MEM0 : MEM0 + MEMROWS, :] = mem[r, 0, :, 96 * h : 96 * h + 96]
            values[n, MEM0 : MEM0 + MEMROWS, :] = mem[r, 1, :, 96 * h : 96 * h + 96]
            shares = softmax_rows(nt(q, keys[n]), ok[...], fill[...])
            mixed = (nn(shares.astype(BF16), values[n]) + q.astype(F32)).astype(BF16)
            mixes[r, :, 96 * h : 96 * h + 96] = mixed
        for s in range(2):
            branch[s] = branch[s] + nt(mixes[r], wa[r, :, 384 * s : 384 * s + 384])
    middle = jnp.concatenate(branch, axis=1) + gains2[2:3, :]
    unit_mid, inv_mid = normalise(middle)
    nm = (unit_mid * gains2[0:1, :] + gains2[1:2, :]).astype(BF16)
    wait_all(waits_u)
    for r in range(4):
        hidden = nn(nm[:, 0:384], wu[r, :, 0:768]) + nn(nm[:, 384:768], wu[r, :, 768:1536])
        active, slope = gelu_both(hidden + bias_up[r : r + 1, :])
        acts[r] = active.astype(BF16)
        slopes[r] = slope
    wait_all(waits_d)
    down = [jnp.zeros((PW, 384), F32), jnp.zeros((PW, 384), F32)]
    for r in range(4):
        for s in range(2):
            down[s] = down[s] + nt(acts[r], wd[r, :, 768 * s : 768 * s + 768])
    output = (middle + gains2[3:4, :] + jnp.concatenate(down, axis=1)).astype(BF16)
    act_out[...] = nt(output, p2[...])[0:WIN].astype(BF16)

    sel2 = s2[...]
    dy_sel = nt(sel2, dyb).astype(BF16)
    nm_sel = nt(sel2, nm).astype(BF16)

    put = functools.partial(put_grad, outs_a, outs_b)
    dnm = [jnp.zeros((PW, 384), F32), jnp.zeros((PW, 384), F32)]
    for r in range(4):
        dact = nn(dyb[:, 0:384], wd[r, :, 0:768]) + nn(dyb[:, 384:768], wd[r, :, 768:1536])
        dh = (dact * slopes[r]).astype(BF16)
        bias_out[r : r + 1, :] = column_sum(dh.astype(F32))
        for s in range(2):
            put(r, 2688 + 768 * s, nn(dy_sel[192 * s : 192 * s + 192], acts[r]))
            put(r, 1152 + 768 * s, nn(nm_sel[192 * s : 192 * s + 192], dh))
            dnm[s] = dnm[s] + nt(dh, wu[r, :, 768 * s : 768 * s + 768])
    dnm = jnp.concatenate(dnm, axis=1)
    dmid = dy + normalise_back(dnm, unit_mid, inv_mid, gains2[0:1, :])
    dbr = dmid.astype(BF16)
    dbr_sel = nt(sel2, dbr).astype(BF16)
    pn_sel = nt(s1[...], pn).astype(BF16)
    dpooled = jnp.zeros((PW, 384), F32)
    part[...] = jnp.zeros_like(part)
    dres = []
    for r in range(4):
        dmm = nn(dbr[:, 0:384], wa[r, :, 0:384]) + nn(dbr[:, 384:768], wa[r, :, 384:768])
        dres.append(dmm[:, 192:288])
        for h in range(2):
            n = 2 * r + h
            dmix = dmm[:, 96 * h : 96 * h + 96].astype(BF16)
            dq, dk, dv = attend_back(queries[n], keys[n], values[n], ok[...], fill[...], dmix)
            part[h, :, 288:384] = dq.astype(BF16)
            part[2, :, 192 * h : 192 * h + 96] = dk[0:PW].astype(BF16)
            part[2, :, 192 * h + 96 : 192 * h + 192] = dv[0:PW].astype(BF16)
        for s in range(2):
            value = nn(dbr_sel[192 * s : 192 * s + 192], mixes[r]) + nn(pn_sel, part[s])
            put(r, 384 * s, value)
            dpooled = dpooled + nt(part[s], wa[r, :, 384 * s : 384 * s + 384])
        put(r, 768, nn(pn_sel, part[2]))
        dpooled = dpooled + nt(part[2], wa[r, :, 768:1152])
    dpooled = dpooled + exact_nt(jnp.concatenate(dres, axis=1), pr[...])
    dpooled = dpooled * 0.25
    dnormed = jnp.concatenate([dpooled, dpooled, dpooled, dpooled], axis=0)
    dpassed[...] = normalise_back(dnormed, unit_in, inv_in, gains[6:7, :]).astype(BF16)
    vec1 = jnp.concatenate(
        [column_sum(dnormed * unit_in), column_sum(dnormed), jnp.zeros((6, 384), F32)], axis=0
    )
    vec1_out[...] = exact_nt(vec1, p1[...])
    vec2 = jnp.concatenate(
        [
            column_sum(dnm * unit_mid),
            column_sum(dnm),
            column_sum(dmid),
            column_sum(dy),
            jnp.zeros((4, 768), F32),
        ],
        axis=0,
    )
    vec2_out[...] = exact_nt(vec2, p2[...])


def spec_vmem():
    return pl.BlockSpec(memory_space=pltpu.VMEM)


def spec_any():
    return pl.BlockSpec(memory_space=pl.ANY)


def spec_smem():
    return pl.BlockSpec(memory_space=pltpu.SMEM)


def call(body, inputs, kinds, outs, scratch, flops, moved):
    specs = {"v": spec_vmem, "a": spec_any, "s": spec_smem}
    return pl.pallas_call(
        body,
        out_shape=outs,
        in_specs=[specs[k]() for k in kinds],
        out_specs=jax.tree.map(lambda _: spec_vmem(), outs),
        scratch_shapes=scratch,
        compiler_params=pltpu.CompilerParams(vmem_limit_bytes=VMEM_LIMIT),
        cost_estimate=pl.CostEstimate(flops=flops, bytes_accessed=moved, transcendentals=0),
    )(*inputs)


def shape(dims, dtype):
    return jax.ShapeDtypeStruct(dims, dtype)


CUT_ONE = 640
CUT_TWO = 768
CUT_GRAD = 2176


def pairs_for(axis, by):
    if axis == "y":
        return "head", [((i + by) % 4, i) for i in range(4)]
    if axis == "x":
        return "dp", [(((i // 4 + by) % 4) * 4 + i % 4, i) for i in range(16)]
    return "dp", [((i // 4) * 4 + (i % 4 + by) % 4, i) for i in range(16)]


def fetch(v, axis, by):
    name, pairs = pairs_for(axis, by)
    return lax.ppermute(v, name, pairs)


def swap(v):
    return lax.ppermute(v, "pipe", [(0, 1), (1, 0)])


def ring_all(v, axis):
    return [v] + [fetch(v, axis, by) for by in (1, 2, 3)]


def ring_sum(slabs, axis):
    total = slabs[0].astype(F32)
    for r in (1, 2, 3):
        total = total + fetch(slabs[r], axis, -r).astype(F32)
    return total


def gather_weights(local, cut):
    rows = jnp.concatenate(ring_all(local, "z"), axis=0)
    first = jnp.concatenate(ring_all(rows[:, :cut], "x"), axis=0)
    last = jnp.stack(ring_all(rows[:, cut:], "y"))
    return ring_all(first, "y") + ring_all(last, "x")


def scatter_sum(slabs_a, slabs_b):
    first = ring_sum(slabs_a, "y").astype(BF16)
    last = ring_sum(slabs_b, "x").astype(BF16)
    first = ring_sum([first[48 * k : 48 * k + 48] for k in range(4)], "x").astype(BF16)
    last = ring_sum([last[k] for k in range(4)], "y").astype(BF16)
    both = jnp.concatenate([first, last], axis=1)
    return ring_sum([both[12 * k : 12 * k + 12] for k in range(4)], "z")


def spread_micro(v, pipe, y):
    def send(rounds):
        pairs = []
        for p, source, target in rounds:
            pairs.append((p * 4 + source, p * 4 + target))
        return lax.ppermute(v, ("pipe", "head"), pairs)

    one = send([(0, 0, 1), (0, 1, 0), (1, 2, 3), (1, 3, 2)])
    two = send([(0, 0, 2), (0, 1, 3), (1, 2, 0), (1, 3, 1)])
    three = send([(0, 0, 3), (0, 1, 2), (1, 2, 1), (1, 3, 0)])
    holder = (y // 2) == pipe
    even = (y % 2) == 0
    low = jnp.where(holder, jnp.where(even, v, one), jnp.where(even, two, three))
    high = jnp.where(holder, jnp.where(even, one, v), jnp.where(even, three, two))
    return jnp.stack([low, high])[:, None]


def token_order():
    order = np.zeros((PT, TOK), np.float32)
    for block in range(4):
        for window in range(WIN):
            row = (window // 10) * 2 + block // 2
            col = (window % 10) * 2 + block % 2
            order[block * PW + window, row * GRID + col] = 1
    return order


def per_device(
    clips_in, cotangent, token_mask, memory_valid, memory_one, memory_two,
    qkv_one, out_one, up_one, down_one, up_bias_one, gains_one, shifts_one,
    qkv_two, out_two, res_two, up_two, down_two, up_bias_two, gain_two_in, shift_two_in, gains_two, shifts_two,
):
    pipe = lax.axis_index("pipe")
    dp = lax.axis_index("dp")
    y = lax.axis_index("head")
    x_at, z_at = dp // 4, dp % 4
    first_core = pipe == 0

    one = jnp.concatenate([out_one.T, qkv_one[:, 0, :], up_one, down_one.T], axis=1)
    out_t, res_t = out_two.T, res_two.T
    q2 = qkv_two
    attn = jnp.concatenate(
        [
            out_t[:24], res_t[:24], q2[:, 0, :96],
            out_t[24:], res_t[24:], q2[:, 1, :96],
            q2[:, 0, 96:], q2[:, 1, 96:],
        ],
        axis=1,
    )
    down_t = down_two.T
    feed_up = jnp.concatenate([up_two[:24], up_two[24:]], axis=1)
    feed_down = jnp.concatenate([down_t[:24], down_t[24:]], axis=1)
    mine_one = gather_weights(jnp.where(first_core, one, attn), CUT_ONE)
    mine_two = gather_weights(jnp.where(first_core, feed_up, feed_down), CUT_TWO)
    other_one = [swap(v) for v in mine_one]
    other_two = [swap(v) for v in mine_two]

    def clip_of(v, at):
        return lax.dynamic_index_in_dim(v, at, 0, keepdims=False)

    biases = jnp.concatenate([up_bias_one, up_bias_two])
    biases = jnp.concatenate(thirds(biases)).reshape(12, 288)
    memory = jnp.concatenate([memory_one[:, 0], memory_two[:, 0]], axis=-1)

    def payload(r):
        part = clip_of(memory, (y - r) % 4).reshape(2 * MEMROWS, 288)
        return jnp.concatenate([part, biases], axis=0)

    parcels = [payload(0)] + [fetch(payload(r), "y", r) for r in (1, 2, 3)]
    parcels = jnp.stack(parcels)
    memory = parcels[:, : 2 * MEMROWS].reshape(4, 2, MEMROWS, 288)
    mem_one, mem_two = memory[..., :96], memory[..., 96:]
    biases = parcels[:, 2 * MEMROWS :].astype(F32).reshape(4, 3, 1152)
    biases = biases[:, 0] + biases[:, 1] + biases[:, 2]
    bias_one, bias_two = biases[:, :384], biases[:, 384:]

    flags = clip_of(token_mask[:, 0], y).reshape(10, 2, 10, 2)[:, 0, :, 0].reshape(WIN)
    key_ok = (flags > 0).astype(F32)
    mem_ok = jnp.repeat((clip_of(memory_valid[:, 0], y) > 0).astype(F32), MEMROWS // 2)
    gap = jnp.zeros((MEM0 - WIN,), F32)
    tail = jnp.zeros((KEYS - MEM0 - MEMROWS,), F32)
    ok = jnp.concatenate([key_ok, gap, mem_ok, tail]).reshape(1, KEYS)
    fill = np.full((1, KEYS), ABSENT, np.float32)
    fill[0, :WIN] = MASKED
    fill[0, MEM0 : MEM0 + MEMROWS] = MASKED
    fill = jnp.asarray(fill)
    key_col = jnp.concatenate([key_ok, jnp.zeros((PW - WIN,), F32)]).reshape(PW, 1)

    k = jnp.arange(384)
    piece = ((x_at + k // 96) % 4) * 4 + (z_at + (k // 24) % 4) % 4
    raw1 = piece * 24 + k % 24
    p1 = (k[:, None] == raw1[None, :]).astype(BF16)
    j = jnp.arange(192)
    piece_j = ((x_at + j // 48) % 4) * 4 + (z_at + (j // 12) % 4) % 4
    s1 = ((pipe * 192 + piece_j * 12 + j % 12)[:, None] == raw1[None, :]).astype(BF16)
    head_raw = ((y + k // 96) % 4) * 96 + k % 96
    pr = (raw1[:, None] == head_raw[None, :]).astype(BF16)
    raw2 = jnp.concatenate([piece * 48 + k % 24, piece * 48 + 24 + k % 24])
    p2 = (jnp.arange(768)[:, None] == raw2[None, :]).astype(BF16)
    row2 = pipe * 384 + piece_j * 24 + j % 12
    s2 = (jnp.concatenate([row2, row2 + 12])[:, None] == raw2[None, :]).astype(BF16)

    order = token_order()
    token_perm = jnp.asarray(order, BF16)
    token_back = jnp.asarray(order.T, BF16)
    vec384 = jnp.concatenate([gains_one, shifts_one, gain_two_in[None], shift_two_in[None]], axis=0)
    vec768 = jnp.concatenate([gains_two[None], shifts_two, jnp.zeros((4, 768), F32)], axis=0)
    place = pipe.astype(jnp.int32).reshape(1)
    x = clip_of(clips_in[:, 0], y)
    cot = clip_of(cotangent[:, 0], y)

    dma = pltpu.SemaphoreType.DMA
    saved = call(
        first_forward,
        (place, x, token_perm, p1, vec384, ok, fill, mem_one, bias_one, *mine_one, *other_one),
        "s" + "v" * 8 + "a" * 16,
        (
            shape((PT, 384), BF16), shape((PT, 384), BF16),
            shape((4, PT, HEAD), BF16), shape((4, KEYS, HEAD), BF16), shape((4, KEYS, HEAD), BF16),
            shape((4, PT, HEAD), BF16), shape((PT, 384), F32),
            shape((4, PT, 384), BF16), shape((4, PT, 384), F32),
        ),
        [pltpu.VMEM((4, 384, 1152), BF16), pltpu.VMEM((8, 384), F32), dma(())],
        1_300_000_000, 8_000_000,
    )
    passed = saved[0]

    rest = 4224 - CUT_GRAD
    grads_two = tuple(shape((192, CUT_GRAD), BF16) for _ in range(4)) + tuple(
        shape((4, 48, rest), BF16) for _ in range(4)
    )
    second = call(
        second_block,
        (
            place, passed, cot, key_col, ok, fill, mem_two, bias_two, p1, p2, pr, s1, s2, vec384, vec768,
            *mine_one, *other_one, *mine_two, *other_two,
        ),
        "s" + "v" * 14 + "a" * 32,
        (
            shape((WIN, 768), BF16), shape((PT, 384), BF16), shape((8, 384), F32), shape((8, 768), F32),
            shape((4, 768), F32),
        )
        + grads_two,
        [
            pltpu.VMEM((4, 384, 1152), BF16), pltpu.VMEM((4, 384, 1536), BF16), pltpu.VMEM((4, 384, 1536), BF16),
            pltpu.VMEM((8, 384), F32), pltpu.VMEM((8, 768), F32),
            pltpu.VMEM((8, KEYS, HEAD), BF16), pltpu.VMEM((8, KEYS, HEAD), BF16), pltpu.VMEM((8, PW, HEAD), BF16),
            pltpu.VMEM((4, PW, 384), BF16), pltpu.VMEM((4, PW, 768), BF16), pltpu.VMEM((4, PW, 768), F32),
            pltpu.VMEM((3, PW, 384), BF16), dma(()), dma(()), dma(()),
        ],
        4_000_000_000, 22_000_000,
    )
    activation, dpassed, vec_in, vec_mid, dbias_two = second[:5]
    summed_two = scatter_sum(second[5:9], second[9:13])
    activations = spread_micro(activation, pipe, y)

    grads_one = tuple(shape((192, CUT_ONE), BF16) for _ in range(4)) + tuple(
        shape((4, 48, 1152 - CUT_ONE), BF16) for _ in range(4)
    )
    third = call(
        first_backward,
        (place, dpassed, *saved[1:], token_back, p1, s1, vec384, ok, fill, *mine_one, *other_one),
        "s" + "v" * 15 + "a" * 16,
        (shape((TOK, 384), BF16), shape((8, 384), F32), shape((4, 384), F32)) + grads_one,
        [
            pltpu.VMEM((4, 384, 1152), BF16), pltpu.VMEM((8, 384), F32), pltpu.VMEM((PT, 384), BF16), dma(()),
        ],
        2_000_000_000, 14_000_000,
    )
    xgrad, vec_one, dbias_one = third[:3]
    summed_one = scatter_sum(third[3:7], third[7:11])
    input_grad = spread_micro(xgrad, pipe, y)

    common = jnp.concatenate([vec_one[:6].reshape(-1), vec_in[:2].reshape(-1), vec_mid[:4].reshape(-1)])
    slabs = [jnp.concatenate([common, dbias_one[r], dbias_two[r]]).reshape(57, 128) for r in range(4)]
    vectors = ring_sum(slabs, "y")
    vectors = ring_sum([vectors] * 4, "x")
    vectors = ring_sum([vectors] * 4, "z").reshape(-1)
    v_one = vectors[:2304].reshape(6, 384)
    v_in = vectors[2304:3072].reshape(2, 384)
    v_mid = vectors[3072:6144].reshape(4, 768)

    g1 = summed_one
    ga, gu, gd = summed_two[:, :1152], summed_two[:, 1152:2688], summed_two[:, 2688:]
    grad_qkv_two = jnp.stack(
        [
            jnp.concatenate([ga[:, 288:384], ga[:, 768:960]], axis=1),
            jnp.concatenate([ga[:, 672:768], ga[:, 960:1152]], axis=1),
        ],
        axis=1,
    )
    return (
        activations,
        input_grad,
        g1[:, None, 96:384],
        g1[:, :96].T,
        g1[:, 384:768],
        g1[:, 768:].T,
        vectors[6144:6528],
        v_one[:2],
        v_one[2:],
        grad_qkv_two,
        jnp.concatenate([ga[:, 0:192], ga[:, 384:576]], axis=0).T,
        jnp.concatenate([ga[:, 192:288], ga[:, 576:672]], axis=0).T,
        jnp.concatenate([gu[:, :768], gu[:, 768:]], axis=0),
        jnp.concatenate([gd[:, :768], gd[:, 768:]], axis=0).T,
        vectors[6528:],
        v_in[0],
        v_in[1],
        v_mid[0],
        v_mid[1:],
    )


def solution(mesh):
    return jax.shard_map(
        per_device,
        mesh=mesh,
        in_specs=(
            P(None, "dp", None, None), P(None, "dp", None, None), P(None, "dp", None), P(None, "dp", None),
            P(None, "dp", None, None, "head"), P(None, "dp", None, None, "head"),
            P("dp", "head", None), P("head", "dp"), P("dp", "head"), P("head", "dp"), P("head"), P(), P(),
            P("dp", "head", None), P("head", "dp"), P("head", "dp"), P("dp", "head"), P("head", "dp"), P("head"),
            P(), P(), P(), P(),
        ),
        out_specs=(
            P("pipe", "dp", None, None), P("pipe", "dp", None, None),
            P(("pipe", "dp"), "head", None), P("head", ("pipe", "dp")), P(("pipe", "dp"), "head"),
            P("head", ("pipe", "dp")), P("head"), P(), P(),
            P(("pipe", "dp"), "head", None), P("head", ("pipe", "dp")), P("head", ("pipe", "dp")),
            P(("pipe", "dp"), "head"), P("head", ("pipe", "dp")), P("head"), P(), P(), P(), P(),
        ),
        check_vma=False,
    )
```

```python
import functools

import jax
import jax.numpy as jnp
import numpy as np
from jax import lax
from jax.experimental import pallas as pl
from jax.experimental.pallas import tpu as pltpu
from jax.sharding import PartitionSpec as P

F32 = jnp.float32
BF16 = jnp.bfloat16
GRID = 20
TOK = 400
WIN = 100
PW = 104
PT = 4 * PW
KEYS = 256
MEM0 = 112
MEMROWS = 50
HEAD = 96
EPS = 1e-06
MASKED = -1000000000.0
ABSENT = -3e38
SCALE = HEAD ** (-0.5)
VMEM_LIMIT = 56 * 1024 * 1024


def nn(a, b):
    return lax.dot_general(a, b, (((1,), (0,)), ((), ())), preferred_element_type=F32)


def nt(a, b):
    return lax.dot_general(a, b, (((1,), (1,)), ((), ())), preferred_element_type=F32)


def tn(a, b):
    return lax.dot_general(a, b, (((0,), (0,)), ((), ())), preferred_element_type=F32)


def thirds(v):
    high = v.astype(BF16)
    rest = v - high.astype(F32)
    mid = rest.astype(BF16)
    low = (rest - mid.astype(F32)).astype(BF16)
    return high, mid, low


def exact_nn(v, m):
    a, b, c = thirds(v)
    return nn(a, m) + nn(b, m) + nn(c, m)


def exact_nt(v, m):
    a, b, c = thirds(v)
    return nt(a, m) + nt(b, m) + nt(c, m)


def normalise(v):
    average = jnp.mean(v, axis=-1, keepdims=True)
    centred = v - average
    variance = jnp.mean(centred * centred, axis=-1, keepdims=True)
    inverse = lax.rsqrt(variance + EPS)
    return centred * inverse, inverse


def normalise_back(grad, unit, inverse, gain):
    scaled = grad * gain
    mean_one = jnp.mean(scaled, axis=-1, keepdims=True)
    mean_two = jnp.mean(scaled * unit, axis=-1, keepdims=True)
    return inverse * (scaled - mean_one - unit * mean_two)


def column_sum(v):
    return jnp.sum(v, axis=0, keepdims=True)


def gelu_both(h):
    cdf = 0.5 + 0.5 * lax.erf(h * 0.7071067811865476)
    density = 0.3989422804014327 * jnp.exp(-0.5 * h * h)
    return h * cdf, cdf + h * density


def pool_rows(v):
    return 0.25 * (v[0:PW] + v[PW : 2 * PW] + v[2 * PW : 3 * PW] + v[3 * PW : 4 * PW])


def softmax_rows(scores, ok, fill):
    scores = jnp.where(ok > 0, scores * SCALE, fill)
    peak = jnp.max(scores, axis=-1, keepdims=True)
    expos = jnp.exp(scores - peak)
    return expos / jnp.sum(expos, axis=-1, keepdims=True)


def attend_back(q, keys, values, ok, fill, dmix):
    shares = softmax_rows(nt(q, keys), ok, fill)
    dvalues = tn(shares.astype(BF16), dmix)
    dshares = nt(dmix, values)
    inner = jnp.sum(shares * dshares, axis=-1, keepdims=True)
    dscores = (shares * (dshares - inner)).astype(BF16)
    dq = nn(dscores, keys) * SCALE + dmix.astype(F32)
    dkeys = tn(dscores, q) * SCALE
    return dq, dkeys, dvalues


def load_weights(core, owner, mine, other, dst, sem):
    def copies(groups, places):
        at = 0
        for kind, low, high in groups:
            cols = pl.ds(at, low.shape[-1])
            at += low.shape[-1]
            for n in range(4):
                slab = (low if n < 2 else high).at[n % 2]
                if kind == "y":
                    pltpu.make_async_copy(slab, dst.at[places[n], :, cols], sem).start()
                else:
                    for h in range(4):
                        pltpu.make_async_copy(slab.at[h], dst.at[places[h], pl.ds(96 * n, 96), cols], sem).start()

    @pl.when(core == owner)
    def _():
        copies(mine, (0, 1, 2, 3))

    @pl.when(core != owner)
    def _():
        copies(other, (0, 2, 1, 3))


def wait_weights(dst, sem):
    pltpu.make_async_copy(dst, dst, sem).wait()


def groups_one(refs):
    return [("y", refs[0], refs[1]), ("rows", refs[2], refs[3])]


def groups_two(refs):
    return [("rows", refs[0], refs[1]), ("y", refs[2], refs[3])]


def forward(
    place, x, token_perm, p1, turn, pr, vec384, out_bias, ok, fill, mem_one, mem_two, bias_up, *rest
):
    mine, other = groups_one(rest[0:4]), groups_one(rest[4:8])
    (passed, x_out, q_out, k_out, v_out, mix_out, mid_out, act_out, slope_out,
     pn_out, q2_out, k2_out, v2_out, mix2_out, mid2_out) = rest[8:23]
    w1, wa, gains, sem_one, sem_attn = rest[23:28]
    load_weights(place[0], 0, mine, other, w1, sem_one)
    load_weights(place[0], 1, mine, other, wa, sem_attn)
    gains[...] = exact_nn(vec384[...], p1[...])
    xb = nn(x[...], p1[...]).astype(BF16)
    xb = nn(token_perm[...], xb).astype(BF16)
    x_out[...] = xb
    xf = xb.astype(F32)
    unit, _ = normalise(xf)
    normed = unit * gains[0:1, :] + gains[2:3, :]
    nb = normed.astype(BF16)
    pn = pool_rows(normed).astype(BF16)
    k_out[...] = jnp.zeros_like(k_out)
    v_out[...] = jnp.zeros_like(v_out)
    k2_out[...] = jnp.zeros_like(k2_out)
    v2_out[...] = jnp.zeros_like(v2_out)
    mix2_out[...] = jnp.zeros_like(mix2_out)
    wait_weights(w1, sem_one)
    branch = jnp.zeros((PT, 384), F32)
    for r in range(4):
        w = w1[r, :, 0:384]
        q = nn(nb, w[:, 0:256])[:, 96:192].astype(BF16)
        kv = nn(pn, w)
        q_out[r] = q
        k_out[r, 0:PW, :] = kv[:, 192:288].astype(BF16)
        v_out[r, 0:PW, :] = kv[:, 288:384].astype(BF16)
        k_out[r, MEM0 : MEM0 + MEMROWS, :] = mem_one[r, 0]
        v_out[r, MEM0 : MEM0 + MEMROWS, :] = mem_one[r, 1]
        shares = softmax_rows(nt(q, k_out[r]), ok[...], fill[...])
        mixed = (nn(shares.astype(BF16), v_out[r]) + q.astype(F32)).astype(BF16)
        mix_out[r] = mixed
        branch = branch + nt(mixed, w[:, 0:96])
    middle = xf + gains[4:5, :] + branch
    mid_out[...] = middle
    unit, _ = normalise(middle)
    nm = (unit * gains[1:2, :] + gains[3:4, :]).astype(BF16)
    total = middle + gains[5:6, :]
    for r in range(4):
        hidden = nn(nm, w1[r, :, 384:768]) + bias_up[r : r + 1, :]
        active, slope = gelu_both(hidden)
        active = active.astype(BF16)
        act_out[r] = active
        slope_out[r] = slope
        total = total + nt(active, w1[r, :, 768:1152])
    xb = nn(total.astype(BF16), turn[...]).astype(BF16)
    passed[...] = xb

    xf = xb.astype(F32)
    gains[...] = exact_nn(gains[...], turn[...])
    unit, _ = normalise(xf)
    normed = unit * gains[6:7, :] + gains[7:8, :]
    pn = pool_rows(normed).astype(BF16)
    pn_out[...] = pn
    pnr = nn(pn, pr[...]).astype(BF16)
    wait_weights(wa, sem_attn)
    branch = [jnp.zeros((PW, 384), F32), jnp.zeros((PW, 384), F32)]
    for r in range(4):
        kv = nn(pn, wa[r, :, 768:1152])
        mix2_out[r, :, 192:288] = pnr[:, r * 96 : (r + 1) * 96]
        for h in range(2):
            q = nn(pn, wa[r, :, 384 * h + 256 : 384 * h + 384])[:, 32:128].astype(BF16)
            n = 2 * r + h
            q2_out[n] = q
            k2_out[n, 0:PW, :] = kv[:, 192 * h : 192 * h + 96].astype(BF16)
            v2_out[n, 0:PW, :] = kv[:, 192 * h + 96 : 192 * h + 192].astype(BF16)
            k2_out[n, MEM0 : MEM0 + MEMROWS, :] = mem_two[r, 0, :, 96 * h : 96 * h + 96]
            v2_out[n, MEM0 : MEM0 + MEMROWS, :] = mem_two[r, 1, :, 96 * h : 96 * h + 96]
            shares = softmax_rows(nt(q, k2_out[n]), ok[...], fill[...])
            mixed = (nn(shares.astype(BF16), v2_out[n]) + q.astype(F32)).astype(BF16)
            mix2_out[r, :, 96 * h : 96 * h + 96] = mixed
        for s in range(2):
            branch[s] = branch[s] + nt(mix2_out[r], wa[r, :, 384 * s : 384 * s + 384])
    mid2_out[...] = jnp.concatenate(branch, axis=1) + out_bias[...]


def feed_two(place, middle_in, cot, key_ok, p2, to_up, to_down, s2f, gains2, bias_up, *rest):
    mine, other = groups_two(rest[0:4]), groups_two(rest[4:8])
    act_out, dmid_out, vec_out, bias_out, keep_rows, send_rows, keep_y, send_y = rest[8:16]
    wu, wd, acts, slopes, sem_u, sem_d = rest[16:22]
    load_weights(place[0], 0, mine, other, wu, sem_u)
    load_weights(place[0], 1, mine, other, wd, sem_d)
    middle = middle_in[...]
    unit, inverse = normalise(middle)
    nm = (unit * gains2[0:1, :] + gains2[1:2, :]).astype(BF16)
    nm_up = [nn(nm[:, 384 * s : 384 * s + 384], to_up[...]).astype(BF16) for s in range(2)]
    dyb = nn(cot[...], p2[...]).astype(BF16)
    dyb = jnp.concatenate([dyb, jnp.zeros((PW - WIN, 768), BF16)], axis=0)
    dy = dyb.astype(F32) * key_ok[...]
    dyb = dy.astype(BF16)
    dy_down = [nn(dyb[:, 384 * s : 384 * s + 384], to_down[...]).astype(BF16) for s in range(2)]
    dy_sel = nt(s2f[...], dyb).astype(BF16)
    nm_sel = nt(s2f[...], nm).astype(BF16)
    wait_weights(wu, sem_u)
    for r in range(4):
        hidden = nn(nm_up[0], wu[r, :, 0:768]) + nn(nm_up[1], wu[r, :, 768:1536])
        active, slope = gelu_both(hidden + bias_up[r : r + 1, :])
        acts[r] = active.astype(BF16)
        slopes[r] = slope
    wait_weights(wd, sem_d)

    def put_rows(r, lo, value):
        value = value.astype(BF16)
        for k in range(4):
            out = keep_rows if k < 2 else send_rows
            out[k % 2, r, :, lo : lo + 768] = value[48 * k : 48 * k + 48]

    def put_head(r, lo, value):
        out = keep_y if r < 2 else send_y
        out[r % 2, :, lo : lo + 768] = value.astype(BF16)

    down = [jnp.zeros((PW, 384), F32), jnp.zeros((PW, 384), F32)]
    dnm = [jnp.zeros((PW, 384), F32), jnp.zeros((PW, 384), F32)]
    for r in range(4):
        active = acts[r]
        dact = nn(dy_down[0], wd[r, :, 0:768]) + nn(dy_down[1], wd[r, :, 768:1536])
        dh = (dact * slopes[r]).astype(BF16)
        bias_out[r : r + 1, :] = column_sum(dh.astype(F32))
        put_rows(r, 0, nn(nm_sel[0:192], dh))
        put_rows(r, 768, nn(dy_sel[0:192], active))
        put_head(r, 0, nn(nm_sel[192:384], dh))
        put_head(r, 768, nn(dy_sel[192:384], active))
        for s in range(2):
            down[s] = down[s] + nt(active, wd[r, :, 768 * s : 768 * s + 768])
            dnm[s] = dnm[s] + nt(dh, wu[r, :, 768 * s : 768 * s + 768])
    down = jnp.concatenate([exact_nt(v, to_down[...]) for v in down], axis=1)
    output = (middle + gains2[3:4, :] + down).astype(BF16)
    act_out[...] = nt(output, p2[...])[0:WIN].astype(BF16)
    dnm = jnp.concatenate([exact_nt(v, to_up[...]) for v in dnm], axis=1)
    dmid = dy + normalise_back(dnm, unit, inverse, gains2[0:1, :])
    dmid_out[...] = dmid
    vec = jnp.concatenate(
        [
            column_sum(dnm * unit),
            column_sum(dnm),
            column_sum(dmid),
            column_sum(dy),
            jnp.zeros((4, 768), F32),
        ],
        axis=0,
    )
    vec_out[...] = exact_nt(vec, p2[...])


def second_backward(
    place, dmid, passed, pn_in, queries, keys, values, mixes, p1, pr, s1, s2, gains_in, ok, fill, *rest
):
    mine, other = groups_one(rest[0:4]), groups_one(rest[4:8])
    dpassed, vec_out, keep, send = rest[8:12]
    wa, part, sem = rest[12:15]
    load_weights(place[0], 1, mine, other, wa, sem)
    xf = passed[...].astype(F32)
    unit, inverse = normalise(xf)
    pn = pn_in[...]
    dbr = dmid[...].astype(BF16)
    dbr_sel = nt(s2[...], dbr).astype(BF16)
    pn_sel = nt(s1[...], pn).astype(BF16)
    dpooled = jnp.zeros((PW, 384), F32)
    part[...] = jnp.zeros_like(part)
    wait_weights(wa, sem)

    def put(r, lo, value):
        value = value.astype(BF16)
        for k in range(4):
            out = keep if k < 2 else send
            out[k % 2, r, :, lo : lo + 384] = value[48 * k : 48 * k + 48]

    dres = []
    for r in range(4):
        dmm = nn(dbr[:, 0:384], wa[r, :, 0:384]) + nn(dbr[:, 384:768], wa[r, :, 384:768])
        dres.append(dmm[:, 192:288])
        for h in range(2):
            n = 2 * r + h
            dmix = dmm[:, 96 * h : 96 * h + 96].astype(BF16)
            dq, dk, dv = attend_back(queries[n], keys[n], values[n], ok[...], fill[...], dmix)
            part[h, :, 288:384] = dq.astype(BF16)
            part[2, :, 192 * h : 192 * h + 96] = dk[0:PW].astype(BF16)
            part[2, :, 192 * h + 96 : 192 * h + 192] = dv[0:PW].astype(BF16)
        for s in range(2):
            put(r, 384 * s, nn(dbr_sel[192 * s : 192 * s + 192], mixes[r]) + nn(pn_sel, part[s]))
            dpooled = dpooled + nt(part[s], wa[r, :, 384 * s : 384 * s + 384])
        put(r, 768, nn(pn_sel, part[2]))
        dpooled = dpooled + nt(part[2], wa[r, :, 768:1152])
    dpooled = dpooled + exact_nt(jnp.concatenate(dres, axis=1), pr[...])
    dpooled = dpooled * 0.25
    dnormed = jnp.concatenate([dpooled, dpooled, dpooled, dpooled], axis=0)
    gain = exact_nn(gains_in[...], p1[...])[0:1]
    dpassed[...] = normalise_back(dnormed, unit, inverse, gain).astype(BF16)
    vec = jnp.concatenate(
        [column_sum(dnormed * unit), column_sum(dnormed), jnp.zeros((6, 384), F32)], axis=0
    )
    vec_out[...] = exact_nt(vec, p1[...])


def first_backward(
    place, dpassed, x, q_in, k_in, v_in, mix_in, mid_in, act_in, slope_in,
    token_back, p1, turn, s1, vec384, ok, fill, *rest
):
    mine, other = groups_one(rest[0:4]), groups_one(rest[4:8])
    xgrad, vec_out, bias_out, keep, send = rest[8:13]
    weights, gains, part, sem = rest[13:17]
    load_weights(place[0], 0, mine, other, weights, sem)
    gains[...] = exact_nn(vec384[...], p1[...])
    xf = x[...].astype(F32)
    unit_in, inv_in = normalise(xf)
    normed = unit_in * gains[0:1, :] + gains[2:3, :]
    nb = normed.astype(BF16)
    pn = pool_rows(normed).astype(BF16)
    middle = mid_in[...]
    unit_mid, inv_mid = normalise(middle)
    nm = (unit_mid * gains[1:2, :] + gains[3:4, :]).astype(BF16)
    sel = s1[...]
    dyb = nt(dpassed[...], turn[...]).astype(BF16)
    dy = dyb.astype(F32)
    dy_sel = nt(sel, dyb).astype(BF16)
    nm_sel = nt(sel, nm).astype(BF16)
    nb_sel = nt(sel, nb).astype(BF16)
    pn_sel = nt(sel, pn).astype(BF16)
    wait_weights(weights, sem)

    def put(r, lo, value):
        out = keep if r < 2 else send
        out[r % 2, :, lo : lo + 384] = value.astype(BF16)

    dnm = jnp.zeros((PT, 384), F32)
    for r in range(4):
        dact = nn(dyb, weights[r, :, 768:1152])
        dh = (dact * slope_in[r]).astype(BF16)
        bias_out[r : r + 1, :] = column_sum(dh.astype(F32))
        put(r, 768, nn(dy_sel, act_in[r]))
        put(r, 384, nn(nm_sel, dh))
        dnm = dnm + nt(dh, weights[r, :, 384:768])
    dmid = dy + normalise_back(dnm, unit_mid, inv_mid, gains[1:2, :])
    dbr = dmid.astype(BF16)
    dbr_sel = nt(sel, dbr).astype(BF16)
    dnormed = jnp.zeros((PT, 384), F32)
    dpooled = jnp.zeros((PW, 384), F32)
    zero = jnp.zeros((PT, HEAD), BF16)
    for r in range(4):
        w = weights[r, :, 0:384]
        dmix = nn(dbr, w[:, 0:96]).astype(BF16)
        dq, dk, dv = attend_back(q_in[r], k_in[r], v_in[r], ok[...], fill[...], dmix)
        part[...] = jnp.zeros_like(part)
        part[:, 0:96] = mix_in[r]
        first = nn(dbr_sel, part[...])
        part[:, 0:96] = zero
        part[:, 96:192] = dq.astype(BF16)
        first = first + nn(nb_sel, part[...])
        dnormed = dnormed + nt(part[:, 0:256], w[:, 0:256])
        part[:, 96:192] = zero
        part[0:PW, 192:288] = (dk[0:PW] * 0.25).astype(BF16)
        part[0:PW, 288:384] = (dv[0:PW] * 0.25).astype(BF16)
        first = first + 4.0 * nn(pn_sel, part[0:PW, :])
        dpooled = dpooled + nt(part[0:PW, 128:384], w[:, 128:384])
        put(r, 0, first)
    dnormed = dnormed + jnp.concatenate([dpooled, dpooled, dpooled, dpooled], axis=0)
    dx = normalise_back(dnormed, unit_in, inv_in, gains[0:1, :]) + dmid
    vec = jnp.concatenate(
        [
            column_sum(dnormed * unit_in),
            column_sum(dnm * unit_mid),
            column_sum(dnormed),
            column_sum(dnm),
            column_sum(dmid),
            column_sum(dy),
            jnp.zeros((2, 384), F32),
        ],
        axis=0,
    )
    vec_out[...] = exact_nt(vec, p1[...])
    dxb = nt(dx.astype(BF16), p1[...]).astype(BF16)
    xgrad[...] = nn(token_back[...], dxb).astype(BF16)


def spec_vmem():
    return pl.BlockSpec(memory_space=pltpu.VMEM)


def spec_any():
    return pl.BlockSpec(memory_space=pl.ANY)


def spec_smem():
    return pl.BlockSpec(memory_space=pltpu.SMEM)


def call(body, inputs, kinds, outs, scratch, micros):
    specs = {"v": spec_vmem, "a": spec_any, "s": spec_smem}
    return pl.pallas_call(
        body,
        out_shape=outs,
        in_specs=[specs[k]() for k in kinds],
        out_specs=jax.tree.map(lambda _: spec_vmem(), outs),
        scratch_shapes=scratch,
        compiler_params=pltpu.CompilerParams(vmem_limit_bytes=VMEM_LIMIT),
        cost_estimate=pl.CostEstimate(flops=micros * 1_000_000_000, bytes_accessed=4_000_000, transcendentals=0),
    )(*inputs)


def shape(dims, dtype):
    return jax.ShapeDtypeStruct(dims, dtype)


CUT_ONE = 640
ORDER = ((0, 1, 3, 2), (0, 3, 1, 2))


def hop(v, axis, late):
    pairs = []
    for core in range(2):
        flip = 3 if (core == 1) != late else 1
        for xi in range(4):
            for zi in range(4):
                for yi in range(4):
                    tx, tz, ty = xi, zi, yi
                    if axis == "x":
                        tx = xi ^ flip
                    elif axis == "z":
                        tz = zi ^ flip
                    else:
                        ty = yi ^ flip
                    here = ((core * 4 + xi) * 4 + zi) * 4 + yi
                    pairs.append((here, ((core * 4 + tx) * 4 + tz) * 4 + ty))
    return lax.ppermute(v, ("pipe", "dp", "head"), pairs)


def swap(v):
    return lax.ppermute(v, "pipe", [(0, 1), (1, 0)])


def ring_pair(v, axis):
    low = jnp.stack([v, hop(v, axis, False)])
    return low, hop(low, axis, True)


def ring_rows(v, axis):
    low, high = ring_pair(v, axis)
    both = jnp.concatenate([low, high], axis=0)
    return jnp.moveaxis(both, 0, -3).reshape(v.shape[:-2] + (4 * v.shape[-2], v.shape[-1]))


def ring_stack(v, axis):
    low, high = ring_pair(v, axis)
    return jnp.concatenate([low, high], axis=0)


def gather_one(local):
    rows = ring_rows(local, "z")
    first = ring_rows(rows[:, :CUT_ONE], "x")
    last = ring_stack(rows[:, CUT_ONE:], "y")
    return ring_pair(first, "y") + ring_pair(last, "x"), (first, last)


def gather_two(local, ready):
    rows = ring_rows(local, "x")
    half = local.shape[1] // 2
    first = ring_stack(rows[:, :half], "y")
    last = ring_rows(rows[:, half:], "z")
    first, last = after((first, last), ready)
    return ring_pair(first, "z") + ring_pair(last, "y")


def ring_begin(keep, send, axis):
    got = hop(send, axis, True)
    onward = (keep[1].astype(F32) + got[1].astype(F32)).astype(keep.dtype)
    return keep[0].astype(F32) + got[0].astype(F32), onward


def ring_end(begun, axis):
    part, onward = begun
    return part + hop(onward, axis, False).astype(F32)


def ring_sum(keep, send, axis):
    return ring_end(ring_begin(keep, send, axis), axis)


def halves(v):
    rows = v.shape[-2] // 4
    parts = [v[..., rows * n : rows * n + rows, :] for n in range(4)]
    return jnp.stack(parts[:2]), jnp.stack(parts[2:])


def low(v):
    return v.astype(BF16)


def after(v, other):
    return lax.optimization_barrier((v, other))[0]


def lock(*values):
    return lax.optimization_barrier(values)


def send_clip(value, rounds):
    pairs = [(p * 4 + source, p * 4 + target) for p, source, target in rounds]
    return lax.ppermute(value, ("pipe", "head"), pairs)


def spread_near(v):
    return send_clip(v, [(0, 0, 1), (0, 1, 0), (1, 2, 3), (1, 3, 2)])


def spread_far(v, near, pipe, y):
    even = (y % 2) == 0
    both = jnp.stack([jnp.where(even, v, near), jnp.where(even, near, v)])
    far = send_clip(both, [(0, 0, 3), (0, 1, 2), (1, 2, 1), (1, 3, 0)])
    return jnp.where((y // 2) == pipe, both, far)[:, None]


def token_order():
    order = np.zeros((PT, TOK), np.float32)
    for block in range(4):
        for window in range(WIN):
            row = (window // 10) * 2 + block // 2
            col = (window % 10) * 2 + block % 2
            order[block * PW + window, row * GRID + col] = 1
    return order


def turn_matrix(core_from, core_to, rows_from, rows_to):
    def labels(core, outer):
        out = []
        for a in range(4):
            for b in range(4):
                one, two = ORDER[core][a], ORDER[core][b]
                out.append((one, two) if outer == "x" else (two, one))
        return out

    source, target = labels(core_from, rows_from), labels(core_to, rows_to)
    matrix = np.zeros((384, 384), np.float32)
    for n, label in enumerate(source):
        m = target.index(label)
        matrix[n * 24 : n * 24 + 24, m * 24 : m * 24 + 24] = np.eye(24)
    return jnp.asarray(matrix, BF16)


def per_device(
    clips_in, cotangent, token_mask, memory_valid, memory_one, memory_two,
    qkv_one, out_one, up_one, down_one, up_bias_one, gains_one, shifts_one,
    qkv_two, out_two, res_two, up_two, down_two, up_bias_two, gain_two_in, shift_two_in, gains_two, shifts_two,
):
    pipe = lax.axis_index("pipe")
    dp = lax.axis_index("dp")
    y = lax.axis_index("head")
    x_at, z_at = dp // 4, dp % 4
    first_core = pipe == 0

    one = jnp.concatenate([out_one.T, qkv_one[:, 0, :], up_one, down_one.T], axis=1)
    out_t, res_t = out_two.T, res_two.T
    q2 = qkv_two
    attn = jnp.concatenate(
        [
            out_t[:24], res_t[:24], q2[:, 0, :96],
            out_t[24:], res_t[24:], q2[:, 1, :96],
            q2[:, 0, 96:], q2[:, 1, 96:],
        ],
        axis=1,
    )
    down_t = down_two.T
    feed_up = jnp.concatenate([up_two[:24], up_two[24:]], axis=1)
    feed_down = jnp.concatenate([down_t[:24], down_t[24:]], axis=1)
    mine_one, ready = gather_one(jnp.where(first_core, one, attn))
    mine_two = gather_two(jnp.where(first_core, feed_up, feed_down), ready)
    other_one = tuple(swap(v) for v in mine_one)
    other_two = tuple(swap(v) for v in mine_two)

    def clip_of(v, at):
        return lax.dynamic_index_in_dim(v, at, 0, keepdims=False)

    near = jnp.where(first_core, 1, 3)
    far = 4 - near
    biases = jnp.concatenate([up_bias_one, up_bias_two])
    biases = jnp.concatenate(thirds(biases)).reshape(12, 288)
    memory = jnp.concatenate([memory_one[:, 0], memory_two[:, 0]], axis=-1)

    def payload(flip):
        part = clip_of(memory, y ^ flip).reshape(2 * MEMROWS, 288)
        return jnp.concatenate([part, biases], axis=0)

    got = hop(jnp.stack([payload(near), payload(2)]), "y", False)
    more = hop(jnp.stack([payload(far), got[1]]), "y", True)
    parcels = jnp.stack([payload(0), got[0], more[0], more[1]])
    memory = parcels[:, : 2 * MEMROWS].reshape(4, 2, MEMROWS, 288)
    mem_one, mem_two = memory[..., :96], memory[..., 96:]
    biases = parcels[:, 2 * MEMROWS :].astype(F32).reshape(4, 3, 1152)
    biases = biases[:, 0] + biases[:, 1] + biases[:, 2]
    bias_one, bias_two = biases[:, :384], biases[:, 384:]

    pipe, y, x_at, z_at = after((pipe, y, x_at, z_at), ready)
    first_core = pipe == 0

    flags = clip_of(token_mask[:, 0], y).reshape(10, 2, 10, 2)[:, 0, :, 0].reshape(WIN)
    key_ok = (flags > 0).astype(F32)
    mem_ok = jnp.repeat((clip_of(memory_valid[:, 0], y) > 0).astype(F32), MEMROWS // 2)
    gap = jnp.zeros((MEM0 - WIN,), F32)
    tail = jnp.zeros((KEYS - MEM0 - MEMROWS,), F32)
    ok = jnp.concatenate([key_ok, gap, mem_ok, tail]).reshape(1, KEYS)
    fill = np.full((1, KEYS), ABSENT, np.float32)
    fill[0, :WIN] = MASKED
    fill[0, MEM0 : MEM0 + MEMROWS] = MASKED
    fill = jnp.asarray(fill)
    key_col = jnp.concatenate([key_ok, jnp.zeros((PW - WIN,), F32)]).reshape(PW, 1)

    def order_of(core, n):
        return jnp.asarray(ORDER[core], jnp.int32)[n]

    def own_order(n):
        return jnp.where(first_core, order_of(0, n), order_of(1, n))

    k = np.arange(384)
    k_outer, k_inner, k_row = k // 96, (k // 24) % 4, k % 24

    def chip(a, b):
        return (x_at ^ a) * 4 + (z_at ^ b)

    piece0 = chip(order_of(0, k_outer), order_of(0, k_inner))
    piece1 = chip(order_of(1, k_outer), order_of(1, k_inner))
    raw0 = piece0 * 24 + k_row
    raw1 = piece1 * 24 + k_row
    raw2 = jnp.concatenate([piece1 * 48 + k_row, piece1 * 48 + 24 + k_row])
    p1a = (k[:, None] == raw0[None, :]).astype(BF16)
    p1b = (k[:, None] == raw1[None, :]).astype(BF16)
    p2 = (np.arange(768)[:, None] == raw2[None, :]).astype(BF16)
    head_raw = (y ^ own_order(k // 96)) * 96 + k % 96
    pr = (raw1[:, None] == head_raw[None, :]).astype(BF16)
    j = np.arange(192)
    j_outer, j_inner, j_row = own_order(j // 48), own_order((j // 12) % 4), j % 12
    rows_x = pipe * 192 + chip(j_outer, j_inner) * 12 + j_row
    s1a = (rows_x[:, None] == raw0[None, :]).astype(BF16)
    s1b = (rows_x[:, None] == raw1[None, :]).astype(BF16)
    rows_x2 = pipe * 384 + chip(j_outer, j_inner) * 24 + j_row
    rows_z2 = pipe * 384 + chip(j_inner, j_outer) * 24 + j_row
    s2 = (jnp.concatenate([rows_x2, rows_x2 + 12])[:, None] == raw2[None, :]).astype(BF16)
    s2f = (jnp.concatenate([rows_z2, rows_z2 + 12])[:, None] == raw2[None, :]).astype(BF16)
    turn = turn_matrix(0, 1, "x", "x")
    to_up = turn_matrix(1, 0, "x", "z")
    to_down = turn_matrix(1, 1, "x", "z")

    order = token_order()
    token_perm = jnp.asarray(order, BF16)
    token_back = jnp.asarray(order.T, BF16)
    vec384 = jnp.concatenate([gains_one, shifts_one, gain_two_in[None], shift_two_in[None]], axis=0)
    gains_in = jnp.concatenate([gain_two_in[None], jnp.zeros((7, 384), F32)], axis=0)
    vec768 = jnp.concatenate([gains_two[None], shifts_two], axis=0)
    gains2 = jnp.take(vec768, raw2, axis=1)
    place = pipe.astype(jnp.int32).reshape(1)
    x = clip_of(clips_in[:, 0], y)
    cot = clip_of(cotangent[:, 0], y)

    dma = pltpu.SemaphoreType.DMA
    saved = call(
        forward,
        (
            place, x, token_perm, p1a, turn, pr, vec384, gains2[2:3], ok, fill, mem_one, mem_two, bias_one,
            *mine_one, *other_one,
        ),
        "s" + "v" * 12 + "a" * 8,
        (
            shape((PT, 384), BF16), shape((PT, 384), BF16),
            shape((4, PT, HEAD), BF16), shape((4, KEYS, HEAD), BF16), shape((4, KEYS, HEAD), BF16),
            shape((4, PT, HEAD), BF16), shape((PT, 384), F32),
            shape((4, PT, 384), BF16), shape((4, PT, 384), F32),
            shape((PW, 384), BF16), shape((8, PW, HEAD), BF16), shape((8, KEYS, HEAD), BF16),
            shape((8, KEYS, HEAD), BF16), shape((4, PW, 384), BF16), shape((PW, 768), F32),
        ),
        [
            pltpu.VMEM((4, 384, 1152), BF16), pltpu.VMEM((4, 384, 1152), BF16), pltpu.VMEM((8, 384), F32),
            dma(()), dma(()),
        ],
        18,
    )
    passed, x_kept, q1, k1, v1, mix1, mid1, act1, slope1, pn2, q2k, k2, v2, mix2, mid2 = saved

    feed = call(
        feed_two,
        (place, mid2, cot, key_col, p2, to_up, to_down, s2f, gains2, bias_two, *mine_two, *other_two),
        "s" + "v" * 9 + "a" * 8,
        (
            shape((WIN, 768), BF16), shape((PW, 768), F32), shape((8, 768), F32), shape((4, 768), F32),
            shape((2, 4, 48, 1536), BF16), shape((2, 4, 48, 1536), BF16),
            shape((2, 192, 1536), BF16), shape((2, 192, 1536), BF16),
        ),
        [
            pltpu.VMEM((4, 384, 1536), BF16), pltpu.VMEM((4, 384, 1536), BF16),
            pltpu.VMEM((4, PW, 768), BF16), pltpu.VMEM((4, PW, 768), F32), dma(()), dma(()),
        ],
        14,
    )
    activation, dmid2, vec_mid, dbias_two, keep_rows, send_rows, keep_y, send_y = feed
    feed_a = ring_begin(keep_rows, send_rows, "z")
    feed_b = ring_begin(keep_y, send_y, "y")

    second = call(
        second_backward,
        (
            place, dmid2, passed, pn2, q2k, k2, v2, mix2, p1b, pr, s1b, s2, gains_in, ok, fill,
            *mine_one, *other_one,
        ),
        "s" + "v" * 14 + "a" * 8,
        (
            shape((PT, 384), BF16), shape((8, 384), F32),
            shape((2, 4, 48, 1152), BF16), shape((2, 4, 48, 1152), BF16),
        ),
        [pltpu.VMEM((4, 384, 1152), BF16), pltpu.VMEM((3, PW, 384), BF16), dma(())],
        10,
    )
    dpassed, vec_in, keep_attn, send_attn = second
    dpassed, activation = after((dpassed, activation), (feed_a[1], feed_b[1]))
    keep_attn, send_attn = after((keep_attn, send_attn), (feed_a[1], feed_b[1]))
    attn_sum = ring_begin(keep_attn, send_attn, "x")
    feed_a = low(ring_end(feed_a, "z"))
    feed_b = low(ring_end(feed_b, "y"))
    act_near = spread_near(activation)

    third = call(
        first_backward,
        (
            place, dpassed, x_kept, q1, k1, v1, mix1, mid1, act1, slope1,
            token_back, p1a, turn, s1a, vec384, ok, fill, *mine_one, *other_one,
        ),
        "s" + "v" * 16 + "a" * 8,
        (
            shape((TOK, 384), BF16), shape((8, 384), F32), shape((4, 384), F32),
            shape((2, 192, 1152), BF16), shape((2, 192, 1152), BF16),
        ),
        [
            pltpu.VMEM((4, 384, 1152), BF16), pltpu.VMEM((8, 384), F32), pltpu.VMEM((PT, 384), BF16), dma(()),
        ],
        16,
    )
    third, feed_a, feed_b, attn_sum, act_near = lock(third, feed_a, feed_b, attn_sum, act_near)
    xgrad, vec_one, dbias_one, keep_one, send_one = third

    vectors = jnp.concatenate([vec_one[:6].reshape(-1), vec_in[:2].reshape(-1), vec_mid[:4].reshape(-1)])
    vectors = vectors.reshape(48, 128)
    dbias = jnp.concatenate([dbias_one, dbias_two], axis=1).reshape(4, 9, 128)

    one_sum = ring_begin(keep_one, send_one, "y")
    got = hop(jnp.concatenate([vectors, dbias[2], dbias[3]], axis=0), "y", True)
    feed_a = ring_begin(feed_a[0:2], feed_a[2:4], "y")
    feed_b = ring_begin(*halves(feed_b), "z")
    attn_sum = low(ring_end(attn_sum, "x"))
    vectors = vectors + got[:48]
    dkeep = dbias[1] + got[57:]
    own = jnp.concatenate([vectors, dbias[0] + got[48:57]], axis=0)
    vectors = jnp.concatenate([vectors, dkeep], axis=0)
    one_sum, vectors, feed_a, feed_b, attn_sum, xgrad = lock(one_sum, vectors, feed_a, feed_b, attn_sum, xgrad)

    one_sum = low(ring_end(one_sum, "y"))
    vectors = own + hop(vectors, "y", False)
    feed_a = low(ring_end(feed_a, "y"))
    feed_b = low(ring_end(feed_b, "z"))
    attn_sum = ring_begin(attn_sum[0:2], attn_sum[2:4], "y")
    grad_near = spread_near(xgrad)
    one_sum, vectors, feed_a, feed_b, attn_sum, grad_near = lock(
        one_sum, vectors, feed_a, feed_b, attn_sum, grad_near
    )

    one_sum = ring_begin(*halves(one_sum), "x")
    vectors = vectors + hop(vectors, "x", True)
    feed_sum = ring_begin(*halves(jnp.concatenate([feed_a, feed_b], axis=1)), "x")
    attn_sum = low(ring_end(attn_sum, "y"))
    input_grad = spread_far(xgrad, grad_near, pipe, y)
    one_sum, vectors, feed_sum, attn_sum, act_near = lock(one_sum, vectors, feed_sum, attn_sum, act_near)

    one_sum = low(ring_end(one_sum, "x"))
    vectors = vectors + hop(vectors, "x", False)
    feed_sum = ring_end(feed_sum, "x")
    activations = spread_far(activation, act_near, pipe, y)
    one_sum, vectors = lock(one_sum, vectors)

    rest_sum = ring_begin(*halves(jnp.concatenate([one_sum, attn_sum], axis=1)), "z")
    vectors = vectors + hop(vectors, "z", True)
    rest_sum, vectors = lock(rest_sum, vectors)

    rest_sum = ring_end(rest_sum, "z")
    vectors = vectors + hop(vectors, "z", False)
    vectors = vectors.reshape(-1)
    v_one = vectors[:2304].reshape(6, 384)
    v_in = vectors[2304:3072].reshape(2, 384)
    v_mid = vectors[3072:6144].reshape(4, 768)

    g1, ga = rest_sum[:, :1152], rest_sum[:, 1152:]
    fa, fb = feed_sum[:, :1536], feed_sum[:, 1536:]
    grad_qkv_two = jnp.stack(
        [
            jnp.concatenate([ga[:, 288:384], ga[:, 768:960]], axis=1),
            jnp.concatenate([ga[:, 672:768], ga[:, 960:1152]], axis=1),
        ],
        axis=1,
    )
    return (
        activations,
        input_grad,
        g1[:, None, 96:384],
        g1[:, :96].T,
        g1[:, 384:768],
        g1[:, 768:].T,
        vectors[6144:6528],
        v_one[:2],
        v_one[2:],
        grad_qkv_two,
        jnp.concatenate([ga[:, 0:192], ga[:, 384:576]], axis=0).T,
        jnp.concatenate([ga[:, 192:288], ga[:, 576:672]], axis=0).T,
        jnp.concatenate([fa[:, :768], fb[:, :768]], axis=0),
        jnp.concatenate([fa[:, 768:], fb[:, 768:]], axis=0).T,
        vectors[6528:],
        v_in[0],
        v_in[1],
        v_mid[0],
        v_mid[1:],
    )


def solution(mesh):
    return jax.shard_map(
        per_device,
        mesh=mesh,
        in_specs=(
            P(None, "dp", None, None), P(None, "dp", None, None), P(None, "dp", None), P(None, "dp", None),
            P(None, "dp", None, None, "head"), P(None, "dp", None, None, "head"),
            P("dp", "head", None), P("head", "dp"), P("dp", "head"), P("head", "dp"), P("head"), P(), P(),
            P("dp", "head", None), P("head", "dp"), P("head", "dp"), P("dp", "head"), P("head", "dp"), P("head"),
            P(), P(), P(), P(),
        ),
        out_specs=(
            P("pipe", "dp", None, None), P("pipe", "dp", None, None),
            P(("pipe", "dp"), "head", None), P("head", ("pipe", "dp")), P(("pipe", "dp"), "head"),
            P("head", ("pipe", "dp")), P("head"), P(), P(),
            P(("pipe", "dp"), "head", None), P("head", ("pipe", "dp")), P("head", ("pipe", "dp")),
            P(("pipe", "dp"), "head"), P("head", ("pipe", "dp")), P("head"), P(), P(), P(), P(),
        ),
        check_vma=False,
    )
```

```python
import functools

import jax
import jax.numpy as jnp
import numpy as np
from jax import lax
from jax.experimental import pallas as pl
from jax.experimental.pallas import tpu as pltpu
from jax.sharding import PartitionSpec as P

F32 = jnp.float32
BF16 = jnp.bfloat16
GRID = 20
TOK = 400
WIN = 100
PW = 104
PT = 4 * PW
KEYS = 256
MEM0 = 112
MEMROWS = 50
HEAD = 96
EPS = 1e-06
MASKED = -1000000000.0
ABSENT = -3e38
SCALE = HEAD ** (-0.5)
VMEM_LIMIT = 56 * 1024 * 1024


def nn(a, b):
    return lax.dot_general(a, b, (((1,), (0,)), ((), ())), preferred_element_type=F32)


def nt(a, b):
    return lax.dot_general(a, b, (((1,), (1,)), ((), ())), preferred_element_type=F32)


def tn(a, b):
    return lax.dot_general(a, b, (((0,), (0,)), ((), ())), preferred_element_type=F32)


def thirds(v):
    high = v.astype(BF16)
    rest = v - high.astype(F32)
    mid = rest.astype(BF16)
    low = (rest - mid.astype(F32)).astype(BF16)
    return high, mid, low


def exact_nn(v, m):
    a, b, c = thirds(v)
    return nn(a, m) + nn(b, m) + nn(c, m)


def exact_nt(v, m):
    a, b, c = thirds(v)
    return nt(a, m) + nt(b, m) + nt(c, m)


def normalise(v):
    average = jnp.mean(v, axis=-1, keepdims=True)
    centred = v - average
    variance = jnp.mean(centred * centred, axis=-1, keepdims=True)
    inverse = lax.rsqrt(variance + EPS)
    return centred * inverse, inverse


def normalise_back(grad, unit, inverse, gain):
    scaled = grad * gain
    mean_one = jnp.mean(scaled, axis=-1, keepdims=True)
    mean_two = jnp.mean(scaled * unit, axis=-1, keepdims=True)
    return inverse * (scaled - mean_one - unit * mean_two)


def column_sum(v):
    return jnp.sum(v, axis=0, keepdims=True)


def gelu_both(h):
    cdf = 0.5 + 0.5 * lax.erf(h * 0.7071067811865476)
    density = 0.3989422804014327 * jnp.exp(-0.5 * h * h)
    return h * cdf, cdf + h * density


def pool_rows(v):
    return 0.25 * (v[0:PW] + v[PW : 2 * PW] + v[2 * PW : 3 * PW] + v[3 * PW : 4 * PW])


def softmax_rows(scores, ok, fill):
    scores = jnp.where(ok > 0, scores * SCALE, fill)
    peak = jnp.max(scores, axis=-1, keepdims=True)
    expos = jnp.exp(scores - peak)
    return expos / jnp.sum(expos, axis=-1, keepdims=True)


def attend_back(q, keys, values, ok, fill, dmix):
    shares = softmax_rows(nt(q, keys), ok, fill)
    dvalues = tn(shares.astype(BF16), dmix)
    dshares = nt(dmix, values)
    inner = jnp.sum(shares * dshares, axis=-1, keepdims=True)
    dscores = (shares * (dshares - inner)).astype(BF16)
    dq = nn(dscores, keys) * SCALE + dmix.astype(F32)
    dkeys = tn(dscores, q) * SCALE
    return dq, dkeys, dvalues


def close_nt(v, m):
    high = v.astype(BF16)
    return nt(high, m) + nt((v - high.astype(F32)).astype(BF16), m)


def load_weights(core, owner, mine, other, dst, sem):
    def copies(groups, places):
        at = 0
        for kind, low, high in groups:
            cols = pl.ds(at, low.shape[-1])
            at += low.shape[-1]
            for n in range(4):
                slab = (low if n < 2 else high).at[n % 2]
                if kind == "y":
                    pltpu.make_async_copy(slab, dst.at[places[n], :, cols], sem).start()
                else:
                    for h in range(4):
                        pltpu.make_async_copy(slab.at[h], dst.at[places[h], pl.ds(96 * n, 96), cols], sem).start()

    @pl.when(core == owner)
    def _():
        copies(mine, (0, 1, 2, 3))

    @pl.when(core != owner)
    def _():
        copies(other, (0, 2, 1, 3))


def wait_weights(dst, sem):
    pltpu.make_async_copy(dst, dst, sem).wait()


def groups_one(refs):
    return [("y", refs[0], refs[1]), ("rows", refs[2], refs[3])]


def groups_two(refs):
    return [("rows", refs[0], refs[1]), ("y", refs[2], refs[3])]


def forward(
    place, x, token_perm, p1, turn, pr, vec384, ok, fill, mem_one, mem_two, bias_up, *rest
):
    mine, other = groups_one(rest[0:4]), groups_one(rest[4:8])
    (passed, x_out, q_out, k_out, v_out, mix_out, mid_out, act_out, slope_out,
     pn_out, q2_out, k2_out, v2_out, mix2_out, mid2_out) = rest[8:23]
    w1, wa, gains, sem_one, sem_attn = rest[23:28]
    load_weights(place[0], 0, mine, other, w1, sem_one)
    load_weights(place[0], 1, mine, other, wa, sem_attn)
    gains[...] = exact_nn(vec384[...], p1[...])
    xb = nn(x[...], p1[...]).astype(BF16)
    xb = nn(token_perm[...], xb).astype(BF16)
    x_out[...] = xb
    xf = xb.astype(F32)
    unit, _ = normalise(xf)
    normed = unit * gains[0:1, :] + gains[2:3, :]
    nb = normed.astype(BF16)
    pn = pool_rows(normed).astype(BF16)
    k_out[...] = jnp.zeros_like(k_out)
    v_out[...] = jnp.zeros_like(v_out)
    k2_out[...] = jnp.zeros_like(k2_out)
    v2_out[...] = jnp.zeros_like(v2_out)
    mix2_out[...] = jnp.zeros_like(mix2_out)
    wait_weights(w1, sem_one)
    branch = jnp.zeros((PT, 384), F32)
    for r in range(4):
        w = w1[r, :, 0:384]
        q = nn(nb, w[:, 0:256])[:, 96:192].astype(BF16)
        kv = nn(pn, w)
        q_out[r] = q
        k_out[r, 0:PW, :] = kv[:, 192:288].astype(BF16)
        v_out[r, 0:PW, :] = kv[:, 288:384].astype(BF16)
        k_out[r, MEM0 : MEM0 + MEMROWS, :] = mem_one[r, 0]
        v_out[r, MEM0 : MEM0 + MEMROWS, :] = mem_one[r, 1]
        shares = softmax_rows(nt(q, k_out[r]), ok[...], fill[...])
        mixed = (nn(shares.astype(BF16), v_out[r]) + q.astype(F32)).astype(BF16)
        mix_out[r] = mixed
        branch = branch + nt(mixed, w[:, 0:96])
    middle = xf + gains[4:5, :] + branch
    mid_out[...] = middle
    unit, _ = normalise(middle)
    nm = (unit * gains[1:2, :] + gains[3:4, :]).astype(BF16)
    total = middle + gains[5:6, :]
    for r in range(4):
        hidden = nn(nm, w1[r, :, 384:768]) + bias_up[r : r + 1, :]
        active, slope = gelu_both(hidden)
        active = active.astype(BF16)
        act_out[r] = active
        slope_out[r] = slope.astype(BF16)
        total = total + nt(active, w1[r, :, 768:1152])
    xb = nn(total.astype(BF16), turn[...]).astype(BF16)
    passed[...] = xb

    xf = xb.astype(F32)
    gains[...] = exact_nn(gains[...], turn[...])
    unit, _ = normalise(xf)
    normed = unit * gains[6:7, :] + gains[7:8, :]
    pn = pool_rows(normed).astype(BF16)
    pn_out[...] = pn
    pnr = nn(pn, pr[...]).astype(BF16)
    wait_weights(wa, sem_attn)
    branch = [jnp.zeros((PW, 384), F32), jnp.zeros((PW, 384), F32)]
    for r in range(4):
        kv = nn(pn, wa[r, :, 768:1152])
        mix2_out[r, :, 192:288] = pnr[:, r * 96 : (r + 1) * 96]
        for h in range(2):
            q = nn(pn, wa[r, :, 384 * h + 256 : 384 * h + 384])[:, 32:128].astype(BF16)
            n = 2 * r + h
            q2_out[n] = q
            k2_out[n, 0:PW, :] = kv[:, 192 * h : 192 * h + 96].astype(BF16)
            v2_out[n, 0:PW, :] = kv[:, 192 * h + 96 : 192 * h + 192].astype(BF16)
            k2_out[n, MEM0 : MEM0 + MEMROWS, :] = mem_two[r, 0, :, 96 * h : 96 * h + 96]
            v2_out[n, MEM0 : MEM0 + MEMROWS, :] = mem_two[r, 1, :, 96 * h : 96 * h + 96]
            shares = softmax_rows(nt(q, k2_out[n]), ok[...], fill[...])
            mixed = (nn(shares.astype(BF16), v2_out[n]) + q.astype(F32)).astype(BF16)
            mix2_out[r, :, 96 * h : 96 * h + 96] = mixed
        for s in range(2):
            branch[s] = branch[s] + nt(mix2_out[r], wa[r, :, 384 * s : 384 * s + 384])
    mid2_out[...] = jnp.concatenate(branch, axis=1)


def feed_two(place, middle_in, cot, key_ok, p2, to_up, to_down, s2f, vec768, bias_up, *rest):
    mine, other = groups_two(rest[0:4]), groups_two(rest[4:8])
    act_out, dmid_out, vec_out, bias_out, keep_rows, send_rows, keep_y, send_y = rest[8:16]
    wu, wd, acts, slopes, sem_u, sem_d = rest[16:22]
    load_weights(place[0], 0, mine, other, wu, sem_u)
    load_weights(place[0], 1, mine, other, wd, sem_d)
    gains2 = exact_nn(vec768[...], p2[...])
    middle = middle_in[...] + gains2[2:3, :]
    unit, inverse = normalise(middle)
    nm = (unit * gains2[0:1, :] + gains2[1:2, :]).astype(BF16)
    nm_up = [nn(nm[:, 384 * s : 384 * s + 384], to_up[...]).astype(BF16) for s in range(2)]
    dyb = nn(cot[...], p2[...]).astype(BF16)
    dyb = jnp.concatenate([dyb, jnp.zeros((PW - WIN, 768), BF16)], axis=0)
    dy = dyb.astype(F32) * key_ok[...]
    dyb = dy.astype(BF16)
    dy_down = [nn(dyb[:, 384 * s : 384 * s + 384], to_down[...]).astype(BF16) for s in range(2)]
    dy_sel = nt(s2f[...], dyb).astype(BF16)
    nm_sel = nt(s2f[...], nm).astype(BF16)
    wait_weights(wu, sem_u)
    for r in range(4):
        hidden = nn(nm_up[0], wu[r, :, 0:768]) + nn(nm_up[1], wu[r, :, 768:1536])
        active, slope = gelu_both(hidden + bias_up[r : r + 1, :])
        acts[r] = active.astype(BF16)
        slopes[r] = slope
    wait_weights(wd, sem_d)

    def put_rows(r, lo, value):
        value = value.astype(BF16)
        for k in range(4):
            out = keep_rows if k < 2 else send_rows
            out[k % 2, r, :, lo : lo + 768] = value[48 * k : 48 * k + 48]

    def put_head(r, lo, value):
        out = keep_y if r < 2 else send_y
        out[r % 2, :, lo : lo + 768] = value.astype(BF16)

    down = [jnp.zeros((PW, 384), F32), jnp.zeros((PW, 384), F32)]
    dnm = [jnp.zeros((PW, 384), F32), jnp.zeros((PW, 384), F32)]
    for r in range(4):
        active = acts[r]
        dact = nn(dy_down[0], wd[r, :, 0:768]) + nn(dy_down[1], wd[r, :, 768:1536])
        dh = (dact * slopes[r]).astype(BF16)
        bias_out[r : r + 1, :] = column_sum(dh.astype(F32))
        put_rows(r, 0, nn(nm_sel[0:192], dh))
        put_rows(r, 768, nn(dy_sel[0:192], active))
        put_head(r, 0, nn(nm_sel[192:384], dh))
        put_head(r, 768, nn(dy_sel[192:384], active))
        for s in range(2):
            down[s] = down[s] + nt(active, wd[r, :, 768 * s : 768 * s + 768])
            dnm[s] = dnm[s] + nt(dh, wu[r, :, 768 * s : 768 * s + 768])
    down = jnp.concatenate([close_nt(v, to_down[...]) for v in down], axis=1)
    output = (middle + gains2[3:4, :] + down).astype(BF16)
    act_out[...] = nt(output, p2[...])[0:WIN].astype(BF16)
    dnm = jnp.concatenate([close_nt(v, to_up[...]) for v in dnm], axis=1)
    dmid = dy + normalise_back(dnm, unit, inverse, gains2[0:1, :])
    dmid_out[...] = dmid
    vec = jnp.concatenate(
        [
            column_sum(dnm * unit),
            column_sum(dnm),
            column_sum(dmid),
            column_sum(dy),
            jnp.zeros((4, 768), F32),
        ],
        axis=0,
    )
    vec_out[...] = exact_nt(vec, p2[...])


def second_backward(
    place, dmid, passed, pn_in, queries, keys, values, mixes, p1, pr, s1, s2, gains_in, ok, fill, *rest
):
    mine, other = groups_one(rest[0:4]), groups_one(rest[4:8])
    dpassed, vec_out, keep, send = rest[8:12]
    wa, part, sem = rest[12:15]
    load_weights(place[0], 1, mine, other, wa, sem)
    xf = passed[...].astype(F32)
    unit, inverse = normalise(xf)
    pn = pn_in[...]
    dbr = dmid[...].astype(BF16)
    dbr_sel = nt(s2[...], dbr).astype(BF16)
    pn_sel = nt(s1[...], pn).astype(BF16)
    dpooled = jnp.zeros((PW, 384), F32)
    part[...] = jnp.zeros_like(part)
    wait_weights(wa, sem)

    def put(r, lo, value):
        out = keep if r < 2 else send
        out[r % 2, :, lo : lo + 384] = value.astype(BF16)

    dres = []
    for r in range(4):
        dmm = nn(dbr[:, 0:384], wa[r, :, 0:384]) + nn(dbr[:, 384:768], wa[r, :, 384:768])
        dres.append(dmm[:, 192:288])
        for h in range(2):
            n = 2 * r + h
            dmix = dmm[:, 96 * h : 96 * h + 96].astype(BF16)
            dq, dk, dv = attend_back(queries[n], keys[n], values[n], ok[...], fill[...], dmix)
            part[h, :, 288:384] = dq.astype(BF16)
            part[2, :, 192 * h : 192 * h + 96] = dk[0:PW].astype(BF16)
            part[2, :, 192 * h + 96 : 192 * h + 192] = dv[0:PW].astype(BF16)
        for s in range(2):
            put(r, 384 * s, nn(dbr_sel[192 * s : 192 * s + 192], mixes[r]) + nn(pn_sel, part[s]))
            dpooled = dpooled + nt(part[s], wa[r, :, 384 * s : 384 * s + 384])
        put(r, 768, nn(pn_sel, part[2]))
        dpooled = dpooled + nt(part[2], wa[r, :, 768:1152])
    dpooled = dpooled + close_nt(jnp.concatenate(dres, axis=1), pr[...])
    dpooled = dpooled * 0.25
    dnormed = jnp.concatenate([dpooled, dpooled, dpooled, dpooled], axis=0)
    gain = exact_nn(gains_in[...], p1[...])[0:1]
    dpassed[...] = normalise_back(dnormed, unit, inverse, gain).astype(BF16)
    vec = jnp.concatenate(
        [column_sum(dnormed * unit), column_sum(dnormed), jnp.zeros((6, 384), F32)], axis=0
    )
    vec_out[...] = exact_nt(vec, p1[...])


def first_backward(
    place, dpassed, x, q_in, k_in, v_in, mix_in, mid_in, act_in, slope_in,
    token_back, p1, turn, s1, vec384, ok, fill, vec_mid, vec_in, dbias_two, *rest
):
    mine, other = groups_one(rest[0:4]), groups_one(rest[4:8])
    xgrad, vec_keep, vec_send, keep, send = rest[8:13]
    weights, gains, part, sem = rest[13:17]
    load_weights(place[0], 0, mine, other, weights, sem)
    gains[...] = exact_nn(vec384[...], p1[...])
    xf = x[...].astype(F32)
    unit_in, inv_in = normalise(xf)
    normed = unit_in * gains[0:1, :] + gains[2:3, :]
    nb = normed.astype(BF16)
    pn = pool_rows(normed).astype(BF16)
    middle = mid_in[...]
    unit_mid, inv_mid = normalise(middle)
    nm = (unit_mid * gains[1:2, :] + gains[3:4, :]).astype(BF16)
    sel = s1[...]
    dyb = nt(dpassed[...], turn[...]).astype(BF16)
    dy = dyb.astype(F32)
    dy_sel = nt(sel, dyb).astype(BF16)
    nm_sel = nt(sel, nm).astype(BF16)
    nb_sel = nt(sel, nb).astype(BF16)
    pn_sel = nt(sel, pn).astype(BF16)
    wait_weights(weights, sem)

    def put(r, lo, value):
        value = value.astype(BF16)
        for k in range(4):
            out = keep if k < 2 else send
            out[k % 2, r, :, lo : lo + 384] = value[48 * k : 48 * k + 48]

    dnm = jnp.zeros((PT, 384), F32)
    for r in range(4):
        dact = nn(dyb, weights[r, :, 768:1152])
        dh = (dact * slope_in[r].astype(F32)).astype(BF16)
        row = 8 + 2 * (r % 2)
        out = vec_keep if r < 2 else vec_send
        out[row : row + 1, :] = dbias_two[r : r + 1, :]
        out[row + 1 : row + 2, 0:384] = column_sum(dh.astype(F32))
        out[row + 1 : row + 2, 384:768] = jnp.zeros((1, 384), F32)
        put(r, 768, nn(dy_sel, act_in[r]))
        put(r, 384, nn(nm_sel, dh))
        dnm = dnm + nt(dh, weights[r, :, 384:768])
    dmid = dy + normalise_back(dnm, unit_mid, inv_mid, gains[1:2, :])
    dbr = dmid.astype(BF16)
    dbr_sel = nt(sel, dbr).astype(BF16)
    dnormed = jnp.zeros((PT, 384), F32)
    dpooled = jnp.zeros((PW, 384), F32)
    zero = jnp.zeros((PT, HEAD), BF16)
    for r in range(4):
        w = weights[r, :, 0:384]
        dmix = nn(dbr, w[:, 0:96]).astype(BF16)
        dq, dk, dv = attend_back(q_in[r], k_in[r], v_in[r], ok[...], fill[...], dmix)
        part[...] = jnp.zeros_like(part)
        part[:, 0:96] = mix_in[r]
        first = nn(dbr_sel, part[...])
        part[:, 0:96] = zero
        part[:, 96:192] = dq.astype(BF16)
        first = first + nn(nb_sel, part[...])
        dnormed = dnormed + nt(part[:, 0:256], w[:, 0:256])
        part[:, 96:192] = zero
        part[0:PW, 192:288] = (dk[0:PW] * 0.25).astype(BF16)
        part[0:PW, 288:384] = (dv[0:PW] * 0.25).astype(BF16)
        first = first + 4.0 * nn(pn_sel, part[0:PW, :])
        dpooled = dpooled + nt(part[0:PW, 128:384], w[:, 128:384])
        put(r, 0, first)
    dnormed = dnormed + jnp.concatenate([dpooled, dpooled, dpooled, dpooled], axis=0)
    dx = normalise_back(dnormed, unit_in, inv_in, gains[0:1, :]) + dmid
    vec = jnp.concatenate(
        [
            column_sum(dnormed * unit_in),
            column_sum(dnm * unit_mid),
            column_sum(dnormed),
            column_sum(dnm),
            column_sum(dmid),
            column_sum(dy),
            jnp.zeros((2, 384), F32),
        ],
        axis=0,
    )
    vec = exact_nt(vec, p1[...])
    for out in (vec_keep, vec_send):
        out[0:4, :] = vec_mid[0:4, :]
        for k in range(3):
            out[4 + k : 5 + k, 0:384] = vec[2 * k : 2 * k + 1, :]
            out[4 + k : 5 + k, 384:768] = vec[2 * k + 1 : 2 * k + 2, :]
        out[7:8, 0:384] = vec_in[0:1, :]
        out[7:8, 384:768] = vec_in[1:2, :]
    dxb = nt(dx.astype(BF16), p1[...]).astype(BF16)
    xgrad[...] = nn(token_back[...], dxb).astype(BF16)


def local_shards(place, out_one, qkv_one, up_one, down_one, out_two, res_two, qkv_two, up_two, down_two, first, second):
    @pl.when(place[0] == 0)
    def _():
        first[:, 0:96] = out_one[...]
        first[:, 96:384] = qkv_one[0]
        first[:, 384:768] = up_one[...]
        first[:, 768:1152] = down_one[...]
        up = up_two[...].astype(F32)
        second[:, 0:768] = up[0:24].astype(BF16)
        second[:, 768:1536] = up[24:48].astype(BF16)

    @pl.when(place[0] != 0)
    def _():
        out_t, res_t = out_two[...].astype(F32), res_two[...].astype(F32)
        for s in range(2):
            first[:, 384 * s : 384 * s + 192] = out_t[24 * s : 24 * s + 24].astype(BF16)
            first[:, 384 * s + 192 : 384 * s + 288] = res_t[24 * s : 24 * s + 24].astype(BF16)
            first[:, 384 * s + 288 : 384 * s + 384] = qkv_two[:, s, 0:96]
            first[:, 768 + 192 * s : 960 + 192 * s] = qkv_two[:, s, 96:288]
        down = down_two[...].astype(F32)
        second[:, 0:768] = down[0:24].astype(BF16)
        second[:, 768:1536] = down[24:48].astype(BF16)


def feed_outputs(part, got, grad_up, grad_down):
    total = part[...] + got[...].astype(F32)
    grad_up[0:12, :] = total[:, 0:768]
    grad_up[12:24, :] = total[:, 1536:2304]
    grad_down[0:12, :] = total[:, 768:1536]
    grad_down[12:24, :] = total[:, 2304:3072]


def last_outputs(
    part, got, vec_part, vec_got,
    qkv1, out1, up1, down1, bias1, gains1, shifts1, qkv2, out2, res2, bias2, gain_in, shift_in, gain_mid, shifts2,
):
    total = part[...] + got[...].astype(F32)
    vec = vec_part[...] + vec_got[...]
    out1[...] = total[:, 0:96]
    qkv1[:, 0, :] = total[:, 96:384]
    up1[...] = total[:, 384:768]
    down1[...] = total[:, 768:1152]
    for s in range(2):
        at = 1152 + 384 * s
        out2[12 * s : 12 * s + 12, :] = total[:, at : at + 192]
        res2[12 * s : 12 * s + 12, :] = total[:, at + 192 : at + 288]
        qkv2[:, s, 0:96] = total[:, at + 288 : at + 384]
        qkv2[:, s, 96:288] = total[:, 1920 + 192 * s : 2112 + 192 * s]
    gain_mid[...] = vec[0]
    shifts2[...] = vec[1:4, :]
    gains1[0:1, :] = vec[4:5, 0:384]
    gains1[1:2, :] = vec[4:5, 384:768]
    for n in range(2):
        shifts1[2 * n : 2 * n + 1, :] = vec[5 + n : 6 + n, 0:384]
        shifts1[2 * n + 1 : 2 * n + 2, :] = vec[5 + n : 6 + n, 384:768]
    gain_in[...] = vec[7, 0:384]
    shift_in[...] = vec[7, 384:768]
    bias2[...] = vec[8]
    bias1[...] = vec[9, 0:384]


def spec_vmem():
    return pl.BlockSpec(memory_space=pltpu.VMEM)


def spec_any():
    return pl.BlockSpec(memory_space=pltpu.HBM)


def spec_smem():
    return pl.BlockSpec(memory_space=pltpu.SMEM)


def call(body, inputs, kinds, outs, scratch, micros):
    specs = {"v": spec_vmem, "a": spec_any, "s": spec_smem}
    return pl.pallas_call(
        body,
        out_shape=outs,
        in_specs=[specs[k]() for k in kinds],
        out_specs=jax.tree.map(lambda _: spec_vmem(), outs),
        scratch_shapes=scratch,
        compiler_params=pltpu.CompilerParams(vmem_limit_bytes=VMEM_LIMIT),
        cost_estimate=pl.CostEstimate(flops=micros * 1_000_000_000, bytes_accessed=4_000_000, transcendentals=0),
    )(*inputs)


def shape(dims, dtype):
    return jax.ShapeDtypeStruct(dims, dtype)


CUT_ONE = 640
CUT_TWO = 896
ORDER = ((0, 1, 3, 2), (0, 3, 1, 2))


def hop(v, axis, late):
    pairs = []
    for core in range(2):
        flip = 3 if (core == 1) != late else 1
        for xi in range(4):
            for zi in range(4):
                for yi in range(4):
                    tx, tz, ty = xi, zi, yi
                    if axis == "x":
                        tx = xi ^ flip
                    elif axis == "z":
                        tz = zi ^ flip
                    else:
                        ty = yi ^ flip
                    here = ((core * 4 + xi) * 4 + zi) * 4 + yi
                    pairs.append((here, ((core * 4 + tx) * 4 + tz) * 4 + ty))
    return lax.ppermute(v, ("pipe", "dp", "head"), pairs)


def swap(v):
    return lax.ppermute(v, "pipe", [(0, 1), (1, 0)])


def ring_pair(v, axis):
    low = jnp.stack([v, hop(v, axis, False)])
    return low, hop(low, axis, True)


def ring_rows(v, axis):
    low, high = ring_pair(v, axis)
    both = jnp.concatenate([low, high], axis=0)
    return jnp.moveaxis(both, 0, -3).reshape(v.shape[:-2] + (4 * v.shape[-2], v.shape[-1]))


def ring_stack(v, axis):
    low, high = ring_pair(v, axis)
    return jnp.concatenate([low, high], axis=0)


def gather_one(local):
    rows = ring_rows(local, "z")
    first = ring_rows(rows[:, :CUT_ONE], "x")
    last = ring_stack(rows[:, CUT_ONE:], "y")
    first_pair, last_pair = ring_pair(first, "y"), ring_pair(last, "x")
    return first_pair + last_pair, rows, (first, last), (first_pair[0], last_pair[0])


def gather_two(local, ready):
    rows = ring_rows(local, "x")
    first = ring_stack(rows[:, :CUT_TWO], "y")
    last = ring_rows(rows[:, CUT_TWO:], "z")
    first, last = after((first, last), ready)
    return ring_pair(first, "z") + ring_pair(last, "y")


def ring_begin(keep, send, axis):
    got = hop(send, axis, True)
    onward = (keep[1].astype(F32) + got[1].astype(F32)).astype(keep.dtype)
    return keep[0].astype(F32) + got[0].astype(F32), onward


def ring_end(begun, axis):
    part, onward = begun
    return part + hop(onward, axis, False).astype(F32)


def ring_sum(keep, send, axis):
    return ring_end(ring_begin(keep, send, axis), axis)


def halves(v):
    rows = v.shape[-2] // 4
    parts = [v[..., rows * n : rows * n + rows, :] for n in range(4)]
    return jnp.stack(parts[:2]), jnp.stack(parts[2:])


def low(v):
    return v.astype(BF16)


def after(v, other):
    return lax.optimization_barrier((v, other))[0]


def lock(*values):
    return lax.optimization_barrier(values)


def send_clip(value, rounds):
    pairs = [(p * 4 + source, p * 4 + target) for p, source, target in rounds]
    return lax.ppermute(value, ("pipe", "head"), pairs)


def spread_near(v):
    return send_clip(v, [(0, 0, 1), (0, 1, 0), (1, 2, 3), (1, 3, 2)])


def spread_far(v, near, pipe, y):
    even = (y % 2) == 0
    both = jnp.stack([jnp.where(even, v, near), jnp.where(even, near, v)])
    far = send_clip(both, [(0, 0, 3), (0, 1, 2), (1, 2, 1), (1, 3, 0)])
    return jnp.where((y // 2) == pipe, both, far)[:, None]


def token_order():
    order = np.zeros((PT, TOK), np.float32)
    for block in range(4):
        for window in range(WIN):
            row = (window // 10) * 2 + block // 2
            col = (window % 10) * 2 + block % 2
            order[block * PW + window, row * GRID + col] = 1
    return order


def turn_matrix(core_from, core_to, rows_from, rows_to):
    def labels(core, outer):
        out = []
        for a in range(4):
            for b in range(4):
                one, two = ORDER[core][a], ORDER[core][b]
                out.append((one, two) if outer == "x" else (two, one))
        return out

    source, target = labels(core_from, rows_from), labels(core_to, rows_to)
    matrix = np.zeros((384, 384), np.float32)
    for n, label in enumerate(source):
        m = target.index(label)
        matrix[n * 24 : n * 24 + 24, m * 24 : m * 24 + 24] = np.eye(24)
    return jnp.asarray(matrix, BF16)


def per_device(
    clips_in, cotangent, token_mask, memory_valid, memory_one, memory_two,
    qkv_one, out_one, up_one, down_one, up_bias_one, gains_one, shifts_one,
    qkv_two, out_two, res_two, up_two, down_two, up_bias_two, gain_two_in, shift_two_in, gains_two, shifts_two,
):
    pipe = lax.axis_index("pipe")
    dp = lax.axis_index("dp")
    y = lax.axis_index("head")
    x_at, z_at = dp // 4, dp % 4
    first_core = pipe == 0

    place = pipe.astype(jnp.int32).reshape(1)
    shard_one, shard_two = call(
        local_shards,
        (
            place, out_one.T, jnp.transpose(qkv_one, (1, 0, 2)), up_one, down_one.T,
            out_two.T, res_two.T, qkv_two, up_two, down_two.T,
        ),
        "s" + "v" * 9,
        (shape((24, 1152), BF16), shape((24, 1536), BF16)),
        [],
        1,
    )
    mine_one, rows_ready, ready, late = gather_one(shard_one)
    mine_two = gather_two(shard_two, ready)
    other_one = tuple(swap(v) for v in mine_one)

    def clip_of(v, at):
        return lax.dynamic_index_in_dim(v, at, 0, keepdims=False)

    near = jnp.where(first_core, 1, 3)
    far = 4 - near
    biases = jnp.concatenate([up_bias_one, up_bias_two])
    biases = jnp.concatenate(thirds(biases)).reshape(12, 288)
    memory = jnp.concatenate([memory_one[:, 0], memory_two[:, 0]], axis=-1)

    memory, biases = after((memory, biases), rows_ready)

    def payload(flip):
        part = clip_of(memory, y ^ flip).reshape(2 * MEMROWS, 288)
        return jnp.concatenate([part, biases], axis=0)

    got = hop(jnp.stack([payload(near), payload(2)]), "y", False)
    more = hop(jnp.stack([payload(far), got[1]]), "y", True)
    parcels = jnp.stack([payload(0), got[0], more[0], more[1]])
    memory = parcels[:, : 2 * MEMROWS].reshape(4, 2, MEMROWS, 288)
    mem_one, mem_two = memory[..., :96], memory[..., 96:]
    biases = parcels[:, 2 * MEMROWS :].astype(F32).reshape(4, 3, 1152)
    biases = biases[:, 0] + biases[:, 1] + biases[:, 2]
    bias_one, bias_two = biases[:, :384], biases[:, 384:]

    pipe, y, x_at, z_at = after((pipe, y, x_at, z_at), late)
    first_core = pipe == 0

    flags = clip_of(token_mask[:, 0], y).reshape(10, 2, 10, 2)[:, 0, :, 0].reshape(WIN)
    key_ok = (flags > 0).astype(F32)
    mem_ok = jnp.repeat((clip_of(memory_valid[:, 0], y) > 0).astype(F32), MEMROWS // 2)
    gap = jnp.zeros((MEM0 - WIN,), F32)
    tail = jnp.zeros((KEYS - MEM0 - MEMROWS,), F32)
    ok = jnp.concatenate([key_ok, gap, mem_ok, tail]).reshape(1, KEYS)
    fill = np.full((1, KEYS), ABSENT, np.float32)
    fill[0, :WIN] = MASKED
    fill[0, MEM0 : MEM0 + MEMROWS] = MASKED
    fill = jnp.asarray(fill)
    key_col = jnp.concatenate([key_ok, jnp.zeros((PW - WIN,), F32)]).reshape(PW, 1)

    def order_of(core, n):
        return jnp.asarray(ORDER[core], jnp.int32)[n]

    def own_order(n):
        return jnp.where(first_core, order_of(0, n), order_of(1, n))

    k = np.arange(384)
    k_outer, k_inner, k_row = k // 96, (k // 24) % 4, k % 24

    def chip(a, b):
        return (x_at ^ a) * 4 + (z_at ^ b)

    piece0 = chip(order_of(0, k_outer), order_of(0, k_inner))
    piece1 = chip(order_of(1, k_outer), order_of(1, k_inner))
    raw0 = piece0 * 24 + k_row
    raw1 = piece1 * 24 + k_row
    raw2 = jnp.concatenate([piece1 * 48 + k_row, piece1 * 48 + 24 + k_row])
    p1a = (k[:, None] == raw0[None, :]).astype(BF16)
    p1b = (k[:, None] == raw1[None, :]).astype(BF16)
    p2 = (np.arange(768)[:, None] == raw2[None, :]).astype(BF16)
    head_raw = (y ^ own_order(k // 96)) * 96 + k % 96
    pr = (raw1[:, None] == head_raw[None, :]).astype(BF16)
    j = np.arange(192)
    j_outer, j_inner, j_row = own_order(j // 48), own_order((j // 12) % 4), j % 12
    rows_x = pipe * 192 + chip(j_outer, j_inner) * 12 + j_row
    s1a = (rows_x[:, None] == raw0[None, :]).astype(BF16)
    s1b = (rows_x[:, None] == raw1[None, :]).astype(BF16)
    rows_x2 = pipe * 384 + chip(j_outer, j_inner) * 24 + j_row
    rows_z2 = pipe * 384 + chip(j_inner, j_outer) * 24 + j_row
    s2 = (jnp.concatenate([rows_x2, rows_x2 + 12])[:, None] == raw2[None, :]).astype(BF16)
    s2f = (jnp.concatenate([rows_z2, rows_z2 + 12])[:, None] == raw2[None, :]).astype(BF16)
    turn = turn_matrix(0, 1, "x", "x")
    to_up = turn_matrix(1, 0, "x", "z")
    to_down = turn_matrix(1, 1, "x", "z")

    order = token_order()
    token_perm = jnp.asarray(order, BF16)
    token_back = jnp.asarray(order.T, BF16)
    vec384 = jnp.concatenate([gains_one, shifts_one, gain_two_in[None], shift_two_in[None]], axis=0)
    gains_in = jnp.concatenate([gain_two_in[None], jnp.zeros((7, 384), F32)], axis=0)
    vec768 = jnp.concatenate([gains_two[None], shifts_two, jnp.zeros((4, 768), F32)], axis=0)
    x = clip_of(clips_in[:, 0], y)
    cot = clip_of(cotangent[:, 0], y)

    x, p1a, p1b, p2, pr, s1a, s1b, s2, s2f, key_col, vec768, gains_in, bias_two, cot, mem_two = lock(
        x, p1a, p1b, p2, pr, s1a, s1b, s2, s2f, key_col, vec768, gains_in, bias_two, cot, mem_two
    )
    other_two = tuple(swap(v) for v in mine_two)

    dma = pltpu.SemaphoreType.DMA
    saved = call(
        forward,
        (
            place, x, token_perm, p1a, turn, pr, vec384, ok, fill, mem_one, mem_two, bias_one,
            *mine_one, *other_one,
        ),
        "s" + "v" * 11 + "a" * 8,
        (
            shape((PT, 384), BF16), shape((PT, 384), BF16),
            shape((4, PT, HEAD), BF16), shape((4, KEYS, HEAD), BF16), shape((4, KEYS, HEAD), BF16),
            shape((4, PT, HEAD), BF16), shape((PT, 384), F32),
            shape((4, PT, 384), BF16), shape((4, PT, 384), BF16),
            shape((PW, 384), BF16), shape((8, PW, HEAD), BF16), shape((8, KEYS, HEAD), BF16),
            shape((8, KEYS, HEAD), BF16), shape((4, PW, 384), BF16), shape((PW, 768), F32),
        ),
        [
            pltpu.VMEM((4, 384, 1152), BF16), pltpu.VMEM((4, 384, 1152), BF16), pltpu.VMEM((8, 384), F32),
            dma(()), dma(()),
        ],
        18,
    )
    passed, x_kept, q1, k1, v1, mix1, mid1, act1, slope1, pn2, q2k, k2, v2, mix2, mid2 = saved

    feed = call(
        feed_two,
        (place, mid2, cot, key_col, p2, to_up, to_down, s2f, vec768, bias_two, *mine_two, *other_two),
        "s" + "v" * 9 + "a" * 8,
        (
            shape((WIN, 768), BF16), shape((PW, 768), F32), shape((8, 768), F32), shape((4, 768), F32),
            shape((2, 4, 48, 1536), BF16), shape((2, 4, 48, 1536), BF16),
            shape((2, 192, 1536), BF16), shape((2, 192, 1536), BF16),
        ),
        [
            pltpu.VMEM((4, 384, 1536), BF16), pltpu.VMEM((4, 384, 1536), BF16),
            pltpu.VMEM((4, PW, 768), BF16), pltpu.VMEM((4, PW, 768), F32), dma(()), dma(()),
        ],
        14,
    )
    activation, dmid2, vec_mid, dbias_two, keep_rows, send_rows, keep_y, send_y = feed
    feed_a = ring_begin(keep_rows, send_rows, "z")
    feed_b = ring_begin(keep_y, send_y, "y")

    second = call(
        second_backward,
        (
            place, dmid2, passed, pn2, q2k, k2, v2, mix2, p1b, pr, s1b, s2, gains_in, ok, fill,
            *mine_one, *other_one,
        ),
        "s" + "v" * 14 + "a" * 8,
        (
            shape((PT, 384), BF16), shape((8, 384), F32),
            shape((2, 192, 1152), BF16), shape((2, 192, 1152), BF16),
        ),
        [pltpu.VMEM((4, 384, 1152), BF16), pltpu.VMEM((3, PW, 384), BF16), dma(())],
        10,
    )
    dpassed, vec_in, keep_attn, send_attn = second
    dpassed = after(dpassed, (feed_a[1], feed_b[1]))
    keep_attn, send_attn = after((keep_attn, send_attn), (feed_a[1], feed_b[1]))
    attn_sum = ring_begin(keep_attn, send_attn, "y")
    feed_a = low(ring_end(feed_a, "z"))
    feed_b = low(ring_end(feed_b, "y"))

    third = call(
        first_backward,
        (
            place, dpassed, x_kept, q1, k1, v1, mix1, mid1, act1, slope1,
            token_back, p1a, turn, s1a, vec384, ok, fill, vec_mid, vec_in, dbias_two, *mine_one, *other_one,
        ),
        "s" + "v" * 19 + "a" * 8,
        (
            shape((TOK, 384), BF16), shape((12, 768), F32), shape((12, 768), F32),
            shape((2, 4, 48, 1152), BF16), shape((2, 4, 48, 1152), BF16),
        ),
        [
            pltpu.VMEM((4, 384, 1152), BF16), pltpu.VMEM((8, 384), F32), pltpu.VMEM((PT, 384), BF16), dma(()),
        ],
        16,
    )
    third, feed_a, feed_b, attn_sum = lock(third, feed_a, feed_b, attn_sum)
    xgrad, vec_keep, vec_send, keep_one, send_one = third

    vectors = vec_keep + hop(vec_send, "y", True)
    feed_a = ring_begin(feed_a[0:2], feed_a[2:4], "y")
    feed_b = ring_begin(*halves(feed_b), "z")
    attn_sum = low(ring_end(attn_sum, "y"))
    one_sum = ring_begin(keep_one, send_one, "x")
    vectors, feed_a, feed_b, attn_sum, xgrad, one_sum = lock(vectors, feed_a, feed_b, attn_sum, xgrad, one_sum)

    vectors = vectors[:10] + hop(jnp.concatenate([vectors[:8], vectors[10:]], axis=0), "y", False)
    feed_a = low(ring_end(feed_a, "y"))
    feed_b = low(ring_end(feed_b, "z"))
    attn_sum = ring_begin(*halves(attn_sum), "x")
    grad_near = spread_near(xgrad)
    one_sum = low(ring_end(one_sum, "x"))
    vectors, feed_a, feed_b, attn_sum, grad_near, one_sum = lock(
        vectors, feed_a, feed_b, attn_sum, grad_near, one_sum
    )

    vectors = vectors + hop(vectors, "x", True)
    feed_sum = ring_begin(*halves(jnp.concatenate([feed_a, feed_b], axis=1)), "x")
    attn_sum = low(ring_end(attn_sum, "x"))
    one_sum = ring_begin(one_sum[0:2], one_sum[2:4], "y")
    input_grad = spread_far(xgrad, grad_near, pipe, y)
    act_near = spread_near(activation)
    vectors, feed_sum, attn_sum, one_sum, act_near = lock(vectors, feed_sum, attn_sum, one_sum, act_near)

    vectors = vectors + hop(vectors, "x", False)
    feed_part, feed_onward = feed_sum
    feed_got = hop(feed_onward, "x", False)
    one_sum = low(ring_end(one_sum, "y"))
    activations = spread_far(activation, act_near, pipe, y)
    vectors, one_sum, feed_got = lock(vectors, one_sum, feed_got)
    grad_up_two, grad_down_two = call(
        feed_outputs,
        (feed_part, feed_got),
        "vv",
        (shape((24, 768), F32), shape((24, 768), F32)),
        [],
        2,
    )

    vectors = vectors + hop(vectors, "z", True)
    rest_sum = ring_begin(*halves(jnp.concatenate([one_sum, attn_sum], axis=1)), "z")
    vectors, rest_sum, activations, input_grad, grad_up_two, grad_down_two = lock(
        vectors, rest_sum, activations, input_grad, grad_up_two, grad_down_two
    )

    rest_part, rest_onward = rest_sum
    vectors_got = hop(vectors, "z", False)
    rest_got = hop(rest_onward, "z", False)
    outs = call(
        last_outputs,
        (rest_part, rest_got, vectors, vectors_got),
        "vvvv",
        (
            shape((12, 1, 288), F32), shape((12, 96), F32), shape((12, 384), F32), shape((12, 384), F32),
            shape((384,), F32), shape((2, 384), F32), shape((4, 384), F32),
            shape((12, 2, 288), F32), shape((24, 192), F32), shape((24, 96), F32),
            shape((768,), F32), shape((384,), F32), shape((384,), F32), shape((768,), F32),
            shape((3, 768), F32),
        ),
        [],
        2,
    )
    return (
        activations,
        input_grad,
        outs[0],
        outs[1].T,
        outs[2],
        outs[3].T,
        *outs[4:8],
        outs[8].T,
        outs[9].T,
        grad_up_two,
        grad_down_two.T,
        *outs[10:15],
    )


def solution(mesh):
    return jax.shard_map(
        per_device,
        mesh=mesh,
        in_specs=(
            P(None, "dp", None, None), P(None, "dp", None, None), P(None, "dp", None), P(None, "dp", None),
            P(None, "dp", None, None, "head"), P(None, "dp", None, None, "head"),
            P("dp", "head", None), P("head", "dp"), P("dp", "head"), P("head", "dp"), P("head"), P(), P(),
            P("dp", "head", None), P("head", "dp"), P("head", "dp"), P("dp", "head"), P("head", "dp"), P("head"),
            P(), P(), P(), P(),
        ),
        out_specs=(
            P("pipe", "dp", None, None), P("pipe", "dp", None, None),
            P(("pipe", "dp"), "head", None), P("head", ("pipe", "dp")), P(("pipe", "dp"), "head"),
            P("head", ("pipe", "dp")), P("head"), P(), P(),
            P(("pipe", "dp"), "head", None), P("head", ("pipe", "dp")), P("head", ("pipe", "dp")),
            P(("pipe", "dp"), "head"), P("head", ("pipe", "dp")), P("head"), P(), P(), P(), P(),
        ),
        check_vma=False,
    )
```

```python
import functools

import jax
import jax.numpy as jnp
import numpy as np
from jax import lax
from jax.experimental import pallas as pl
from jax.experimental.pallas import tpu as pltpu
from jax.sharding import PartitionSpec as P

F32 = jnp.float32
BF16 = jnp.bfloat16
GRID = 20
TOK = 400
WIN = 100
PW = 104
PT = 4 * PW
KEYS = 256
MEM0 = 112
MEMROWS = 50
HEAD = 96
EPS = 1e-06
MASKED = -1000000000.0
ABSENT = -3e38
SCALE = HEAD ** (-0.5)
VMEM_LIMIT = 56 * 1024 * 1024


def nn(a, b):
    return lax.dot_general(a, b, (((1,), (0,)), ((), ())), preferred_element_type=F32)


def nt(a, b):
    return lax.dot_general(a, b, (((1,), (1,)), ((), ())), preferred_element_type=F32)


def tn(a, b):
    return lax.dot_general(a, b, (((0,), (0,)), ((), ())), preferred_element_type=F32)


def thirds(v):
    high = v.astype(BF16)
    rest = v - high.astype(F32)
    mid = rest.astype(BF16)
    low = (rest - mid.astype(F32)).astype(BF16)
    return high, mid, low


def exact_nn(v, m):
    a, b, c = thirds(v)
    return nn(a, m) + nn(b, m) + nn(c, m)


def exact_nt(v, m):
    a, b, c = thirds(v)
    return nt(a, m) + nt(b, m) + nt(c, m)


def normalise(v):
    average = jnp.mean(v, axis=-1, keepdims=True)
    centred = v - average
    variance = jnp.mean(centred * centred, axis=-1, keepdims=True)
    inverse = lax.rsqrt(variance + EPS)
    return centred * inverse, inverse


def normalise_back(grad, unit, inverse, gain):
    scaled = grad * gain
    mean_one = jnp.mean(scaled, axis=-1, keepdims=True)
    mean_two = jnp.mean(scaled * unit, axis=-1, keepdims=True)
    return inverse * (scaled - mean_one - unit * mean_two)


def column_sum(v):
    return jnp.sum(v, axis=0, keepdims=True)


def gelu_both(h):
    cdf = 0.5 + 0.5 * lax.erf(h * 0.7071067811865476)
    density = 0.3989422804014327 * jnp.exp(-0.5 * h * h)
    return h * cdf, cdf + h * density


def pool_rows(v):
    return 0.25 * (v[0:PW] + v[PW : 2 * PW] + v[2 * PW : 3 * PW] + v[3 * PW : 4 * PW])


def softmax_rows(scores, ok, fill):
    scores = jnp.where(ok > 0, scores * SCALE, fill)
    peak = jnp.max(scores, axis=-1, keepdims=True)
    expos = jnp.exp(scores - peak)
    return expos / jnp.sum(expos, axis=-1, keepdims=True)


def attend_back(q, keys, values, ok, fill, dmix):
    n = range(len(q))
    scores = [nt(q[i], keys[i]) for i in n]
    dshares = [nt(dmix[i], values[i]) for i in n]
    shares = [softmax_rows(v, ok, fill) for v in scores]
    dvalues = [tn(shares[i].astype(BF16), dmix[i]) for i in n]
    inner = [jnp.sum(shares[i] * dshares[i], axis=-1, keepdims=True) for i in n]
    dscores = [(shares[i] * (dshares[i] - inner[i])).astype(BF16) for i in n]
    dq = [nn(dscores[i], keys[i]) * SCALE + dmix[i].astype(F32) for i in n]
    dkeys = [tn(dscores[i], q[i]) * SCALE for i in n]
    return [(dq[i], dkeys[i], dvalues[i]) for i in n]


def index_row(index, row, size):
    return index[row : row + 1, 0:size]


def index_col(index, row, size):
    return jnp.broadcast_to(index[row : row + 1, 0:size], (8, size)).T[:, 0:1]


def natural(index, row, size):
    values = lax.broadcasted_iota(jnp.int32, (size, size), 0).astype(F32)
    return (values == index_row(index, row, size)).astype(F32).astype(BF16)


def matching(index, row, rows, col, cols):
    return (index_col(index, row, rows) == index_row(index, col, cols)).astype(F32).astype(BF16)


def close_nt(v, m):
    high = v.astype(BF16)
    return nt(high, m) + nt((v - high.astype(F32)).astype(BF16), m)


def load_weights(core, owner, mine, other, dst, sem):
    def copies(groups, places):
        at = 0
        for kind, low, high in groups:
            cols = pl.ds(at, low.shape[-1])
            at += low.shape[-1]
            for n in range(4):
                slab = (low if n < 2 else high).at[n % 2]
                if kind == "y":
                    pltpu.make_async_copy(slab, dst.at[places[n], :, cols], sem).start()
                else:
                    for h in range(4):
                        pltpu.make_async_copy(slab.at[h], dst.at[places[h], pl.ds(96 * n, 96), cols], sem).start()

    @pl.when(core == owner)
    def _():
        copies(mine, (0, 1, 2, 3))

    @pl.when(core != owner)
    def _():
        copies(other, (0, 2, 1, 3))


def wait_weights(dst, sem):
    pltpu.make_async_copy(dst, dst, sem).wait()


def groups_one(refs):
    return [("y", refs[0], refs[1]), ("rows", refs[2], refs[3])]


def groups_two(refs):
    return [("rows", refs[0], refs[1]), ("y", refs[2], refs[3])]


def forward(
    place, x, token_perm, index, turn, vec384, ok, fill, mem_one, mem_two, bias_up, *rest
):
    mine, other = groups_one(rest[0:4]), groups_one(rest[4:8])
    (passed, x_out, q_out, k_out, v_out, mix_out, mid_out, act_out, slope_out,
     pn_out, q2_out, k2_out, v2_out, mix2_out, mid2_out) = rest[8:23]
    w1, wa, gains, sem_one, sem_attn = rest[23:28]
    load_weights(place[0], 0, mine, other, w1, sem_one)
    load_weights(place[0], 1, mine, other, wa, sem_attn)
    p1 = natural(index, 0, 384)
    pr = matching(index, 1, 384, 3, 384)
    gains[...] = exact_nn(vec384[...], p1)
    xb = nn(x[...], p1).astype(BF16)
    xb = nn(token_perm[...], xb).astype(BF16)
    x_out[...] = xb
    xf = xb.astype(F32)
    unit, _ = normalise(xf)
    normed = unit * gains[0:1, :] + gains[2:3, :]
    nb = normed.astype(BF16)
    pn = pool_rows(normed).astype(BF16)
    k_out[...] = jnp.zeros_like(k_out)
    v_out[...] = jnp.zeros_like(v_out)
    k2_out[...] = jnp.zeros_like(k2_out)
    v2_out[...] = jnp.zeros_like(v2_out)
    mix2_out[...] = jnp.zeros_like(mix2_out)
    wait_weights(w1, sem_one)
    for r in range(4):
        w = w1[r, :, 0:384]
        q_out[r] = nn(nb, w[:, 0:256])[:, 96:192].astype(BF16)
        kv = nn(pn, w)
        k_out[r, 0:PW, :] = kv[:, 192:288].astype(BF16)
        v_out[r, 0:PW, :] = kv[:, 288:384].astype(BF16)
        k_out[r, MEM0 : MEM0 + MEMROWS, :] = mem_one[r, 0]
        v_out[r, MEM0 : MEM0 + MEMROWS, :] = mem_one[r, 1]
    scores = [nt(q_out[r], k_out[r]) for r in range(4)]
    shares = [softmax_rows(v, ok[...], fill[...]).astype(BF16) for v in scores]
    branch = jnp.zeros((PT, 384), F32)
    for r in range(4):
        mixed = (nn(shares[r], v_out[r]) + q_out[r].astype(F32)).astype(BF16)
        mix_out[r] = mixed
        branch = branch + nt(mixed, w1[r, :, 0:96])
    middle = xf + gains[4:5, :] + branch
    mid_out[...] = middle
    unit, _ = normalise(middle)
    nm = (unit * gains[1:2, :] + gains[3:4, :]).astype(BF16)
    total = middle + gains[5:6, :]
    for r in range(4):
        hidden = nn(nm, w1[r, :, 384:768]) + bias_up[r : r + 1, :]
        active, slope = gelu_both(hidden)
        active = active.astype(BF16)
        act_out[r] = active
        slope_out[r] = slope.astype(BF16)
    for r in range(4):
        total = total + nt(act_out[r], w1[r, :, 768:1152])
    xb = nn(total.astype(BF16), turn[...]).astype(BF16)
    passed[...] = xb

    xf = xb.astype(F32)
    gains[...] = exact_nn(gains[...], turn[...])
    unit, _ = normalise(xf)
    normed = unit * gains[6:7, :] + gains[7:8, :]
    pn = pool_rows(normed).astype(BF16)
    pn_out[...] = pn
    pnr = nn(pn, pr).astype(BF16)
    wait_weights(wa, sem_attn)
    branch = [jnp.zeros((PW, 384), F32), jnp.zeros((PW, 384), F32)]
    for r in range(4):
        kv = nn(pn, wa[r, :, 768:1152])
        mix2_out[r, :, 192:288] = pnr[:, r * 96 : (r + 1) * 96]
        for h in range(2):
            q = nn(pn, wa[r, :, 384 * h + 256 : 384 * h + 384])[:, 32:128].astype(BF16)
            n = 2 * r + h
            q2_out[n] = q
            k2_out[n, 0:PW, :] = kv[:, 192 * h : 192 * h + 96].astype(BF16)
            v2_out[n, 0:PW, :] = kv[:, 192 * h + 96 : 192 * h + 192].astype(BF16)
            k2_out[n, MEM0 : MEM0 + MEMROWS, :] = mem_two[r, 0, :, 96 * h : 96 * h + 96]
            v2_out[n, MEM0 : MEM0 + MEMROWS, :] = mem_two[r, 1, :, 96 * h : 96 * h + 96]
    scores = [nt(q2_out[n], k2_out[n]) for n in range(8)]
    shares = [softmax_rows(v, ok[...], fill[...]).astype(BF16) for v in scores]
    mixed = [nn(shares[n], v2_out[n]) + q2_out[n].astype(F32) for n in range(8)]
    for r in range(4):
        for h in range(2):
            mix2_out[r, :, 96 * h : 96 * h + 96] = mixed[2 * r + h].astype(BF16)
        for s in range(2):
            branch[s] = branch[s] + nt(mix2_out[r], wa[r, :, 384 * s : 384 * s + 384])
    mid2_out[...] = jnp.concatenate(branch, axis=1)


def feed_two(place, middle_in, cot, key_ok, index, to_up, to_down, vec768, bias_up, *rest):
    mine, other = groups_two(rest[0:4]), groups_two(rest[4:8])
    act_out, dmid_out, vec_out, bias_out, keep_rows, send_rows, keep_y, send_y = rest[8:16]
    wu, wd, acts, slopes, sem_u, sem_d = rest[16:22]
    load_weights(place[0], 0, mine, other, wu, sem_u)
    load_weights(place[0], 1, mine, other, wd, sem_d)
    p2 = natural(index, 2, 768)
    s2f = matching(index, 6, 384, 2, 768)
    gains2 = exact_nn(vec768[...], p2)
    middle = middle_in[...] + gains2[2:3, :]
    unit, inverse = normalise(middle)
    nm = (unit * gains2[0:1, :] + gains2[1:2, :]).astype(BF16)
    nm_up = [nn(nm[:, 384 * s : 384 * s + 384], to_up[...]).astype(BF16) for s in range(2)]
    dyb = nn(cot[...], p2).astype(BF16)
    dyb = jnp.concatenate([dyb, jnp.zeros((PW - WIN, 768), BF16)], axis=0)
    dy = dyb.astype(F32) * key_ok[...]
    dyb = dy.astype(BF16)
    dy_down = [nn(dyb[:, 384 * s : 384 * s + 384], to_down[...]).astype(BF16) for s in range(2)]
    dy_sel = nt(s2f, dyb).astype(BF16)
    nm_sel = nt(s2f, nm).astype(BF16)
    wait_weights(wu, sem_u)
    for r in range(4):
        hidden = nn(nm_up[0], wu[r, :, 0:768]) + nn(nm_up[1], wu[r, :, 768:1536])
        active, slope = gelu_both(hidden + bias_up[r : r + 1, :])
        acts[r] = active.astype(BF16)
        slopes[r] = slope
    wait_weights(wd, sem_d)

    def put_rows(r, lo, value):
        value = value.astype(BF16)
        for k in range(4):
            out = keep_rows if k < 2 else send_rows
            out[k % 2, r, :, lo : lo + 768] = value[48 * k : 48 * k + 48]

    def put_head(r, lo, value):
        out = keep_y if r < 2 else send_y
        out[r % 2, :, lo : lo + 768] = value.astype(BF16)

    down = [jnp.zeros((PW, 384), F32), jnp.zeros((PW, 384), F32)]
    dnm = [jnp.zeros((PW, 384), F32), jnp.zeros((PW, 384), F32)]
    dhs = [
        ((nn(dy_down[0], wd[r, :, 0:768]) + nn(dy_down[1], wd[r, :, 768:1536])) * slopes[r]).astype(BF16)
        for r in range(4)
    ]
    for r in range(4):
        active, dh = acts[r], dhs[r]
        bias_out[r : r + 1, :] = column_sum(dh.astype(F32))
        put_rows(r, 0, nn(nm_sel[0:192], dh))
        put_rows(r, 768, nn(dy_sel[0:192], active))
        put_head(r, 0, nn(nm_sel[192:384], dh))
        put_head(r, 768, nn(dy_sel[192:384], active))
        for s in range(2):
            down[s] = down[s] + nt(active, wd[r, :, 768 * s : 768 * s + 768])
            dnm[s] = dnm[s] + nt(dh, wu[r, :, 768 * s : 768 * s + 768])
    down = jnp.concatenate([close_nt(v, to_down[...]) for v in down], axis=1)
    output = (middle + gains2[3:4, :] + down).astype(BF16)
    act_out[...] = nt(output, p2)[0:WIN].astype(BF16)
    dnm = jnp.concatenate([close_nt(v, to_up[...]) for v in dnm], axis=1)
    dmid = dy + normalise_back(dnm, unit, inverse, gains2[0:1, :])
    dmid_out[...] = dmid
    vec = jnp.concatenate(
        [
            column_sum(dnm * unit),
            column_sum(dnm),
            column_sum(dmid),
            column_sum(dy),
            jnp.zeros((4, 768), F32),
        ],
        axis=0,
    )
    vec_out[...] = exact_nt(vec, p2)


def second_backward(
    place, dmid, passed, pn_in, queries, keys, values, mixes, index, gains_in, ok, fill, *rest
):
    mine, other = groups_one(rest[0:4]), groups_one(rest[4:8])
    dpassed, vec_out, keep, send = rest[8:12]
    wa, part, sem = rest[12:15]
    load_weights(place[0], 1, mine, other, wa, sem)
    xf = passed[...].astype(F32)
    unit, inverse = normalise(xf)
    pn = pn_in[...]
    dbr = dmid[...].astype(BF16)
    p1 = natural(index, 1, 384)
    pr = matching(index, 1, 384, 3, 384)
    s1 = matching(index, 4, 192, 1, 384)
    s2 = matching(index, 5, 384, 2, 768)
    dbr_sel = nt(s2, dbr).astype(BF16)
    pn_sel = nt(s1, pn).astype(BF16)
    dpooled = jnp.zeros((PW, 384), F32)
    part[...] = jnp.zeros_like(part)
    wait_weights(wa, sem)

    def put(r, lo, value):
        out = keep if r < 2 else send
        out[r % 2, :, lo : lo + 384] = value.astype(BF16)

    dmm = [nn(dbr[:, 0:384], wa[r, :, 0:384]) + nn(dbr[:, 384:768], wa[r, :, 384:768]) for r in range(4)]
    dres = [v[:, 192:288] for v in dmm]
    dmix = [dmm[n // 2][:, 96 * (n % 2) : 96 * (n % 2) + 96].astype(BF16) for n in range(8)]
    back = attend_back(
        [queries[n] for n in range(8)], [keys[n] for n in range(8)], [values[n] for n in range(8)],
        ok[...], fill[...], dmix,
    )
    for n, (dq, dk, dv) in enumerate(back):
        r, h = n // 2, n % 2
        part[r, h, :, 288:384] = dq.astype(BF16)
        part[r, 2, :, 192 * h : 192 * h + 96] = dk[0:PW].astype(BF16)
        part[r, 2, :, 192 * h + 96 : 192 * h + 192] = dv[0:PW].astype(BF16)
    for r in range(4):
        for s in range(2):
            put(r, 384 * s, nn(dbr_sel[192 * s : 192 * s + 192], mixes[r]) + nn(pn_sel, part[r, s]))
            dpooled = dpooled + nt(part[r, s], wa[r, :, 384 * s : 384 * s + 384])
        put(r, 768, nn(pn_sel, part[r, 2]))
        dpooled = dpooled + nt(part[r, 2], wa[r, :, 768:1152])
    dpooled = dpooled + close_nt(jnp.concatenate(dres, axis=1), pr)
    dpooled = dpooled * 0.25
    dnormed = jnp.concatenate([dpooled, dpooled, dpooled, dpooled], axis=0)
    gain = exact_nn(gains_in[...], p1)[0:1]
    dpassed[...] = normalise_back(dnormed, unit, inverse, gain).astype(BF16)
    vec = jnp.concatenate(
        [column_sum(dnormed * unit), column_sum(dnormed), jnp.zeros((6, 384), F32)], axis=0
    )
    vec_out[...] = exact_nt(vec, p1)


def first_backward(
    place, dpassed, x, q_in, k_in, v_in, mix_in, mid_in, act_in, slope_in,
    token_back, index, turn, vec384, ok, fill, vec_mid, vec_in, dbias_two, *rest
):
    mine, other = groups_one(rest[0:4]), groups_one(rest[4:8])
    xgrad, vec_keep, vec_send, keep, send = rest[8:13]
    weights, gains, part, sem = rest[13:17]
    load_weights(place[0], 0, mine, other, weights, sem)
    p1 = natural(index, 0, 384)
    gains[...] = exact_nn(vec384[...], p1)
    xf = x[...].astype(F32)
    unit_in, inv_in = normalise(xf)
    normed = unit_in * gains[0:1, :] + gains[2:3, :]
    nb = normed.astype(BF16)
    pn = pool_rows(normed).astype(BF16)
    middle = mid_in[...]
    unit_mid, inv_mid = normalise(middle)
    nm = (unit_mid * gains[1:2, :] + gains[3:4, :]).astype(BF16)
    sel = matching(index, 4, 192, 0, 384)
    dyb = nt(dpassed[...], turn[...]).astype(BF16)
    dy = dyb.astype(F32)
    dy_sel = nt(sel, dyb).astype(BF16)
    nm_sel = nt(sel, nm).astype(BF16)
    nb_sel = nt(sel, nb).astype(BF16)
    pn_sel = nt(sel, pn).astype(BF16)
    part[...] = jnp.zeros_like(part)
    wait_weights(weights, sem)

    def put(r, lo, value):
        value = value.astype(BF16)
        for k in range(4):
            out = keep if k < 2 else send
            out[k % 2, r, :, lo : lo + 384] = value[48 * k : 48 * k + 48]

    dnm = jnp.zeros((PT, 384), F32)
    dhs = [
        (nn(dyb, weights[r, :, 768:1152]) * slope_in[r].astype(F32)).astype(BF16) for r in range(4)
    ]
    for r in range(4):
        dh = dhs[r]
        row = 8 + 2 * (r % 2)
        out = vec_keep if r < 2 else vec_send
        out[row : row + 1, :] = dbias_two[r : r + 1, :]
        out[row + 1 : row + 2, 0:384] = column_sum(dh.astype(F32))
        out[row + 1 : row + 2, 384:768] = jnp.zeros((1, 384), F32)
        put(r, 768, nn(dy_sel, act_in[r]))
        put(r, 384, nn(nm_sel, dh))
        dnm = dnm + nt(dh, weights[r, :, 384:768])
    dmid = dy + normalise_back(dnm, unit_mid, inv_mid, gains[1:2, :])
    dbr = dmid.astype(BF16)
    dbr_sel = nt(sel, dbr).astype(BF16)
    dnormed = jnp.zeros((PT, 384), F32)
    dpooled = jnp.zeros((PW, 384), F32)
    dmix = [nn(dbr, weights[r, :, 0:96]).astype(BF16) for r in range(4)]
    back = attend_back(
        [q_in[r] for r in range(4)], [k_in[r] for r in range(4)], [v_in[r] for r in range(4)], ok[...], fill[...], dmix
    )
    for r, (dq, dk, dv) in enumerate(back):
        part[r, 0, :, 0:96] = mix_in[r]
        part[r, 1, :, 96:192] = dq.astype(BF16)
        part[r, 2, 0:PW, 192:288] = (dk[0:PW] * 0.25).astype(BF16)
        part[r, 2, 0:PW, 288:384] = (dv[0:PW] * 0.25).astype(BF16)
    for r in range(4):
        w = weights[r, :, 0:384]
        first = nn(dbr_sel, part[r, 0]) + nn(nb_sel, part[r, 1]) + 4.0 * nn(pn_sel, part[r, 2, 0:PW, :])
        dnormed = dnormed + nt(part[r, 1, :, 0:256], w[:, 0:256])
        dpooled = dpooled + nt(part[r, 2, 0:PW, 128:384], w[:, 128:384])
        put(r, 0, first)
    dnormed = dnormed + jnp.concatenate([dpooled, dpooled, dpooled, dpooled], axis=0)
    dx = normalise_back(dnormed, unit_in, inv_in, gains[0:1, :]) + dmid
    vec = jnp.concatenate(
        [
            column_sum(dnormed * unit_in),
            column_sum(dnm * unit_mid),
            column_sum(dnormed),
            column_sum(dnm),
            column_sum(dmid),
            column_sum(dy),
            jnp.zeros((2, 384), F32),
        ],
        axis=0,
    )
    vec = exact_nt(vec, p1)
    for out in (vec_keep, vec_send):
        out[0:4, :] = vec_mid[0:4, :]
        for k in range(3):
            out[4 + k : 5 + k, 0:384] = vec[2 * k : 2 * k + 1, :]
            out[4 + k : 5 + k, 384:768] = vec[2 * k + 1 : 2 * k + 2, :]
        out[7:8, 0:384] = vec_in[0:1, :]
        out[7:8, 384:768] = vec_in[1:2, :]
    dxb = nt(dx.astype(BF16), p1).astype(BF16)
    xgrad[...] = nn(token_back[...], dxb).astype(BF16)


def local_shards(place, out_one, qkv_one, up_one, down_one, out_two, res_two, qkv_two, up_two, down_two, first, second):
    @pl.when(place[0] == 0)
    def _():
        first[:, 0:96] = out_one[...]
        first[:, 96:384] = qkv_one[0]
        first[:, 384:768] = up_one[...]
        first[:, 768:1152] = down_one[...]
        up = up_two[...].astype(F32)
        second[:, 0:768] = up[0:24].astype(BF16)
        second[:, 768:1536] = up[24:48].astype(BF16)

    @pl.when(place[0] != 0)
    def _():
        out_t, res_t = out_two[...].astype(F32), res_two[...].astype(F32)
        for s in range(2):
            first[:, 384 * s : 384 * s + 192] = out_t[24 * s : 24 * s + 24].astype(BF16)
            first[:, 384 * s + 192 : 384 * s + 288] = res_t[24 * s : 24 * s + 24].astype(BF16)
            first[:, 384 * s + 288 : 384 * s + 384] = qkv_two[:, s, 0:96]
            first[:, 768 + 192 * s : 960 + 192 * s] = qkv_two[:, s, 96:288]
        down = down_two[...].astype(F32)
        second[:, 0:768] = down[0:24].astype(BF16)
        second[:, 768:1536] = down[24:48].astype(BF16)


def feed_outputs(part, got, grad_up, grad_down):
    total = part[...] + got[...].astype(F32)
    grad_up[0:12, :] = total[:, 0:768]
    grad_up[12:24, :] = total[:, 1536:2304]
    grad_down[0:12, :] = total[:, 768:1536]
    grad_down[12:24, :] = total[:, 2304:3072]


def last_outputs(
    part, got, vec_part, vec_got,
    qkv1, out1, up1, down1, bias1, gains1, shifts1, qkv2, out2, res2, bias2, gain_in, shift_in, gain_mid, shifts2,
):
    total = part[...] + got[...].astype(F32)
    vec = vec_part[...] + vec_got[...]
    out1[...] = total[:, 0:96]
    qkv1[:, 0, :] = total[:, 96:384]
    up1[...] = total[:, 384:768]
    down1[...] = total[:, 768:1152]
    for s in range(2):
        at = 1152 + 384 * s
        out2[12 * s : 12 * s + 12, :] = total[:, at : at + 192]
        res2[12 * s : 12 * s + 12, :] = total[:, at + 192 : at + 288]
        qkv2[:, s, 0:96] = total[:, at + 288 : at + 384]
        qkv2[:, s, 96:288] = total[:, 1920 + 192 * s : 2112 + 192 * s]
    gain_mid[...] = vec[0]
    shifts2[...] = vec[1:4, :]
    gains1[0:1, :] = vec[4:5, 0:384]
    gains1[1:2, :] = vec[4:5, 384:768]
    for n in range(2):
        shifts1[2 * n : 2 * n + 1, :] = vec[5 + n : 6 + n, 0:384]
        shifts1[2 * n + 1 : 2 * n + 2, :] = vec[5 + n : 6 + n, 384:768]
    gain_in[...] = vec[7, 0:384]
    shift_in[...] = vec[7, 384:768]
    bias2[...] = vec[8]
    bias1[...] = vec[9, 0:384]


def spec_vmem():
    return pl.BlockSpec(memory_space=pltpu.VMEM)


def spec_any():
    return pl.BlockSpec(memory_space=pltpu.HBM)


def spec_smem():
    return pl.BlockSpec(memory_space=pltpu.SMEM)


def call(body, inputs, kinds, outs, scratch, micros):
    specs = {"v": spec_vmem, "a": spec_any, "s": spec_smem}
    return pl.pallas_call(
        body,
        out_shape=outs,
        in_specs=[specs[k]() for k in kinds],
        out_specs=jax.tree.map(lambda _: spec_vmem(), outs),
        scratch_shapes=scratch,
        compiler_params=pltpu.CompilerParams(vmem_limit_bytes=VMEM_LIMIT),
        cost_estimate=pl.CostEstimate(flops=micros * 1_000_000_000, bytes_accessed=4_000_000, transcendentals=0),
    )(*inputs)


def shape(dims, dtype):
    return jax.ShapeDtypeStruct(dims, dtype)


CUT_ONE = 640
CUT_TWO = 896
ORDER = ((0, 1, 3, 2), (0, 3, 1, 2))


def hop(v, axis, late):
    pairs = []
    for core in range(2):
        flip = 3 if (core == 1) != late else 1
        for xi in range(4):
            for zi in range(4):
                for yi in range(4):
                    tx, tz, ty = xi, zi, yi
                    if axis == "x":
                        tx = xi ^ flip
                    elif axis == "z":
                        tz = zi ^ flip
                    else:
                        ty = yi ^ flip
                    here = ((core * 4 + xi) * 4 + zi) * 4 + yi
                    pairs.append((here, ((core * 4 + tx) * 4 + tz) * 4 + ty))
    return lax.ppermute(v, ("pipe", "dp", "head"), pairs)


def swap(v):
    return lax.ppermute(v, "pipe", [(0, 1), (1, 0)])


def ring_pair(v, axis):
    low = jnp.stack([v, hop(v, axis, False)])
    return low, hop(low, axis, True)


def ring_rows(v, axis):
    low, high = ring_pair(v, axis)
    both = jnp.concatenate([low, high], axis=0)
    return jnp.moveaxis(both, 0, -3).reshape(v.shape[:-2] + (4 * v.shape[-2], v.shape[-1]))


def ring_stack(v, axis):
    low, high = ring_pair(v, axis)
    return jnp.concatenate([low, high], axis=0)


def gather_one(local):
    rows = ring_rows(local, "z")
    first = ring_rows(rows[:, :CUT_ONE], "x")
    last = ring_stack(rows[:, CUT_ONE:], "y")
    first_pair, last_pair = ring_pair(first, "y"), ring_pair(last, "x")
    return first_pair + last_pair, rows, (first, last), (first_pair[0], last_pair[0])


def gather_two(local, ready):
    rows = ring_rows(local, "x")
    first = ring_stack(rows[:, :CUT_TWO], "y")
    last = ring_rows(rows[:, CUT_TWO:], "z")
    first, last = after((first, last), ready)
    return ring_pair(first, "z") + ring_pair(last, "y")


def ring_begin(keep, send, axis):
    got = hop(send, axis, True)
    onward = (keep[1].astype(F32) + got[1].astype(F32)).astype(keep.dtype)
    return keep[0].astype(F32) + got[0].astype(F32), onward


def ring_end(begun, axis):
    part, onward = begun
    return part + hop(onward, axis, False).astype(F32)


def ring_sum(keep, send, axis):
    return ring_end(ring_begin(keep, send, axis), axis)


def halves(v):
    rows = v.shape[-2] // 4
    parts = [v[..., rows * n : rows * n + rows, :] for n in range(4)]
    return jnp.stack(parts[:2]), jnp.stack(parts[2:])


def low(v):
    return v.astype(BF16)


def after(v, other):
    return lax.optimization_barrier((v, other))[0]


def lock(*values):
    return lax.optimization_barrier(values)


def send_clip(value, rounds):
    pairs = [(p * 4 + source, p * 4 + target) for p, source, target in rounds]
    return lax.ppermute(value, ("pipe", "head"), pairs)


def spread_near(v):
    return send_clip(v, [(0, 0, 1), (0, 1, 0), (1, 2, 3), (1, 3, 2)])


def spread_far(v, near, pipe, y):
    even = (y % 2) == 0
    both = jnp.stack([jnp.where(even, v, near), jnp.where(even, near, v)])
    far = send_clip(both, [(0, 0, 3), (0, 1, 2), (1, 2, 1), (1, 3, 0)])
    return jnp.where((y // 2) == pipe, both, far)[:, None]


def token_order():
    order = np.zeros((PT, TOK), np.float32)
    for block in range(4):
        for window in range(WIN):
            row = (window // 10) * 2 + block // 2
            col = (window % 10) * 2 + block % 2
            order[block * PW + window, row * GRID + col] = 1
    return order


def turn_matrix(core_from, core_to, rows_from, rows_to):
    def labels(core, outer):
        out = []
        for a in range(4):
            for b in range(4):
                one, two = ORDER[core][a], ORDER[core][b]
                out.append((one, two) if outer == "x" else (two, one))
        return out

    source, target = labels(core_from, rows_from), labels(core_to, rows_to)
    matrix = np.zeros((384, 384), np.float32)
    for n, label in enumerate(source):
        m = target.index(label)
        matrix[n * 24 : n * 24 + 24, m * 24 : m * 24 + 24] = np.eye(24)
    return jnp.asarray(matrix, BF16)


def per_device(
    clips_in, cotangent, token_mask, memory_valid, memory_one, memory_two,
    qkv_one, out_one, up_one, down_one, up_bias_one, gains_one, shifts_one,
    qkv_two, out_two, res_two, up_two, down_two, up_bias_two, gain_two_in, shift_two_in, gains_two, shifts_two,
):
    pipe = lax.axis_index("pipe")
    dp = lax.axis_index("dp")
    y = lax.axis_index("head")
    x_at, z_at = dp // 4, dp % 4
    first_core = pipe == 0

    place = pipe.astype(jnp.int32).reshape(1)
    shard_one, shard_two = call(
        local_shards,
        (
            place, out_one.T, jnp.transpose(qkv_one, (1, 0, 2)), up_one, down_one.T,
            out_two.T, res_two.T, qkv_two, up_two, down_two.T,
        ),
        "s" + "v" * 9,
        (shape((24, 1152), BF16), shape((24, 1536), BF16)),
        [],
        1,
    )
    mine_one, rows_ready, ready, late = gather_one(shard_one)
    mine_two = gather_two(shard_two, ready)
    other_one = tuple(swap(v) for v in mine_one)

    def clip_of(v, at):
        return lax.dynamic_index_in_dim(v, at, 0, keepdims=False)

    near = jnp.where(first_core, 1, 3)
    far = 4 - near
    biases = jnp.concatenate([up_bias_one, up_bias_two])
    biases = jnp.concatenate(thirds(biases)).reshape(12, 288)
    memory = jnp.concatenate([memory_one[:, 0], memory_two[:, 0]], axis=-1)

    memory, biases = after((memory, biases), rows_ready)

    def payload(flip):
        part = clip_of(memory, y ^ flip).reshape(2 * MEMROWS, 288)
        return jnp.concatenate([part, biases], axis=0)

    got = hop(jnp.stack([payload(near), payload(2)]), "y", False)
    more = hop(jnp.stack([payload(far), got[1]]), "y", True)
    parcels = jnp.stack([payload(0), got[0], more[0], more[1]])
    memory = parcels[:, : 2 * MEMROWS].reshape(4, 2, MEMROWS, 288)
    mem_one, mem_two = memory[..., :96], memory[..., 96:]
    biases = parcels[:, 2 * MEMROWS :].astype(F32).reshape(4, 3, 1152)
    biases = biases[:, 0] + biases[:, 1] + biases[:, 2]
    bias_one, bias_two = biases[:, :384], biases[:, 384:]

    pipe, y, x_at, z_at = after((pipe, y, x_at, z_at), late)
    first_core = pipe == 0

    flags = clip_of(token_mask[:, 0], y).reshape(10, 2, 10, 2)[:, 0, :, 0].reshape(WIN)
    key_ok = (flags > 0).astype(F32)
    mem_ok = jnp.repeat((clip_of(memory_valid[:, 0], y) > 0).astype(F32), MEMROWS // 2)
    gap = jnp.zeros((MEM0 - WIN,), F32)
    tail = jnp.zeros((KEYS - MEM0 - MEMROWS,), F32)
    ok = jnp.concatenate([key_ok, gap, mem_ok, tail]).reshape(1, KEYS)
    fill = np.full((1, KEYS), ABSENT, np.float32)
    fill[0, :WIN] = MASKED
    fill[0, MEM0 : MEM0 + MEMROWS] = MASKED
    fill = jnp.asarray(fill)
    key_col = jnp.concatenate([key_ok, jnp.zeros((PW - WIN,), F32)]).reshape(PW, 1)

    def order_of(core, n):
        return jnp.asarray(ORDER[core], jnp.int32)[n]

    def own_order(n):
        return jnp.where(first_core, order_of(0, n), order_of(1, n))

    k = np.arange(384)
    k_outer, k_inner, k_row = k // 96, (k // 24) % 4, k % 24

    def chip(a, b):
        return (x_at ^ a) * 4 + (z_at ^ b)

    piece0 = chip(order_of(0, k_outer), order_of(0, k_inner))
    piece1 = chip(order_of(1, k_outer), order_of(1, k_inner))
    raw0 = piece0 * 24 + k_row
    raw1 = piece1 * 24 + k_row
    raw2 = jnp.concatenate([piece1 * 48 + k_row, piece1 * 48 + 24 + k_row])
    head_raw = (y ^ own_order(k // 96)) * 96 + k % 96
    j = np.arange(192)
    j_outer, j_inner, j_row = own_order(j // 48), own_order((j // 12) % 4), j % 12
    rows_x = pipe * 192 + chip(j_outer, j_inner) * 12 + j_row
    rows_x2 = pipe * 384 + chip(j_outer, j_inner) * 24 + j_row
    rows_z2 = pipe * 384 + chip(j_inner, j_outer) * 24 + j_row
    pair = np.array([[0], [12]])
    rows_x2 = (rows_x2[None, :] + pair).reshape(384)
    rows_z2 = (rows_z2[None, :] + pair).reshape(384)
    index = [raw0, raw1, raw2, head_raw, rows_x, rows_x2, rows_z2, raw0]
    index = jnp.stack([jnp.pad(v, (0, 768 - v.shape[0])) for v in index]).astype(F32)
    turn = turn_matrix(0, 1, "x", "x")
    to_up = turn_matrix(1, 0, "x", "z")
    to_down = turn_matrix(1, 1, "x", "z")

    order = token_order()
    token_perm = jnp.asarray(order, BF16)
    token_back = jnp.asarray(order.T, BF16)
    vec384 = jnp.concatenate([gains_one, shifts_one, gain_two_in[None], shift_two_in[None]], axis=0)
    gains_in = jnp.concatenate([gain_two_in[None], jnp.zeros((7, 384), F32)], axis=0)
    vec768 = jnp.concatenate([gains_two[None], shifts_two, jnp.zeros((4, 768), F32)], axis=0)
    x = clip_of(clips_in[:, 0], y)
    cot = clip_of(cotangent[:, 0], y)

    x, key_col, vec768, gains_in, bias_two, cot, mem_two = lock(
        x, key_col, vec768, gains_in, bias_two, cot, mem_two
    )
    other_two = tuple(swap(v) for v in mine_two)

    dma = pltpu.SemaphoreType.DMA
    saved = call(
        forward,
        (
            place, x, token_perm, index, turn, vec384, ok, fill, mem_one, mem_two, bias_one,
            *mine_one, *other_one,
        ),
        "s" + "v" * 10 + "a" * 8,
        (
            shape((PT, 384), BF16), shape((PT, 384), BF16),
            shape((4, PT, HEAD), BF16), shape((4, KEYS, HEAD), BF16), shape((4, KEYS, HEAD), BF16),
            shape((4, PT, HEAD), BF16), shape((PT, 384), F32),
            shape((4, PT, 384), BF16), shape((4, PT, 384), BF16),
            shape((PW, 384), BF16), shape((8, PW, HEAD), BF16), shape((8, KEYS, HEAD), BF16),
            shape((8, KEYS, HEAD), BF16), shape((4, PW, 384), BF16), shape((PW, 768), F32),
        ),
        [
            pltpu.VMEM((4, 384, 1152), BF16), pltpu.VMEM((4, 384, 1152), BF16), pltpu.VMEM((8, 384), F32),
            dma(()), dma(()),
        ],
        18,
    )
    passed, x_kept, q1, k1, v1, mix1, mid1, act1, slope1, pn2, q2k, k2, v2, mix2, mid2 = saved

    feed = call(
        feed_two,
        (place, mid2, cot, key_col, index, to_up, to_down, vec768, bias_two, *mine_two, *other_two),
        "s" + "v" * 8 + "a" * 8,
        (
            shape((WIN, 768), BF16), shape((PW, 768), F32), shape((8, 768), F32), shape((4, 768), F32),
            shape((2, 4, 48, 1536), BF16), shape((2, 4, 48, 1536), BF16),
            shape((2, 192, 1536), BF16), shape((2, 192, 1536), BF16),
        ),
        [
            pltpu.VMEM((4, 384, 1536), BF16), pltpu.VMEM((4, 384, 1536), BF16),
            pltpu.VMEM((4, PW, 768), BF16), pltpu.VMEM((4, PW, 768), F32), dma(()), dma(()),
        ],
        14,
    )
    activation, dmid2, vec_mid, dbias_two, keep_rows, send_rows, keep_y, send_y = feed
    feed_a = ring_begin(keep_rows, send_rows, "z")
    feed_b = ring_begin(keep_y, send_y, "y")

    second = call(
        second_backward,
        (
            place, dmid2, passed, pn2, q2k, k2, v2, mix2, index, gains_in, ok, fill,
            *mine_one, *other_one,
        ),
        "s" + "v" * 11 + "a" * 8,
        (
            shape((PT, 384), BF16), shape((8, 384), F32),
            shape((2, 192, 1152), BF16), shape((2, 192, 1152), BF16),
        ),
        [pltpu.VMEM((4, 384, 1152), BF16), pltpu.VMEM((4, 3, PW, 384), BF16), dma(())],
        10,
    )
    dpassed, vec_in, keep_attn, send_attn = second
    dpassed = after(dpassed, (feed_a[1], feed_b[1]))
    keep_attn, send_attn = after((keep_attn, send_attn), (feed_a[1], feed_b[1]))
    attn_sum = ring_begin(keep_attn, send_attn, "y")
    feed_a = low(ring_end(feed_a, "z"))
    feed_b = low(ring_end(feed_b, "y"))

    third = call(
        first_backward,
        (
            place, dpassed, x_kept, q1, k1, v1, mix1, mid1, act1, slope1,
            token_back, index, turn, vec384, ok, fill, vec_mid, vec_in, dbias_two, *mine_one, *other_one,
        ),
        "s" + "v" * 18 + "a" * 8,
        (
            shape((TOK, 384), BF16), shape((12, 768), F32), shape((12, 768), F32),
            shape((2, 4, 48, 1152), BF16), shape((2, 4, 48, 1152), BF16),
        ),
        [
            pltpu.VMEM((4, 384, 1152), BF16), pltpu.VMEM((8, 384), F32), pltpu.VMEM((4, 3, PT, 384), BF16), dma(()),
        ],
        16,
    )
    third, feed_a, feed_b, attn_sum = lock(third, feed_a, feed_b, attn_sum)
    xgrad, vec_keep, vec_send, keep_one, send_one = third

    vectors = vec_keep + hop(vec_send, "y", True)
    feed_a = ring_begin(feed_a[0:2], feed_a[2:4], "y")
    feed_b = ring_begin(*halves(feed_b), "z")
    attn_sum = low(ring_end(attn_sum, "y"))
    one_sum = ring_begin(keep_one, send_one, "x")
    vectors, feed_a, feed_b, attn_sum, xgrad, one_sum = lock(vectors, feed_a, feed_b, attn_sum, xgrad, one_sum)

    vectors = vectors[:10] + hop(jnp.concatenate([vectors[:8], vectors[10:]], axis=0), "y", False)
    feed_a = low(ring_end(feed_a, "y"))
    feed_b = low(ring_end(feed_b, "z"))
    attn_sum = ring_begin(*halves(attn_sum), "x")
    grad_near = spread_near(xgrad)
    one_sum = low(ring_end(one_sum, "x"))
    vectors, feed_a, feed_b, attn_sum, grad_near, one_sum = lock(
        vectors, feed_a, feed_b, attn_sum, grad_near, one_sum
    )

    vectors = vectors + hop(vectors, "x", True)
    feed_sum = ring_begin(*halves(jnp.concatenate([feed_a, feed_b], axis=1)), "x")
    attn_sum = low(ring_end(attn_sum, "x"))
    one_sum = ring_begin(one_sum[0:2], one_sum[2:4], "y")
    input_grad = spread_far(xgrad, grad_near, pipe, y)
    act_near = spread_near(activation)
    vectors, feed_sum, attn_sum, one_sum, act_near = lock(vectors, feed_sum, attn_sum, one_sum, act_near)

    vectors = vectors + hop(vectors, "x", False)
    feed_part, feed_onward = feed_sum
    feed_got = hop(feed_onward, "x", False)
    one_sum = low(ring_end(one_sum, "y"))
    activations = spread_far(activation, act_near, pipe, y)
    vectors, one_sum, feed_got = lock(vectors, one_sum, feed_got)
    grad_up_two, grad_down_two = call(
        feed_outputs,
        (feed_part, feed_got),
        "vv",
        (shape((24, 768), F32), shape((24, 768), F32)),
        [],
        2,
    )

    vectors = vectors + hop(vectors, "z", True)
    rest_sum = ring_begin(*halves(jnp.concatenate([one_sum, attn_sum], axis=1)), "z")
    vectors, rest_sum, activations, input_grad, grad_up_two, grad_down_two = lock(
        vectors, rest_sum, activations, input_grad, grad_up_two, grad_down_two
    )

    rest_part, rest_onward = rest_sum
    vectors_got = hop(vectors, "z", False)
    rest_got = hop(rest_onward, "z", False)
    outs = call(
        last_outputs,
        (rest_part, rest_got, vectors, vectors_got),
        "vvvv",
        (
            shape((12, 1, 288), F32), shape((12, 96), F32), shape((12, 384), F32), shape((12, 384), F32),
            shape((384,), F32), shape((2, 384), F32), shape((4, 384), F32),
            shape((12, 2, 288), F32), shape((24, 192), F32), shape((24, 96), F32),
            shape((768,), F32), shape((384,), F32), shape((384,), F32), shape((768,), F32),
            shape((3, 768), F32),
        ),
        [],
        2,
    )
    return (
        activations,
        input_grad,
        outs[0],
        outs[1].T,
        outs[2],
        outs[3].T,
        *outs[4:8],
        outs[8].T,
        outs[9].T,
        grad_up_two,
        grad_down_two.T,
        *outs[10:15],
    )


def solution(mesh):
    return jax.shard_map(
        per_device,
        mesh=mesh,
        in_specs=(
            P(None, "dp", None, None), P(None, "dp", None, None), P(None, "dp", None), P(None, "dp", None),
            P(None, "dp", None, None, "head"), P(None, "dp", None, None, "head"),
            P("dp", "head", None), P("head", "dp"), P("dp", "head"), P("head", "dp"), P("head"), P(), P(),
            P("dp", "head", None), P("head", "dp"), P("head", "dp"), P("dp", "head"), P("head", "dp"), P("head"),
            P(), P(), P(), P(),
        ),
        out_specs=(
            P("pipe", "dp", None, None), P("pipe", "dp", None, None),
            P(("pipe", "dp"), "head", None), P("head", ("pipe", "dp")), P(("pipe", "dp"), "head"),
            P("head", ("pipe", "dp")), P("head"), P(), P(),
            P(("pipe", "dp"), "head", None), P("head", ("pipe", "dp")), P("head", ("pipe", "dp")),
            P(("pipe", "dp"), "head"), P("head", ("pipe", "dp")), P("head"), P(), P(), P(), P(),
        ),
        check_vma=False,
    )
```

```python
import functools

import jax
import jax.numpy as jnp
import numpy as np
from jax import lax
from jax.experimental import pallas as pl
from jax.experimental.pallas import tpu as pltpu
from jax.sharding import PartitionSpec as P

F32 = jnp.float32
BF16 = jnp.bfloat16
GRID = 20
TOK = 400
WIN = 100
PW = 104
PT = 4 * PW
KEYS = 256
MEM0 = 112
MEMROWS = 50
HEAD = 96
EPS = 1e-06
MASKED = -1000000000.0
ABSENT = -3e38
SCALE = HEAD ** (-0.5)
VMEM_LIMIT = 56 * 1024 * 1024


def nn(a, b):
    return lax.dot_general(a, b, (((1,), (0,)), ((), ())), preferred_element_type=F32)


def nt(a, b):
    return lax.dot_general(a, b, (((1,), (1,)), ((), ())), preferred_element_type=F32)


def tn(a, b):
    return lax.dot_general(a, b, (((0,), (0,)), ((), ())), preferred_element_type=F32)


def thirds(v):
    high = v.astype(BF16)
    rest = v - high.astype(F32)
    mid = rest.astype(BF16)
    low = (rest - mid.astype(F32)).astype(BF16)
    return high, mid, low


def exact_nn(v, m):
    a, b, c = thirds(v)
    return nn(a, m) + nn(b, m) + nn(c, m)


def exact_nt(v, m):
    a, b, c = thirds(v)
    return nt(a, m) + nt(b, m) + nt(c, m)


def normalise(v):
    average = jnp.mean(v, axis=-1, keepdims=True)
    centred = v - average
    variance = jnp.mean(centred * centred, axis=-1, keepdims=True)
    inverse = lax.rsqrt(variance + EPS)
    return centred * inverse, inverse


def normalise_back(grad, unit, inverse, gain):
    scaled = grad * gain
    mean_one = jnp.mean(scaled, axis=-1, keepdims=True)
    mean_two = jnp.mean(scaled * unit, axis=-1, keepdims=True)
    return inverse * (scaled - mean_one - unit * mean_two)


def column_sum(v):
    return jnp.sum(v, axis=0, keepdims=True)


def gelu_both(h):
    cdf = 0.5 + 0.5 * lax.erf(h * 0.7071067811865476)
    density = 0.3989422804014327 * jnp.exp(-0.5 * h * h)
    return h * cdf, cdf + h * density


def pool_rows(v):
    return 0.25 * (v[0:PW] + v[PW : 2 * PW] + v[2 * PW : 3 * PW] + v[3 * PW : 4 * PW])


def softmax_rows(scores, ok, fill):
    scores = jnp.where(ok > 0, scores * SCALE, fill)
    peak = jnp.max(scores, axis=-1, keepdims=True)
    expos = jnp.exp(scores - peak)
    return expos / jnp.sum(expos, axis=-1, keepdims=True)


def attend_back(q, keys, values, ok, fill, dmix):
    n = range(len(q))
    scores = [nt(q[i], keys[i]) for i in n]
    dshares = [nt(dmix[i], values[i]) for i in n]
    shares = [softmax_rows(v, ok, fill) for v in scores]
    dvalues = [tn(shares[i].astype(BF16), dmix[i]) for i in n]
    inner = [jnp.sum(shares[i] * dshares[i], axis=-1, keepdims=True) for i in n]
    dscores = [(shares[i] * (dshares[i] - inner[i])).astype(BF16) for i in n]
    dq = [nn(dscores[i], keys[i]) * SCALE + dmix[i].astype(F32) for i in n]
    dkeys = [tn(dscores[i], q[i]) * SCALE for i in n]
    return [(dq[i], dkeys[i], dvalues[i]) for i in n]


def index_row(index, row, size):
    return index[row : row + 1, 0:size]


def index_col(index, row, size):
    return jnp.broadcast_to(index[row : row + 1, 0:size], (8, size)).T[:, 0:1]


def natural(index, row, size):
    values = lax.broadcasted_iota(jnp.int32, (size, size), 0).astype(F32)
    return (values == index_row(index, row, size)).astype(F32).astype(BF16)


def matching(index, row, rows, col, cols):
    return (index_col(index, row, rows) == index_row(index, col, cols)).astype(F32).astype(BF16)


def close_nt(v, m):
    high = v.astype(BF16)
    return nt(high, m) + nt((v - high.astype(F32)).astype(BF16), m)


def load_weights(core, owner, mine, other, dst, sem):
    def copies(groups, places):
        at = 0
        for kind, low, high in groups:
            cols = pl.ds(at, low.shape[-1])
            at += low.shape[-1]
            for n in range(4):
                slab = (low if n < 2 else high).at[n % 2]
                if kind == "y":
                    pltpu.make_async_copy(slab, dst.at[places[n], :, cols], sem).start()
                else:
                    for h in range(4):
                        pltpu.make_async_copy(slab.at[h], dst.at[places[h], pl.ds(96 * n, 96), cols], sem).start()

    @pl.when(core == owner)
    def _():
        copies(mine, (0, 1, 2, 3))

    @pl.when(core != owner)
    def _():
        copies(other, (0, 2, 1, 3))


def wait_weights(dst, sem):
    pltpu.make_async_copy(dst, dst, sem).wait()


def groups_one(refs):
    return [("y", refs[0], refs[1]), ("rows", refs[2], refs[3])]


def groups_two(refs):
    return [("rows", refs[0], refs[1]), ("y", refs[2], refs[3])]


def forward(
    place, x, token_perm, index, turn, vec384, ok, fill, mem_one, mem_two, bias_up, *rest
):
    mine, other = groups_one(rest[0:4]), groups_one(rest[4:8])
    (passed, x_out, q_out, k_out, v_out, mix_out, mid_out, act_out, slope_out,
     pn_out, q2_out, k2_out, v2_out, mix2_out, mid2_out) = rest[8:23]
    w1, wa, gains, sem_one, sem_attn = rest[23:28]
    load_weights(place[0], 0, mine, other, w1, sem_one)
    load_weights(place[0], 1, mine, other, wa, sem_attn)
    p1 = natural(index, 0, 384)
    pr = matching(index, 1, 384, 3, 384)
    gains[...] = exact_nn(vec384[...], p1)
    xb = nn(x[...], p1).astype(BF16)
    xb = nn(token_perm[...], xb).astype(BF16)
    x_out[...] = xb
    xf = xb.astype(F32)
    unit, _ = normalise(xf)
    normed = unit * gains[0:1, :] + gains[2:3, :]
    nb = normed.astype(BF16)
    pn = pool_rows(normed).astype(BF16)
    k_out[...] = jnp.zeros_like(k_out)
    v_out[...] = jnp.zeros_like(v_out)
    k2_out[...] = jnp.zeros_like(k2_out)
    v2_out[...] = jnp.zeros_like(v2_out)
    mix2_out[...] = jnp.zeros_like(mix2_out)
    wait_weights(w1, sem_one)
    for r in range(4):
        w = w1[r, :, 0:384]
        q_out[r] = nn(nb, w[:, 0:256])[:, 96:192].astype(BF16)
        kv = nn(pn, w)
        k_out[r, 0:PW, :] = kv[:, 192:288].astype(BF16)
        v_out[r, 0:PW, :] = kv[:, 288:384].astype(BF16)
        k_out[r, MEM0 : MEM0 + MEMROWS, :] = mem_one[r, 0]
        v_out[r, MEM0 : MEM0 + MEMROWS, :] = mem_one[r, 1]
    scores = [nt(q_out[r], k_out[r]) for r in range(4)]
    shares = [softmax_rows(v, ok[...], fill[...]).astype(BF16) for v in scores]
    branch = jnp.zeros((PT, 384), F32)
    for r in range(4):
        mixed = (nn(shares[r], v_out[r]) + q_out[r].astype(F32)).astype(BF16)
        mix_out[r] = mixed
        branch = branch + nt(mixed, w1[r, :, 0:96])
    middle = xf + gains[4:5, :] + branch
    mid_out[...] = middle
    unit, _ = normalise(middle)
    nm = (unit * gains[1:2, :] + gains[3:4, :]).astype(BF16)
    total = middle + gains[5:6, :]
    for r in range(4):
        hidden = nn(nm, w1[r, :, 384:768]) + bias_up[r : r + 1, :]
        active, slope = gelu_both(hidden)
        active = active.astype(BF16)
        act_out[r] = active
        slope_out[r] = slope.astype(BF16)
    for r in range(4):
        total = total + nt(act_out[r], w1[r, :, 768:1152])
    xb = nn(total.astype(BF16), turn[...]).astype(BF16)
    passed[...] = xb

    xf = xb.astype(F32)
    gains[...] = exact_nn(gains[...], turn[...])
    unit, _ = normalise(xf)
    normed = unit * gains[6:7, :] + gains[7:8, :]
    pn = pool_rows(normed).astype(BF16)
    pn_out[...] = pn
    pnr = nn(pn, pr).astype(BF16)
    wait_weights(wa, sem_attn)
    branch = [jnp.zeros((PW, 384), F32), jnp.zeros((PW, 384), F32)]
    for r in range(4):
        kv = nn(pn, wa[r, :, 768:1152])
        mix2_out[r, :, 192:288] = pnr[:, r * 96 : (r + 1) * 96]
        for h in range(2):
            q = nn(pn, wa[r, :, 384 * h + 256 : 384 * h + 384])[:, 32:128].astype(BF16)
            n = 2 * r + h
            q2_out[n] = q
            k2_out[n, 0:PW, :] = kv[:, 192 * h : 192 * h + 96].astype(BF16)
            v2_out[n, 0:PW, :] = kv[:, 192 * h + 96 : 192 * h + 192].astype(BF16)
            k2_out[n, MEM0 : MEM0 + MEMROWS, :] = mem_two[r, 0, :, 96 * h : 96 * h + 96]
            v2_out[n, MEM0 : MEM0 + MEMROWS, :] = mem_two[r, 1, :, 96 * h : 96 * h + 96]
    scores = [nt(q2_out[n], k2_out[n]) for n in range(8)]
    shares = [softmax_rows(v, ok[...], fill[...]).astype(BF16) for v in scores]
    mixed = [nn(shares[n], v2_out[n]) + q2_out[n].astype(F32) for n in range(8)]
    for r in range(4):
        for h in range(2):
            mix2_out[r, :, 96 * h : 96 * h + 96] = mixed[2 * r + h].astype(BF16)
        for s in range(2):
            branch[s] = branch[s] + nt(mix2_out[r], wa[r, :, 384 * s : 384 * s + 384])
    mid2_out[...] = jnp.concatenate(branch, axis=1)


def feed_two(place, middle_in, cot, key_ok, index, to_up, to_down, vec768, bias_up, *rest):
    mine, other = groups_two(rest[0:4]), groups_two(rest[4:8])
    act_out, dmid_out, vec_out, bias_out, keep_rows, send_rows, keep_y, send_y = rest[8:16]
    wu, wd, acts, slopes, sem_u, sem_d = rest[16:22]
    load_weights(place[0], 0, mine, other, wu, sem_u)
    load_weights(place[0], 1, mine, other, wd, sem_d)
    p2 = natural(index, 2, 768)
    s2f = matching(index, 6, 384, 2, 768)
    gains2 = exact_nn(vec768[...], p2)
    middle = middle_in[...] + gains2[2:3, :]
    unit, inverse = normalise(middle)
    nm = (unit * gains2[0:1, :] + gains2[1:2, :]).astype(BF16)
    nm_up = [nn(nm[:, 384 * s : 384 * s + 384], to_up[...]).astype(BF16) for s in range(2)]
    dyb = nn(cot[...], p2).astype(BF16)
    dyb = jnp.concatenate([dyb, jnp.zeros((PW - WIN, 768), BF16)], axis=0)
    dy = dyb.astype(F32) * key_ok[...]
    dyb = dy.astype(BF16)
    dy_down = [nn(dyb[:, 384 * s : 384 * s + 384], to_down[...]).astype(BF16) for s in range(2)]
    dy_sel = nt(s2f, dyb).astype(BF16)
    nm_sel = nt(s2f, nm).astype(BF16)
    wait_weights(wu, sem_u)
    for r in range(4):
        hidden = nn(nm_up[0], wu[r, :, 0:768]) + nn(nm_up[1], wu[r, :, 768:1536])
        active, slope = gelu_both(hidden + bias_up[r : r + 1, :])
        acts[r] = active.astype(BF16)
        slopes[r] = slope
    wait_weights(wd, sem_d)

    def put_rows(r, lo, value):
        value = value.astype(BF16)
        for k in range(4):
            out = keep_rows if k < 2 else send_rows
            out[k % 2, r, :, lo : lo + 768] = value[48 * k : 48 * k + 48]

    def put_head(r, lo, value):
        out = keep_y if r < 2 else send_y
        out[r % 2, :, lo : lo + 768] = value.astype(BF16)

    down = [jnp.zeros((PW, 384), F32), jnp.zeros((PW, 384), F32)]
    dnm = [jnp.zeros((PW, 384), F32), jnp.zeros((PW, 384), F32)]
    dhs = [
        ((nn(dy_down[0], wd[r, :, 0:768]) + nn(dy_down[1], wd[r, :, 768:1536])) * slopes[r]).astype(BF16)
        for r in range(4)
    ]
    for r in range(4):
        active, dh = acts[r], dhs[r]
        bias_out[r : r + 1, :] = column_sum(dh.astype(F32))
        put_rows(r, 0, nn(nm_sel[0:192], dh))
        put_rows(r, 768, nn(dy_sel[0:192], active))
        put_head(r, 0, nn(nm_sel[192:384], dh))
        put_head(r, 768, nn(dy_sel[192:384], active))
        for s in range(2):
            down[s] = down[s] + nt(active, wd[r, :, 768 * s : 768 * s + 768])
            dnm[s] = dnm[s] + nt(dh, wu[r, :, 768 * s : 768 * s + 768])
    down = jnp.concatenate([close_nt(v, to_down[...]) for v in down], axis=1)
    output = (middle + gains2[3:4, :] + down).astype(BF16)
    act_out[...] = nt(output, p2)[0:WIN].astype(BF16)
    dnm = jnp.concatenate([close_nt(v, to_up[...]) for v in dnm], axis=1)
    dmid = dy + normalise_back(dnm, unit, inverse, gains2[0:1, :])
    dmid_out[...] = dmid
    vec = jnp.concatenate(
        [
            column_sum(dnm * unit),
            column_sum(dnm),
            column_sum(dmid),
            column_sum(dy),
            jnp.zeros((4, 768), F32),
        ],
        axis=0,
    )
    vec_out[...] = exact_nt(vec, p2)


def second_backward(
    place, dmid, passed, pn_in, queries, keys, values, mixes, index, gains_in, ok, fill, *rest
):
    mine, other = groups_one(rest[0:4]), groups_one(rest[4:8])
    dpassed, vec_out, keep, send = rest[8:12]
    wa, part, sem = rest[12:15]
    load_weights(place[0], 1, mine, other, wa, sem)
    xf = passed[...].astype(F32)
    unit, inverse = normalise(xf)
    pn = pn_in[...]
    dbr = dmid[...].astype(BF16)
    p1 = natural(index, 1, 384)
    pr = matching(index, 1, 384, 3, 384)
    s1 = matching(index, 4, 192, 1, 384)
    s2 = matching(index, 5, 384, 2, 768)
    dbr_sel = nt(s2, dbr).astype(BF16)
    pn_sel = nt(s1, pn).astype(BF16)
    dpooled = jnp.zeros((PW, 384), F32)
    part[...] = jnp.zeros_like(part)
    wait_weights(wa, sem)

    def put(r, lo, value):
        out = keep if r < 2 else send
        out[r % 2, :, lo : lo + 384] = value.astype(BF16)

    dmm = [nn(dbr[:, 0:384], wa[r, :, 0:384]) + nn(dbr[:, 384:768], wa[r, :, 384:768]) for r in range(4)]
    dres = [v[:, 192:288] for v in dmm]
    dmix = [dmm[n // 2][:, 96 * (n % 2) : 96 * (n % 2) + 96].astype(BF16) for n in range(8)]
    back = attend_back(
        [queries[n] for n in range(8)], [keys[n] for n in range(8)], [values[n] for n in range(8)],
        ok[...], fill[...], dmix,
    )
    for n, (dq, dk, dv) in enumerate(back):
        r, h = n // 2, n % 2
        part[r, h, :, 288:384] = dq.astype(BF16)
        part[r, 2, :, 192 * h : 192 * h + 96] = dk[0:PW].astype(BF16)
        part[r, 2, :, 192 * h + 96 : 192 * h + 192] = dv[0:PW].astype(BF16)
    for r in range(4):
        for s in range(2):
            put(r, 384 * s, nn(dbr_sel[192 * s : 192 * s + 192], mixes[r]) + nn(pn_sel, part[r, s]))
            dpooled = dpooled + nt(part[r, s], wa[r, :, 384 * s : 384 * s + 384])
        put(r, 768, nn(pn_sel, part[r, 2]))
        dpooled = dpooled + nt(part[r, 2], wa[r, :, 768:1152])
    dpooled = dpooled + close_nt(jnp.concatenate(dres, axis=1), pr)
    dpooled = dpooled * 0.25
    dnormed = jnp.concatenate([dpooled, dpooled, dpooled, dpooled], axis=0)
    gain = exact_nn(gains_in[...], p1)[0:1]
    dpassed[...] = normalise_back(dnormed, unit, inverse, gain).astype(BF16)
    vec = jnp.concatenate(
        [column_sum(dnormed * unit), column_sum(dnormed), jnp.zeros((6, 384), F32)], axis=0
    )
    vec_out[...] = exact_nt(vec, p1)


def first_backward(
    place, dpassed, x, q_in, k_in, v_in, mix_in, mid_in, act_in, slope_in,
    token_back, index, turn, vec384, ok, fill, vec_mid, vec_in, dbias_two, *rest
):
    mine, other = groups_one(rest[0:4]), groups_one(rest[4:8])
    xgrad, vec_keep, vec_send, keep, send = rest[8:13]
    weights, gains, part, sem = rest[13:17]
    load_weights(place[0], 0, mine, other, weights, sem)
    p1 = natural(index, 0, 384)
    gains[...] = exact_nn(vec384[...], p1)
    xf = x[...].astype(F32)
    unit_in, inv_in = normalise(xf)
    normed = unit_in * gains[0:1, :] + gains[2:3, :]
    nb = normed.astype(BF16)
    pn = pool_rows(normed).astype(BF16)
    middle = mid_in[...]
    unit_mid, inv_mid = normalise(middle)
    nm = (unit_mid * gains[1:2, :] + gains[3:4, :]).astype(BF16)
    sel = matching(index, 4, 192, 0, 384)
    dyb = nt(dpassed[...], turn[...]).astype(BF16)
    dy = dyb.astype(F32)
    dy_sel = nt(sel, dyb).astype(BF16)
    nm_sel = nt(sel, nm).astype(BF16)
    nb_sel = nt(sel, nb).astype(BF16)
    pn_sel = nt(sel, pn).astype(BF16)
    part[...] = jnp.zeros_like(part)
    wait_weights(weights, sem)

    def put(r, lo, value):
        value = value.astype(BF16)
        for k in range(4):
            out = keep if k < 2 else send
            out[k % 2, r, :, lo : lo + 384] = value[48 * k : 48 * k + 48]

    dnm = jnp.zeros((PT, 384), F32)
    dhs = [
        (nn(dyb, weights[r, :, 768:1152]) * slope_in[r].astype(F32)).astype(BF16) for r in range(4)
    ]
    for r in range(4):
        dh = dhs[r]
        row = 8 + 2 * (r % 2)
        out = vec_keep if r < 2 else vec_send
        out[row : row + 1, :] = dbias_two[r : r + 1, :]
        out[row + 1 : row + 2, 0:384] = column_sum(dh.astype(F32))
        out[row + 1 : row + 2, 384:768] = jnp.zeros((1, 384), F32)
        put(r, 768, nn(dy_sel, act_in[r]))
        put(r, 384, nn(nm_sel, dh))
        dnm = dnm + nt(dh, weights[r, :, 384:768])
    dmid = dy + normalise_back(dnm, unit_mid, inv_mid, gains[1:2, :])
    dbr = dmid.astype(BF16)
    dbr_sel = nt(sel, dbr).astype(BF16)
    dnormed = jnp.zeros((PT, 384), F32)
    dpooled = jnp.zeros((PW, 384), F32)
    dmix = [nn(dbr, weights[r, :, 0:96]).astype(BF16) for r in range(4)]
    back = attend_back(
        [q_in[r] for r in range(4)], [k_in[r] for r in range(4)], [v_in[r] for r in range(4)], ok[...], fill[...], dmix
    )
    for r, (dq, dk, dv) in enumerate(back):
        part[r, 0, :, 0:96] = mix_in[r]
        part[r, 1, :, 96:192] = dq.astype(BF16)
        part[r, 2, 0:PW, 192:288] = (dk[0:PW] * 0.25).astype(BF16)
        part[r, 2, 0:PW, 288:384] = (dv[0:PW] * 0.25).astype(BF16)
    for r in range(4):
        w = weights[r, :, 0:384]
        first = nn(dbr_sel, part[r, 0]) + nn(nb_sel, part[r, 1]) + 4.0 * nn(pn_sel, part[r, 2, 0:PW, :])
        dnormed = dnormed + nt(part[r, 1, :, 0:256], w[:, 0:256])
        dpooled = dpooled + nt(part[r, 2, 0:PW, 128:384], w[:, 128:384])
        put(r, 0, first)
    dnormed = dnormed + jnp.concatenate([dpooled, dpooled, dpooled, dpooled], axis=0)
    dx = normalise_back(dnormed, unit_in, inv_in, gains[0:1, :]) + dmid
    vec = jnp.concatenate(
        [
            column_sum(dnormed * unit_in),
            column_sum(dnm * unit_mid),
            column_sum(dnormed),
            column_sum(dnm),
            column_sum(dmid),
            column_sum(dy),
            jnp.zeros((2, 384), F32),
        ],
        axis=0,
    )
    vec = exact_nt(vec, p1)
    for out in (vec_keep, vec_send):
        out[0:4, :] = vec_mid[0:4, :]
        for k in range(3):
            out[4 + k : 5 + k, 0:384] = vec[2 * k : 2 * k + 1, :]
            out[4 + k : 5 + k, 384:768] = vec[2 * k + 1 : 2 * k + 2, :]
        out[7:8, 0:384] = vec_in[0:1, :]
        out[7:8, 384:768] = vec_in[1:2, :]
    dxb = nt(dx.astype(BF16), p1).astype(BF16)
    xgrad[...] = nn(token_back[...], dxb).astype(BF16)


def local_shards(place, out_one, qkv_one, up_one, down_one, out_two, res_two, qkv_two, up_two, down_two, first, second):
    @pl.when(place[0] == 0)
    def _():
        first[:, 0:96] = out_one[...]
        first[:, 96:384] = qkv_one[0]
        first[:, 384:768] = up_one[...]
        first[:, 768:1152] = down_one[...]
        up = up_two[...].astype(F32)
        second[:, 0:768] = up[0:24].astype(BF16)
        second[:, 768:1536] = up[24:48].astype(BF16)

    @pl.when(place[0] != 0)
    def _():
        out_t, res_t = out_two[...].astype(F32), res_two[...].astype(F32)
        for s in range(2):
            first[:, 384 * s : 384 * s + 192] = out_t[24 * s : 24 * s + 24].astype(BF16)
            first[:, 384 * s + 192 : 384 * s + 288] = res_t[24 * s : 24 * s + 24].astype(BF16)
            first[:, 384 * s + 288 : 384 * s + 384] = qkv_two[:, s, 0:96]
            first[:, 768 + 192 * s : 960 + 192 * s] = qkv_two[:, s, 96:288]
        down = down_two[...].astype(F32)
        second[:, 0:768] = down[0:24].astype(BF16)
        second[:, 768:1536] = down[24:48].astype(BF16)


def feed_outputs(part, got, grad_up, grad_down):
    total = part[...] + got[...].astype(F32)
    grad_up[0:12, :] = total[:, 0:768]
    grad_up[12:24, :] = total[:, 1536:2304]
    grad_down[0:12, :] = total[:, 768:1536]
    grad_down[12:24, :] = total[:, 2304:3072]


def last_outputs(
    part, got, vec_part, vec_got,
    qkv1, out1, up1, down1, bias1, gains1, shifts1, qkv2, out2, res2, bias2, gain_in, shift_in, gain_mid, shifts2,
):
    total = part[...] + got[...].astype(F32)
    vec = vec_part[...] + vec_got[...]
    out1[...] = total[:, 0:96]
    qkv1[:, 0, :] = total[:, 96:384]
    up1[...] = total[:, 384:768]
    down1[...] = total[:, 768:1152]
    for s in range(2):
        at = 1152 + 384 * s
        out2[12 * s : 12 * s + 12, :] = total[:, at : at + 192]
        res2[12 * s : 12 * s + 12, :] = total[:, at + 192 : at + 288]
        qkv2[:, s, 0:96] = total[:, at + 288 : at + 384]
        qkv2[:, s, 96:288] = total[:, 1920 + 192 * s : 2112 + 192 * s]
    gain_mid[...] = vec[0]
    shifts2[...] = vec[1:4, :]
    gains1[0:1, :] = vec[4:5, 0:384]
    gains1[1:2, :] = vec[4:5, 384:768]
    for n in range(2):
        shifts1[2 * n : 2 * n + 1, :] = vec[5 + n : 6 + n, 0:384]
        shifts1[2 * n + 1 : 2 * n + 2, :] = vec[5 + n : 6 + n, 384:768]
    gain_in[...] = vec[7, 0:384]
    shift_in[...] = vec[7, 384:768]
    bias2[...] = vec[8]
    bias1[...] = vec[9, 0:384]


def spec_vmem():
    return pl.BlockSpec(memory_space=pltpu.VMEM)


def spec_any():
    return pl.BlockSpec(memory_space=pltpu.HBM)


def spec_smem():
    return pl.BlockSpec(memory_space=pltpu.SMEM)


def call(body, inputs, kinds, outs, scratch, micros):
    specs = {"v": spec_vmem, "a": spec_any, "s": spec_smem}
    return pl.pallas_call(
        body,
        out_shape=outs,
        in_specs=[specs[k]() for k in kinds],
        out_specs=jax.tree.map(lambda _: spec_vmem(), outs),
        scratch_shapes=scratch,
        compiler_params=pltpu.CompilerParams(vmem_limit_bytes=VMEM_LIMIT),
        cost_estimate=pl.CostEstimate(flops=micros * 1_000_000_000, bytes_accessed=4_000_000, transcendentals=0),
    )(*inputs)


def shape(dims, dtype):
    return jax.ShapeDtypeStruct(dims, dtype)


CUT_ONE = 512
CUT_TWO = 896
ORDER = ((0, 1, 3, 2), (0, 3, 1, 2))


def hop(v, axis, late):
    pairs = []
    for core in range(2):
        flip = 3 if (core == 1) != late else 1
        for xi in range(4):
            for zi in range(4):
                for yi in range(4):
                    tx, tz, ty = xi, zi, yi
                    if axis == "x":
                        tx = xi ^ flip
                    elif axis == "z":
                        tz = zi ^ flip
                    else:
                        ty = yi ^ flip
                    here = ((core * 4 + xi) * 4 + zi) * 4 + yi
                    pairs.append((here, ((core * 4 + tx) * 4 + tz) * 4 + ty))
    return lax.ppermute(v, ("pipe", "dp", "head"), pairs)


def swap(v):
    return lax.ppermute(v, "pipe", [(0, 1), (1, 0)])


def ring_pair(v, axis):
    low = jnp.stack([v, hop(v, axis, False)])
    return low, hop(low, axis, True)


def ring_rows(v, axis):
    low, high = ring_pair(v, axis)
    both = jnp.concatenate([low, high], axis=0)
    return jnp.moveaxis(both, 0, -3).reshape(v.shape[:-2] + (4 * v.shape[-2], v.shape[-1]))


def ring_stack(v, axis):
    low, high = ring_pair(v, axis)
    return jnp.concatenate([low, high], axis=0)


def gather_one(local):
    rows = ring_rows(local, "z")
    first = ring_rows(rows[:, :CUT_ONE], "x")
    last = ring_stack(rows[:, CUT_ONE:], "y")
    first_pair, last_pair = ring_pair(first, "y"), ring_pair(last, "x")
    return first_pair + last_pair, rows, (first, last), (first_pair[0], last_pair[0])


def gather_two(local, ready):
    rows = ring_rows(local, "x")
    first = ring_stack(rows[:, :CUT_TWO], "y")
    last = ring_rows(rows[:, CUT_TWO:], "z")
    first, last = after((first, last), ready)
    return ring_pair(first, "z") + ring_pair(last, "y")


def half_sums(keep, got):
    onward = (keep[1].astype(F32) + got[1].astype(F32)).astype(keep.dtype)
    return keep[0].astype(F32) + got[0].astype(F32), onward


def ring_begin(keep, send, axis):
    return half_sums(keep, hop(send, axis, True))


def ring_end(begun, axis):
    part, onward = begun
    return part + hop(onward, axis, False).astype(F32)


def ring_sum(keep, send, axis):
    return ring_end(ring_begin(keep, send, axis), axis)


def halves(v):
    rows = v.shape[-2] // 4
    parts = [v[..., rows * n : rows * n + rows, :] for n in range(4)]
    return jnp.stack(parts[:2]), jnp.stack(parts[2:])


def low(v):
    return v.astype(BF16)


def after(v, other):
    return lax.optimization_barrier((v, other))[0]


def lock(*values):
    return lax.optimization_barrier(values)


def send_clip(value, rounds):
    pairs = [(p * 4 + source, p * 4 + target) for p, source, target in rounds]
    return lax.ppermute(value, ("pipe", "head"), pairs)


def spread_near(v):
    return send_clip(v, [(0, 0, 1), (0, 1, 0), (1, 2, 3), (1, 3, 2)])


def spread_far(v, near, pipe, y):
    even = (y % 2) == 0
    both = jnp.stack([jnp.where(even, v, near), jnp.where(even, near, v)])
    far = send_clip(both, [(0, 0, 3), (0, 1, 2), (1, 2, 1), (1, 3, 0)])
    return jnp.where((y // 2) == pipe, both, far)[:, None]


def token_order():
    order = np.zeros((PT, TOK), np.float32)
    for block in range(4):
        for window in range(WIN):
            row = (window // 10) * 2 + block // 2
            col = (window % 10) * 2 + block % 2
            order[block * PW + window, row * GRID + col] = 1
    return order


def turn_matrix(core_from, core_to, rows_from, rows_to):
    def labels(core, outer):
        out = []
        for a in range(4):
            for b in range(4):
                one, two = ORDER[core][a], ORDER[core][b]
                out.append((one, two) if outer == "x" else (two, one))
        return out

    source, target = labels(core_from, rows_from), labels(core_to, rows_to)
    matrix = np.zeros((384, 384), np.float32)
    for n, label in enumerate(source):
        m = target.index(label)
        matrix[n * 24 : n * 24 + 24, m * 24 : m * 24 + 24] = np.eye(24)
    return jnp.asarray(matrix, BF16)


def per_device(
    clips_in, cotangent, token_mask, memory_valid, memory_one, memory_two,
    qkv_one, out_one, up_one, down_one, up_bias_one, gains_one, shifts_one,
    qkv_two, out_two, res_two, up_two, down_two, up_bias_two, gain_two_in, shift_two_in, gains_two, shifts_two,
):
    pipe = lax.axis_index("pipe")
    dp = lax.axis_index("dp")
    y = lax.axis_index("head")
    x_at, z_at = dp // 4, dp % 4
    first_core = pipe == 0

    place = pipe.astype(jnp.int32).reshape(1)
    shard_one, shard_two = call(
        local_shards,
        (
            place, out_one.T, jnp.transpose(qkv_one, (1, 0, 2)), up_one, down_one.T,
            out_two.T, res_two.T, qkv_two, up_two, down_two.T,
        ),
        "s" + "v" * 9,
        (shape((24, 1152), BF16), shape((24, 1536), BF16)),
        [],
        1,
    )
    mine_one, rows_ready, ready, late = gather_one(shard_one)
    mine_two = gather_two(shard_two, ready)
    other_one = tuple(swap(v) for v in mine_one)

    def clip_of(v, at):
        return lax.dynamic_index_in_dim(v, at, 0, keepdims=False)

    near = jnp.where(first_core, 1, 3)
    far = 4 - near
    biases = jnp.concatenate([up_bias_one, up_bias_two])
    biases = jnp.concatenate(thirds(biases)).reshape(12, 288)
    memory = jnp.concatenate([memory_one[:, 0], memory_two[:, 0]], axis=-1)

    memory, biases = after((memory, biases), rows_ready)

    def payload(flip):
        part = clip_of(memory, y ^ flip).reshape(2 * MEMROWS, 288)
        return jnp.concatenate([part, biases], axis=0)

    got = hop(jnp.stack([payload(near), payload(2)]), "y", False)
    more = hop(jnp.stack([payload(far), got[1]]), "y", True)
    parcels = jnp.stack([payload(0), got[0], more[0], more[1]])
    memory = parcels[:, : 2 * MEMROWS].reshape(4, 2, MEMROWS, 288)
    mem_one, mem_two = memory[..., :96], memory[..., 96:]
    biases = parcels[:, 2 * MEMROWS :].astype(F32).reshape(4, 3, 1152)
    biases = biases[:, 0] + biases[:, 1] + biases[:, 2]
    bias_one, bias_two = biases[:, :384], biases[:, 384:]

    pipe, y, x_at, z_at = after((pipe, y, x_at, z_at), late)
    first_core = pipe == 0

    flags = clip_of(token_mask[:, 0], y).reshape(10, 2, 10, 2)[:, 0, :, 0].reshape(WIN)
    key_ok = (flags > 0).astype(F32)
    mem_ok = jnp.repeat((clip_of(memory_valid[:, 0], y) > 0).astype(F32), MEMROWS // 2)
    gap = jnp.zeros((MEM0 - WIN,), F32)
    tail = jnp.zeros((KEYS - MEM0 - MEMROWS,), F32)
    ok = jnp.concatenate([key_ok, gap, mem_ok, tail]).reshape(1, KEYS)
    fill = np.full((1, KEYS), ABSENT, np.float32)
    fill[0, :WIN] = MASKED
    fill[0, MEM0 : MEM0 + MEMROWS] = MASKED
    fill = jnp.asarray(fill)
    key_col = jnp.concatenate([key_ok, jnp.zeros((PW - WIN,), F32)]).reshape(PW, 1)

    def order_of(core, n):
        return jnp.asarray(ORDER[core], jnp.int32)[n]

    def own_order(n):
        return jnp.where(first_core, order_of(0, n), order_of(1, n))

    k = np.arange(384)
    k_outer, k_inner, k_row = k // 96, (k // 24) % 4, k % 24

    def chip(a, b):
        return (x_at ^ a) * 4 + (z_at ^ b)

    piece0 = chip(order_of(0, k_outer), order_of(0, k_inner))
    piece1 = chip(order_of(1, k_outer), order_of(1, k_inner))
    raw0 = piece0 * 24 + k_row
    raw1 = piece1 * 24 + k_row
    raw2 = jnp.concatenate([piece1 * 48 + k_row, piece1 * 48 + 24 + k_row])
    head_raw = (y ^ own_order(k // 96)) * 96 + k % 96
    j = np.arange(192)
    j_outer, j_inner, j_row = own_order(j // 48), own_order((j // 12) % 4), j % 12
    rows_x = pipe * 192 + chip(j_outer, j_inner) * 12 + j_row
    rows_x2 = pipe * 384 + chip(j_outer, j_inner) * 24 + j_row
    rows_z2 = pipe * 384 + chip(j_inner, j_outer) * 24 + j_row
    pair = np.array([[0], [12]])
    rows_x2 = (rows_x2[None, :] + pair).reshape(384)
    rows_z2 = (rows_z2[None, :] + pair).reshape(384)
    index = [raw0, raw1, raw2, head_raw, rows_x, rows_x2, rows_z2, raw0]
    index = jnp.stack([jnp.pad(v, (0, 768 - v.shape[0])) for v in index]).astype(F32)
    turn = turn_matrix(0, 1, "x", "x")
    to_up = turn_matrix(1, 0, "x", "z")
    to_down = turn_matrix(1, 1, "x", "z")

    order = token_order()
    token_perm = jnp.asarray(order, BF16)
    token_back = jnp.asarray(order.T, BF16)
    vec384 = jnp.concatenate([gains_one, shifts_one, gain_two_in[None], shift_two_in[None]], axis=0)
    gains_in = jnp.concatenate([gain_two_in[None], jnp.zeros((7, 384), F32)], axis=0)
    vec768 = jnp.concatenate([gains_two[None], shifts_two, jnp.zeros((4, 768), F32)], axis=0)
    x = clip_of(clips_in[:, 0], y)
    cot = clip_of(cotangent[:, 0], y)

    x, key_col, vec768, gains_in, bias_two, cot, mem_two = lock(
        x, key_col, vec768, gains_in, bias_two, cot, mem_two
    )
    other_two = tuple(swap(v) for v in mine_two)

    dma = pltpu.SemaphoreType.DMA
    saved = call(
        forward,
        (
            place, x, token_perm, index, turn, vec384, ok, fill, mem_one, mem_two, bias_one,
            *mine_one, *other_one,
        ),
        "s" + "v" * 10 + "a" * 8,
        (
            shape((PT, 384), BF16), shape((PT, 384), BF16),
            shape((4, PT, HEAD), BF16), shape((4, KEYS, HEAD), BF16), shape((4, KEYS, HEAD), BF16),
            shape((4, PT, HEAD), BF16), shape((PT, 384), F32),
            shape((4, PT, 384), BF16), shape((4, PT, 384), BF16),
            shape((PW, 384), BF16), shape((8, PW, HEAD), BF16), shape((8, KEYS, HEAD), BF16),
            shape((8, KEYS, HEAD), BF16), shape((4, PW, 384), BF16), shape((PW, 768), F32),
        ),
        [
            pltpu.VMEM((4, 384, 1152), BF16), pltpu.VMEM((4, 384, 1152), BF16), pltpu.VMEM((8, 384), F32),
            dma(()), dma(()),
        ],
        18,
    )
    passed, x_kept, q1, k1, v1, mix1, mid1, act1, slope1, pn2, q2k, k2, v2, mix2, mid2 = saved

    feed = call(
        feed_two,
        (place, mid2, cot, key_col, index, to_up, to_down, vec768, bias_two, *mine_two, *other_two),
        "s" + "v" * 8 + "a" * 8,
        (
            shape((WIN, 768), BF16), shape((PW, 768), F32), shape((8, 768), F32), shape((4, 768), F32),
            shape((2, 4, 48, 1536), BF16), shape((2, 4, 48, 1536), BF16),
            shape((2, 192, 1536), BF16), shape((2, 192, 1536), BF16),
        ),
        [
            pltpu.VMEM((4, 384, 1536), BF16), pltpu.VMEM((4, 384, 1536), BF16),
            pltpu.VMEM((4, PW, 768), BF16), pltpu.VMEM((4, PW, 768), F32), dma(()), dma(()),
        ],
        14,
    )
    activation, dmid2, vec_mid, dbias_two, keep_rows, send_rows, keep_y, send_y = feed
    got_a = hop(send_rows, "z", True)
    got_b = hop(send_y, "y", True)

    second = call(
        second_backward,
        (
            place, dmid2, passed, pn2, q2k, k2, v2, mix2, index, gains_in, ok, fill,
            *mine_one, *other_one,
        ),
        "s" + "v" * 11 + "a" * 8,
        (
            shape((PT, 384), BF16), shape((8, 384), F32),
            shape((2, 192, 1152), BF16), shape((2, 192, 1152), BF16),
        ),
        [pltpu.VMEM((4, 384, 1152), BF16), pltpu.VMEM((4, 3, PW, 384), BF16), dma(())],
        1,
    )
    dpassed, vec_in, keep_attn, send_attn = second
    attn_got = hop(send_attn, "y", True)

    third = call(
        first_backward,
        (
            place, dpassed, x_kept, q1, k1, v1, mix1, mid1, act1, slope1,
            token_back, index, turn, vec384, ok, fill, vec_mid, vec_in, dbias_two, *mine_one, *other_one,
        ),
        "s" + "v" * 18 + "a" * 8,
        (
            shape((TOK, 384), BF16), shape((12, 768), F32), shape((12, 768), F32),
            shape((2, 4, 48, 1152), BF16), shape((2, 4, 48, 1152), BF16),
        ),
        [
            pltpu.VMEM((4, 384, 1152), BF16), pltpu.VMEM((8, 384), F32), pltpu.VMEM((4, 3, PT, 384), BF16), dma(()),
        ],
        1,
    )
    third, got_a, got_b, attn_got, activation = lock(third, got_a, got_b, attn_got, activation)
    xgrad, vec_keep, vec_send, keep_one, send_one = third

    vectors = vec_keep + hop(vec_send, "y", True)
    act_near = spread_near(activation)
    one_sum = ring_begin(keep_one, send_one, "x")
    feed_a = low(ring_end(half_sums(keep_rows, got_a), "z"))
    feed_b = low(ring_end(half_sums(keep_y, got_b), "y"))
    attn_sum = half_sums(keep_attn, attn_got)
    vectors, attn_sum, one_sum, feed_a, feed_b, xgrad, act_near = lock(
        vectors, attn_sum, one_sum, feed_a, feed_b, xgrad, act_near
    )

    vectors = vectors[:10] + hop(jnp.concatenate([vectors[:8], vectors[10:]], axis=0), "y", False)
    feed_a = ring_begin(feed_a[0:2], feed_a[2:4], "y")
    feed_b = ring_begin(*halves(feed_b), "z")
    attn_sum = low(ring_end(attn_sum, "y"))
    one_sum = low(ring_end(one_sum, "x"))
    vectors, feed_a, feed_b, attn_sum, one_sum, xgrad, act_near = lock(
        vectors, feed_a, feed_b, attn_sum, one_sum, xgrad, act_near
    )

    vectors = vectors + hop(vectors, "x", True)
    feed_a = low(ring_end(feed_a, "y"))
    feed_b = low(ring_end(feed_b, "z"))
    attn_sum = ring_begin(*halves(attn_sum), "x")
    one_sum = ring_begin(one_sum[0:2], one_sum[2:4], "y")
    grad_near = spread_near(xgrad)
    vectors, feed_a, feed_b, attn_sum, one_sum, grad_near, act_near = lock(
        vectors, feed_a, feed_b, attn_sum, one_sum, grad_near, act_near
    )

    vectors = vectors + hop(vectors, "x", False)
    feed_sum = ring_begin(*halves(jnp.concatenate([feed_a, feed_b], axis=1)), "x")
    attn_sum = low(ring_end(attn_sum, "x"))
    one_sum = low(ring_end(one_sum, "y"))
    input_grad = spread_far(xgrad, grad_near, pipe, y)
    vectors, feed_sum, attn_sum, one_sum, act_near = lock(vectors, feed_sum, attn_sum, one_sum, act_near)

    feed_part, feed_onward = feed_sum
    feed_got = hop(feed_onward, "x", False)
    activations = spread_far(activation, act_near, pipe, y)
    vectors = vectors + hop(vectors, "z", True)
    rest_sum = ring_begin(*halves(jnp.concatenate([one_sum, attn_sum], axis=1)), "z")
    vectors, rest_sum, input_grad, feed_got = lock(vectors, rest_sum, input_grad, feed_got)
    grad_up_two, grad_down_two = call(
        feed_outputs,
        (feed_part, feed_got),
        "vv",
        (shape((24, 768), F32), shape((24, 768), F32)),
        [],
        2,
    )

    rest_part, rest_onward = rest_sum
    vectors_got = hop(vectors, "z", False)
    rest_got = hop(rest_onward, "z", False)
    outs = call(
        last_outputs,
        (rest_part, rest_got, vectors, vectors_got),
        "vvvv",
        (
            shape((12, 1, 288), F32), shape((12, 96), F32), shape((12, 384), F32), shape((12, 384), F32),
            shape((384,), F32), shape((2, 384), F32), shape((4, 384), F32),
            shape((12, 2, 288), F32), shape((24, 192), F32), shape((24, 96), F32),
            shape((768,), F32), shape((384,), F32), shape((384,), F32), shape((768,), F32),
            shape((3, 768), F32),
        ),
        [],
        2,
    )
    return (
        activations,
        input_grad,
        outs[0],
        outs[1].T,
        outs[2],
        outs[3].T,
        *outs[4:8],
        outs[8].T,
        outs[9].T,
        grad_up_two,
        grad_down_two.T,
        *outs[10:15],
    )


def solution(mesh):
    return jax.shard_map(
        per_device,
        mesh=mesh,
        in_specs=(
            P(None, "dp", None, None), P(None, "dp", None, None), P(None, "dp", None), P(None, "dp", None),
            P(None, "dp", None, None, "head"), P(None, "dp", None, None, "head"),
            P("dp", "head", None), P("head", "dp"), P("dp", "head"), P("head", "dp"), P("head"), P(), P(),
            P("dp", "head", None), P("head", "dp"), P("head", "dp"), P("dp", "head"), P("head", "dp"), P("head"),
            P(), P(), P(), P(),
        ),
        out_specs=(
            P("pipe", "dp", None, None), P("pipe", "dp", None, None),
            P(("pipe", "dp"), "head", None), P("head", ("pipe", "dp")), P(("pipe", "dp"), "head"),
            P("head", ("pipe", "dp")), P("head"), P(), P(),
            P(("pipe", "dp"), "head", None), P("head", ("pipe", "dp")), P("head", ("pipe", "dp")),
            P(("pipe", "dp"), "head"), P("head", ("pipe", "dp")), P("head"), P(), P(), P(), P(),
        ),
        check_vma=False,
    )
```

```python
import functools

import jax
import jax.numpy as jnp
import numpy as np
from jax import lax
from jax.experimental import pallas as pl
from jax.experimental.pallas import tpu as pltpu
from jax.sharding import PartitionSpec as P

F32 = jnp.float32
BF16 = jnp.bfloat16
GRID = 20
TOK = 400
WIN = 100
PW = 104
PT = 4 * PW
KEYS = 256
MEM0 = 112
MEMROWS = 50
HEAD = 96
EPS = 1e-06
MASKED = -1000000000.0
ABSENT = -3e38
SCALE = HEAD ** (-0.5)
VMEM_LIMIT = 56 * 1024 * 1024


def nn(a, b):
    return lax.dot_general(a, b, (((1,), (0,)), ((), ())), preferred_element_type=F32)


def nt(a, b):
    return lax.dot_general(a, b, (((1,), (1,)), ((), ())), preferred_element_type=F32)


def tn(a, b):
    return lax.dot_general(a, b, (((0,), (0,)), ((), ())), preferred_element_type=F32)


def thirds(v):
    high = v.astype(BF16)
    rest = v - high.astype(F32)
    mid = rest.astype(BF16)
    low = (rest - mid.astype(F32)).astype(BF16)
    return high, mid, low


def exact_nn(v, m):
    a, b, c = thirds(v)
    return nn(a, m) + nn(b, m) + nn(c, m)


def exact_nt(v, m):
    a, b, c = thirds(v)
    return nt(a, m) + nt(b, m) + nt(c, m)


def normalise(v):
    average = jnp.mean(v, axis=-1, keepdims=True)
    centred = v - average
    variance = jnp.mean(centred * centred, axis=-1, keepdims=True)
    inverse = lax.rsqrt(variance + EPS)
    return centred * inverse, inverse


def normalise_back(grad, unit, inverse, gain):
    scaled = grad * gain
    mean_one = jnp.mean(scaled, axis=-1, keepdims=True)
    mean_two = jnp.mean(scaled * unit, axis=-1, keepdims=True)
    return inverse * (scaled - mean_one - unit * mean_two)


def column_sum(v):
    return jnp.sum(v, axis=0, keepdims=True)


def gelu_both(h):
    cdf = 0.5 + 0.5 * lax.erf(h * 0.7071067811865476)
    density = 0.3989422804014327 * jnp.exp(-0.5 * h * h)
    return h * cdf, cdf + h * density


def pool_rows(v):
    return 0.25 * (v[0:PW] + v[PW : 2 * PW] + v[2 * PW : 3 * PW] + v[3 * PW : 4 * PW])


def softmax_rows(scores, ok, fill):
    scores = jnp.where(ok > 0, scores * SCALE, fill)
    peak = jnp.max(scores, axis=-1, keepdims=True)
    expos = jnp.exp(scores - peak)
    return expos / jnp.sum(expos, axis=-1, keepdims=True)


def attend_back(q, keys, values, ok, fill, dmix):
    n = range(len(q))
    scores = [nt(q[i], keys[i]) for i in n]
    dshares = [nt(dmix[i], values[i]) for i in n]
    shares = [softmax_rows(v, ok, fill) for v in scores]
    dvalues = [tn(shares[i].astype(BF16), dmix[i]) for i in n]
    inner = [jnp.sum(shares[i] * dshares[i], axis=-1, keepdims=True) for i in n]
    dscores = [(shares[i] * (dshares[i] - inner[i])).astype(BF16) for i in n]
    dq = [nn(dscores[i], keys[i]) * SCALE + dmix[i].astype(F32) for i in n]
    dkeys = [tn(dscores[i], q[i]) * SCALE for i in n]
    return [(dq[i], dkeys[i], dvalues[i]) for i in n]


def index_row(index, row, size):
    return index[row : row + 1, 0:size]


def index_col(index, row, size):
    return jnp.broadcast_to(index[row : row + 1, 0:size], (8, size)).T[:, 0:1]


def natural(index, row, size):
    values = lax.broadcasted_iota(jnp.int32, (size, size), 0).astype(F32)
    return (values == index_row(index, row, size)).astype(F32).astype(BF16)


def matching(index, row, rows, col, cols):
    return (index_col(index, row, rows) == index_row(index, col, cols)).astype(F32).astype(BF16)


def close_nt(v, m):
    high = v.astype(BF16)
    return nt(high, m) + nt((v - high.astype(F32)).astype(BF16), m)


def load_weights(core, owner, mine, other, dst, sem):
    def copies(groups, places):
        for h in (0, *(n for n in (1, 2, 3) if places[n] == 1), *(n for n in (1, 2, 3) if places[n] != 1)):
            at = 0
            done = sem.at[places[h]]
            for kind, low, high in groups:
                cols = pl.ds(at, low.shape[-1])
                at += low.shape[-1]
                if kind == "y":
                    slab = (low if h < 2 else high).at[h % 2]
                    pltpu.make_async_copy(slab, dst.at[places[h], :, cols], done).start()
                else:
                    for n in range(4):
                        slab = (low if n < 2 else high).at[n % 2, h]
                        pltpu.make_async_copy(slab, dst.at[places[h], pl.ds(96 * n, 96), cols], done).start()

    @pl.when(core == owner)
    def _():
        copies(mine, (0, 1, 2, 3))

    @pl.when(core != owner)
    def _():
        copies(other, (0, 2, 1, 3))


def heads_ready(dst, sem):
    for r in range(4):
        pltpu.make_async_copy(dst.at[r], dst.at[r], sem.at[r]).wait()
        yield r


def groups_one(refs):
    return [("y", refs[0], refs[1]), ("rows", refs[2], refs[3])]


def groups_two(refs):
    return [("rows", refs[0], refs[1]), ("y", refs[2], refs[3])]


def forward(
    place, x, token_perm, index, turn, vec384, ok, fill, mem_one, mem_two, bias_up, *rest
):
    mine, other = groups_one(rest[0:4]), groups_one(rest[4:8])
    (passed, x_out, q_out, k_out, v_out, mix_out, mid_out, act_out, slope_out,
     pn_out, q2_out, k2_out, v2_out, mix2_out, mid2_out) = rest[8:23]
    w1, wa, gains, sem_one, sem_attn = rest[23:28]
    load_weights(place[0], 0, mine, other, w1, sem_one)
    load_weights(place[0], 1, mine, other, wa, sem_attn)
    p1 = natural(index, 0, 384)
    pr = matching(index, 1, 384, 3, 384)
    gains[...] = exact_nn(vec384[...], p1)
    xb = nn(x[...], p1).astype(BF16)
    xb = nn(token_perm[...], xb).astype(BF16)
    x_out[...] = xb
    xf = xb.astype(F32)
    unit, _ = normalise(xf)
    normed = unit * gains[0:1, :] + gains[2:3, :]
    nb = normed.astype(BF16)
    pn = pool_rows(normed).astype(BF16)
    k_out[...] = jnp.zeros_like(k_out)
    v_out[...] = jnp.zeros_like(v_out)
    k2_out[...] = jnp.zeros_like(k2_out)
    v2_out[...] = jnp.zeros_like(v2_out)
    mix2_out[...] = jnp.zeros_like(mix2_out)
    for r in heads_ready(w1, sem_one):
        w = w1[r, :, 0:384]
        q_out[r] = nn(nb, w[:, 0:256])[:, 96:192].astype(BF16)
        kv = nn(pn, w)
        k_out[r, 0:PW, :] = kv[:, 192:288].astype(BF16)
        v_out[r, 0:PW, :] = kv[:, 288:384].astype(BF16)
        k_out[r, MEM0 : MEM0 + MEMROWS, :] = mem_one[r, 0]
        v_out[r, MEM0 : MEM0 + MEMROWS, :] = mem_one[r, 1]
    scores = [nt(q_out[r], k_out[r]) for r in range(4)]
    shares = [softmax_rows(v, ok[...], fill[...]).astype(BF16) for v in scores]
    branch = jnp.zeros((PT, 384), F32)
    for r in range(4):
        mixed = (nn(shares[r], v_out[r]) + q_out[r].astype(F32)).astype(BF16)
        mix_out[r] = mixed
        branch = branch + nt(mixed, w1[r, :, 0:96])
    middle = xf + gains[4:5, :] + branch
    mid_out[...] = middle
    unit, _ = normalise(middle)
    nm = (unit * gains[1:2, :] + gains[3:4, :]).astype(BF16)
    total = middle + gains[5:6, :]
    for r in range(4):
        hidden = nn(nm, w1[r, :, 384:768]) + bias_up[r : r + 1, :]
        active, slope = gelu_both(hidden)
        active = active.astype(BF16)
        act_out[r] = active
        slope_out[r] = slope.astype(BF16)
    for r in range(4):
        total = total + nt(act_out[r], w1[r, :, 768:1152])
    xb = nn(total.astype(BF16), turn[...]).astype(BF16)
    passed[...] = xb

    xf = xb.astype(F32)
    gains[...] = exact_nn(gains[...], turn[...])
    unit, _ = normalise(xf)
    normed = unit * gains[6:7, :] + gains[7:8, :]
    pn = pool_rows(normed).astype(BF16)
    pn_out[...] = pn
    pnr = nn(pn, pr).astype(BF16)
    branch = [jnp.zeros((PW, 384), F32), jnp.zeros((PW, 384), F32)]
    for r in heads_ready(wa, sem_attn):
        kv = nn(pn, wa[r, :, 768:1152])
        mix2_out[r, :, 192:288] = pnr[:, r * 96 : (r + 1) * 96]
        for h in range(2):
            q = nn(pn, wa[r, :, 384 * h + 256 : 384 * h + 384])[:, 32:128].astype(BF16)
            n = 2 * r + h
            q2_out[n] = q
            k2_out[n, 0:PW, :] = kv[:, 192 * h : 192 * h + 96].astype(BF16)
            v2_out[n, 0:PW, :] = kv[:, 192 * h + 96 : 192 * h + 192].astype(BF16)
            k2_out[n, MEM0 : MEM0 + MEMROWS, :] = mem_two[r, 0, :, 96 * h : 96 * h + 96]
            v2_out[n, MEM0 : MEM0 + MEMROWS, :] = mem_two[r, 1, :, 96 * h : 96 * h + 96]
    scores = [nt(q2_out[n], k2_out[n]) for n in range(8)]
    shares = [softmax_rows(v, ok[...], fill[...]).astype(BF16) for v in scores]
    mixed = [nn(shares[n], v2_out[n]) + q2_out[n].astype(F32) for n in range(8)]
    for r in range(4):
        for h in range(2):
            mix2_out[r, :, 96 * h : 96 * h + 96] = mixed[2 * r + h].astype(BF16)
        for s in range(2):
            branch[s] = branch[s] + nt(mix2_out[r], wa[r, :, 384 * s : 384 * s + 384])
    mid2_out[...] = jnp.concatenate(branch, axis=1)


def feed_two(place, middle_in, cot, key_ok, index, to_up, to_down, vec768, bias_up, *rest):
    mine, other = groups_two(rest[0:4]), groups_two(rest[4:8])
    act_out, dmid_out, vec_out, bias_out, keep_rows, send_rows, keep_y, send_y = rest[8:16]
    wu, wd, acts, slopes, sem_u, sem_d = rest[16:22]
    load_weights(place[0], 0, mine, other, wu, sem_u)
    load_weights(place[0], 1, mine, other, wd, sem_d)
    p2 = natural(index, 2, 768)
    s2f = matching(index, 6, 384, 2, 768)
    gains2 = exact_nn(vec768[...], p2)
    middle = middle_in[...] + gains2[2:3, :]
    unit, inverse = normalise(middle)
    nm = (unit * gains2[0:1, :] + gains2[1:2, :]).astype(BF16)
    nm_up = [nn(nm[:, 384 * s : 384 * s + 384], to_up[...]).astype(BF16) for s in range(2)]
    dyb = nn(cot[...], p2).astype(BF16)
    dyb = jnp.concatenate([dyb, jnp.zeros((PW - WIN, 768), BF16)], axis=0)
    dy = dyb.astype(F32) * key_ok[...]
    dyb = dy.astype(BF16)
    dy_down = [nn(dyb[:, 384 * s : 384 * s + 384], to_down[...]).astype(BF16) for s in range(2)]
    dy_sel = nt(s2f, dyb).astype(BF16)
    nm_sel = nt(s2f, nm).astype(BF16)
    for r in heads_ready(wu, sem_u):
        hidden = nn(nm_up[0], wu[r, :, 0:768]) + nn(nm_up[1], wu[r, :, 768:1536])
        active, slope = gelu_both(hidden + bias_up[r : r + 1, :])
        acts[r] = active.astype(BF16)
        slopes[r] = slope

    def put_rows(r, lo, value):
        value = value.astype(BF16)
        for k in range(4):
            out = keep_rows if k < 2 else send_rows
            out[k % 2, r, :, lo : lo + 768] = value[48 * k : 48 * k + 48]

    def put_head(r, lo, value):
        out = keep_y if r < 2 else send_y
        out[r % 2, :, lo : lo + 768] = value.astype(BF16)

    down = [jnp.zeros((PW, 384), F32), jnp.zeros((PW, 384), F32)]
    dnm = [jnp.zeros((PW, 384), F32), jnp.zeros((PW, 384), F32)]
    dhs = [
        ((nn(dy_down[0], wd[r, :, 0:768]) + nn(dy_down[1], wd[r, :, 768:1536])) * slopes[r]).astype(BF16)
        for r in heads_ready(wd, sem_d)
    ]
    for r in range(4):
        active, dh = acts[r], dhs[r]
        bias_out[r : r + 1, :] = column_sum(dh.astype(F32))
        put_rows(r, 0, nn(nm_sel[0:192], dh))
        put_rows(r, 768, nn(dy_sel[0:192], active))
        put_head(r, 0, nn(nm_sel[192:384], dh))
        put_head(r, 768, nn(dy_sel[192:384], active))
        for s in range(2):
            down[s] = down[s] + nt(active, wd[r, :, 768 * s : 768 * s + 768])
            dnm[s] = dnm[s] + nt(dh, wu[r, :, 768 * s : 768 * s + 768])
    down = jnp.concatenate([close_nt(v, to_down[...]) for v in down], axis=1)
    output = (middle + gains2[3:4, :] + down).astype(BF16)
    act_out[...] = nt(output, p2)[0:WIN].astype(BF16)
    dnm = jnp.concatenate([close_nt(v, to_up[...]) for v in dnm], axis=1)
    dmid = dy + normalise_back(dnm, unit, inverse, gains2[0:1, :])
    dmid_out[...] = dmid
    vec = jnp.concatenate(
        [
            column_sum(dnm * unit),
            column_sum(dnm),
            column_sum(dmid),
            column_sum(dy),
            jnp.zeros((4, 768), F32),
        ],
        axis=0,
    )
    vec_out[...] = exact_nt(vec, p2)


def second_backward(
    place, dmid, passed, pn_in, queries, keys, values, mixes, index, gains_in, ok, fill, *rest
):
    mine, other = groups_one(rest[0:4]), groups_one(rest[4:8])
    dpassed, vec_out, keep, send = rest[8:12]
    wa, part, sem = rest[12:15]
    load_weights(place[0], 1, mine, other, wa, sem)
    xf = passed[...].astype(F32)
    unit, inverse = normalise(xf)
    pn = pn_in[...]
    dbr = dmid[...].astype(BF16)
    p1 = natural(index, 1, 384)
    pr = matching(index, 1, 384, 3, 384)
    s1 = matching(index, 4, 192, 1, 384)
    s2 = matching(index, 5, 384, 2, 768)
    dbr_sel = nt(s2, dbr).astype(BF16)
    pn_sel = nt(s1, pn).astype(BF16)
    dpooled = jnp.zeros((PW, 384), F32)
    part[...] = jnp.zeros_like(part)

    def put(r, lo, value):
        out = keep if r < 2 else send
        out[r % 2, :, lo : lo + 384] = value.astype(BF16)

    dmm = [nn(dbr[:, 0:384], wa[r, :, 0:384]) + nn(dbr[:, 384:768], wa[r, :, 384:768]) for r in heads_ready(wa, sem)]
    dres = [v[:, 192:288] for v in dmm]
    dmix = [dmm[n // 2][:, 96 * (n % 2) : 96 * (n % 2) + 96].astype(BF16) for n in range(8)]
    back = attend_back(
        [queries[n] for n in range(8)], [keys[n] for n in range(8)], [values[n] for n in range(8)],
        ok[...], fill[...], dmix,
    )
    for n, (dq, dk, dv) in enumerate(back):
        r, h = n // 2, n % 2
        part[r, h, :, 288:384] = dq.astype(BF16)
        part[r, 2, :, 192 * h : 192 * h + 96] = dk[0:PW].astype(BF16)
        part[r, 2, :, 192 * h + 96 : 192 * h + 192] = dv[0:PW].astype(BF16)
    for r in range(4):
        for s in range(2):
            put(r, 384 * s, nn(dbr_sel[192 * s : 192 * s + 192], mixes[r]) + nn(pn_sel, part[r, s]))
            dpooled = dpooled + nt(part[r, s], wa[r, :, 384 * s : 384 * s + 384])
        put(r, 768, nn(pn_sel, part[r, 2]))
        dpooled = dpooled + nt(part[r, 2], wa[r, :, 768:1152])
    dpooled = dpooled + close_nt(jnp.concatenate(dres, axis=1), pr)
    dpooled = dpooled * 0.25
    dnormed = jnp.concatenate([dpooled, dpooled, dpooled, dpooled], axis=0)
    gain = exact_nn(gains_in[...], p1)[0:1]
    dpassed[...] = normalise_back(dnormed, unit, inverse, gain).astype(BF16)
    vec = jnp.concatenate(
        [column_sum(dnormed * unit), column_sum(dnormed), jnp.zeros((6, 384), F32)], axis=0
    )
    vec_out[...] = exact_nt(vec, p1)


def first_backward(
    place, dpassed, x, q_in, k_in, v_in, mix_in, mid_in, act_in, slope_in,
    token_back, index, turn, vec384, ok, fill, vec_mid, vec_in, dbias_two, *rest
):
    mine, other = groups_one(rest[0:4]), groups_one(rest[4:8])
    xgrad, vec_keep, vec_send, keep, send = rest[8:13]
    weights, gains, part, sem = rest[13:17]
    load_weights(place[0], 0, mine, other, weights, sem)
    p1 = natural(index, 0, 384)
    gains[...] = exact_nn(vec384[...], p1)
    xf = x[...].astype(F32)
    unit_in, inv_in = normalise(xf)
    normed = unit_in * gains[0:1, :] + gains[2:3, :]
    nb = normed.astype(BF16)
    pn = pool_rows(normed).astype(BF16)
    middle = mid_in[...]
    unit_mid, inv_mid = normalise(middle)
    nm = (unit_mid * gains[1:2, :] + gains[3:4, :]).astype(BF16)
    sel = matching(index, 4, 192, 0, 384)
    dyb = nt(dpassed[...], turn[...]).astype(BF16)
    dy = dyb.astype(F32)
    dy_sel = nt(sel, dyb).astype(BF16)
    nm_sel = nt(sel, nm).astype(BF16)
    nb_sel = nt(sel, nb).astype(BF16)
    pn_sel = nt(sel, pn).astype(BF16)
    part[...] = jnp.zeros_like(part)

    def put(r, lo, value):
        value = value.astype(BF16)
        for k in range(4):
            out = keep if k < 2 else send
            out[k % 2, r, :, lo : lo + 384] = value[48 * k : 48 * k + 48]

    dnm = jnp.zeros((PT, 384), F32)
    dhs = [
        (nn(dyb, weights[r, :, 768:1152]) * slope_in[r].astype(F32)).astype(BF16)
        for r in heads_ready(weights, sem)
    ]
    for r in range(4):
        dh = dhs[r]
        row = 8 + 2 * (r % 2)
        out = vec_keep if r < 2 else vec_send
        out[row : row + 1, :] = dbias_two[r : r + 1, :]
        out[row + 1 : row + 2, 0:384] = column_sum(dh.astype(F32))
        out[row + 1 : row + 2, 384:768] = jnp.zeros((1, 384), F32)
        put(r, 768, nn(dy_sel, act_in[r]))
        put(r, 384, nn(nm_sel, dh))
        dnm = dnm + nt(dh, weights[r, :, 384:768])
    dmid = dy + normalise_back(dnm, unit_mid, inv_mid, gains[1:2, :])
    dbr = dmid.astype(BF16)
    dbr_sel = nt(sel, dbr).astype(BF16)
    dnormed = jnp.zeros((PT, 384), F32)
    dpooled = jnp.zeros((PW, 384), F32)
    dmix = [nn(dbr, weights[r, :, 0:96]).astype(BF16) for r in range(4)]
    back = attend_back(
        [q_in[r] for r in range(4)], [k_in[r] for r in range(4)], [v_in[r] for r in range(4)], ok[...], fill[...], dmix
    )
    for r, (dq, dk, dv) in enumerate(back):
        part[r, 0, :, 0:96] = mix_in[r]
        part[r, 1, :, 96:192] = dq.astype(BF16)
        part[r, 2, 0:PW, 192:288] = (dk[0:PW] * 0.25).astype(BF16)
        part[r, 2, 0:PW, 288:384] = (dv[0:PW] * 0.25).astype(BF16)
    for r in range(4):
        w = weights[r, :, 0:384]
        first = nn(dbr_sel, part[r, 0]) + nn(nb_sel, part[r, 1]) + 4.0 * nn(pn_sel, part[r, 2, 0:PW, :])
        dnormed = dnormed + nt(part[r, 1, :, 0:256], w[:, 0:256])
        dpooled = dpooled + nt(part[r, 2, 0:PW, 128:384], w[:, 128:384])
        put(r, 0, first)
    dnormed = dnormed + jnp.concatenate([dpooled, dpooled, dpooled, dpooled], axis=0)
    dx = normalise_back(dnormed, unit_in, inv_in, gains[0:1, :]) + dmid
    vec = jnp.concatenate(
        [
            column_sum(dnormed * unit_in),
            column_sum(dnm * unit_mid),
            column_sum(dnormed),
            column_sum(dnm),
            column_sum(dmid),
            column_sum(dy),
            jnp.zeros((2, 384), F32),
        ],
        axis=0,
    )
    vec = exact_nt(vec, p1)
    for out in (vec_keep, vec_send):
        out[0:4, :] = vec_mid[0:4, :]
        for k in range(3):
            out[4 + k : 5 + k, 0:384] = vec[2 * k : 2 * k + 1, :]
            out[4 + k : 5 + k, 384:768] = vec[2 * k + 1 : 2 * k + 2, :]
        out[7:8, 0:384] = vec_in[0:1, :]
        out[7:8, 384:768] = vec_in[1:2, :]
    dxb = nt(dx.astype(BF16), p1).astype(BF16)
    xgrad[...] = nn(token_back[...], dxb).astype(BF16)


def local_shards(place, out_one, qkv_one, up_one, down_one, out_two, res_two, qkv_two, up_two, down_two, first, second):
    @pl.when(place[0] == 0)
    def _():
        first[:, 0:96] = out_one[...]
        first[:, 96:384] = qkv_one[0]
        first[:, 384:768] = up_one[...]
        first[:, 768:1152] = down_one[...]
        up = up_two[...].astype(F32)
        second[:, 0:768] = up[0:24].astype(BF16)
        second[:, 768:1536] = up[24:48].astype(BF16)

    @pl.when(place[0] != 0)
    def _():
        out_t, res_t = out_two[...].astype(F32), res_two[...].astype(F32)
        for s in range(2):
            first[:, 384 * s : 384 * s + 192] = out_t[24 * s : 24 * s + 24].astype(BF16)
            first[:, 384 * s + 192 : 384 * s + 288] = res_t[24 * s : 24 * s + 24].astype(BF16)
            first[:, 384 * s + 288 : 384 * s + 384] = qkv_two[:, s, 0:96]
            first[:, 768 + 192 * s : 960 + 192 * s] = qkv_two[:, s, 96:288]
        down = down_two[...].astype(F32)
        second[:, 0:768] = down[0:24].astype(BF16)
        second[:, 768:1536] = down[24:48].astype(BF16)


def feed_outputs(part, got, grad_up, grad_down):
    total = part[...] + got[...].astype(F32)
    grad_up[0:12, :] = total[:, 0:768]
    grad_up[12:24, :] = total[:, 1536:2304]
    grad_down[0:12, :] = total[:, 768:1536]
    grad_down[12:24, :] = total[:, 2304:3072]


def last_outputs(
    part, got, vec_part, vec_got,
    qkv1, out1, up1, down1, bias1, gains1, shifts1, qkv2, out2, res2, bias2, gain_in, shift_in, gain_mid, shifts2,
):
    total = part[...] + got[...].astype(F32)
    vec = vec_part[...] + vec_got[...]
    out1[...] = total[:, 0:96]
    qkv1[:, 0, :] = total[:, 96:384]
    up1[...] = total[:, 384:768]
    down1[...] = total[:, 768:1152]
    for s in range(2):
        at = 1152 + 384 * s
        out2[12 * s : 12 * s + 12, :] = total[:, at : at + 192]
        res2[12 * s : 12 * s + 12, :] = total[:, at + 192 : at + 288]
        qkv2[:, s, 0:96] = total[:, at + 288 : at + 384]
        qkv2[:, s, 96:288] = total[:, 1920 + 192 * s : 2112 + 192 * s]
    gain_mid[...] = vec[0]
    shifts2[...] = vec[1:4, :]
    gains1[0:1, :] = vec[4:5, 0:384]
    gains1[1:2, :] = vec[4:5, 384:768]
    for n in range(2):
        shifts1[2 * n : 2 * n + 1, :] = vec[5 + n : 6 + n, 0:384]
        shifts1[2 * n + 1 : 2 * n + 2, :] = vec[5 + n : 6 + n, 384:768]
    gain_in[...] = vec[7, 0:384]
    shift_in[...] = vec[7, 384:768]
    bias2[...] = vec[8]
    bias1[...] = vec[9, 0:384]


def spec_vmem():
    return pl.BlockSpec(memory_space=pltpu.VMEM)


def spec_any():
    return pl.BlockSpec(memory_space=pltpu.HBM)


def spec_smem():
    return pl.BlockSpec(memory_space=pltpu.SMEM)


def call(body, inputs, kinds, outs, scratch, micros):
    specs = {"v": spec_vmem, "a": spec_any, "s": spec_smem}
    return pl.pallas_call(
        body,
        out_shape=outs,
        in_specs=[specs[k]() for k in kinds],
        out_specs=jax.tree.map(lambda _: spec_vmem(), outs),
        scratch_shapes=scratch,
        compiler_params=pltpu.CompilerParams(vmem_limit_bytes=VMEM_LIMIT),
        cost_estimate=pl.CostEstimate(flops=micros * 1_000_000_000, bytes_accessed=4_000_000, transcendentals=0),
    )(*inputs)


def shape(dims, dtype):
    return jax.ShapeDtypeStruct(dims, dtype)


CUT_ONE = 512
CUT_TWO = 896
ORDER = ((0, 1, 3, 2), (0, 3, 1, 2))


def hop(v, axis, late):
    pairs = []
    for core in range(2):
        flip = 3 if (core == 1) != late else 1
        for xi in range(4):
            for zi in range(4):
                for yi in range(4):
                    tx, tz, ty = xi, zi, yi
                    if axis == "x":
                        tx = xi ^ flip
                    elif axis == "z":
                        tz = zi ^ flip
                    else:
                        ty = yi ^ flip
                    here = ((core * 4 + xi) * 4 + zi) * 4 + yi
                    pairs.append((here, ((core * 4 + tx) * 4 + tz) * 4 + ty))
    return lax.ppermute(v, ("pipe", "dp", "head"), pairs)


def swap(v):
    return lax.ppermute(v, "pipe", [(0, 1), (1, 0)])


def ring_pair(v, axis):
    low = jnp.stack([v, hop(v, axis, False)])
    return low, hop(low, axis, True)


def ring_rows(v, axis):
    low, high = ring_pair(v, axis)
    both = jnp.concatenate([low, high], axis=0)
    return jnp.moveaxis(both, 0, -3).reshape(v.shape[:-2] + (4 * v.shape[-2], v.shape[-1]))


def ring_stack(v, axis):
    low, high = ring_pair(v, axis)
    return jnp.concatenate([low, high], axis=0)


def gather_one(local):
    rows = ring_rows(local, "z")
    first = ring_rows(rows[:, :CUT_ONE], "x")
    last = ring_stack(rows[:, CUT_ONE:], "y")
    first_pair, last_pair = ring_pair(first, "y"), ring_pair(last, "x")
    return first_pair + last_pair, rows, (first, last), (first_pair[0], last_pair[0])


def gather_two(local, ready):
    rows = ring_rows(local, "x")
    first = ring_stack(rows[:, :CUT_TWO], "y")
    last = ring_rows(rows[:, CUT_TWO:], "z")
    first, last = after((first, last), ready)
    return ring_pair(first, "z") + ring_pair(last, "y")


def half_sums(keep, got):
    onward = (keep[1].astype(F32) + got[1].astype(F32)).astype(keep.dtype)
    return keep[0].astype(F32) + got[0].astype(F32), onward


def ring_begin(keep, send, axis):
    return half_sums(keep, hop(send, axis, True))


def ring_end(begun, axis):
    part, onward = begun
    return part + hop(onward, axis, False).astype(F32)


def ring_sum(keep, send, axis):
    return ring_end(ring_begin(keep, send, axis), axis)


def halves(v):
    rows = v.shape[-2] // 4
    parts = [v[..., rows * n : rows * n + rows, :] for n in range(4)]
    return jnp.stack(parts[:2]), jnp.stack(parts[2:])


def low(v):
    return v.astype(BF16)


def after(v, other):
    return lax.optimization_barrier((v, other))[0]


def lock(*values):
    return lax.optimization_barrier(values)


def send_clip(value, rounds):
    pairs = [(p * 4 + source, p * 4 + target) for p, source, target in rounds]
    return lax.ppermute(value, ("pipe", "head"), pairs)


def spread_near(v):
    return send_clip(v, [(0, 0, 1), (0, 1, 0), (1, 2, 3), (1, 3, 2)])


def spread_far(v, near, pipe, y):
    even = (y % 2) == 0
    both = jnp.stack([jnp.where(even, v, near), jnp.where(even, near, v)])
    far = send_clip(both, [(0, 0, 3), (0, 1, 2), (1, 2, 1), (1, 3, 0)])
    return jnp.where((y // 2) == pipe, both, far)[:, None]


def token_order():
    order = np.zeros((PT, TOK), np.float32)
    for block in range(4):
        for window in range(WIN):
            row = (window // 10) * 2 + block // 2
            col = (window % 10) * 2 + block % 2
            order[block * PW + window, row * GRID + col] = 1
    return order


def turn_matrix(core_from, core_to, rows_from, rows_to):
    def labels(core, outer):
        out = []
        for a in range(4):
            for b in range(4):
                one, two = ORDER[core][a], ORDER[core][b]
                out.append((one, two) if outer == "x" else (two, one))
        return out

    source, target = labels(core_from, rows_from), labels(core_to, rows_to)
    matrix = np.zeros((384, 384), np.float32)
    for n, label in enumerate(source):
        m = target.index(label)
        matrix[n * 24 : n * 24 + 24, m * 24 : m * 24 + 24] = np.eye(24)
    return jnp.asarray(matrix, BF16)


def per_device(
    clips_in, cotangent, token_mask, memory_valid, memory_one, memory_two,
    qkv_one, out_one, up_one, down_one, up_bias_one, gains_one, shifts_one,
    qkv_two, out_two, res_two, up_two, down_two, up_bias_two, gain_two_in, shift_two_in, gains_two, shifts_two,
):
    pipe = lax.axis_index("pipe")
    dp = lax.axis_index("dp")
    y = lax.axis_index("head")
    x_at, z_at = dp // 4, dp % 4
    first_core = pipe == 0

    place = pipe.astype(jnp.int32).reshape(1)
    shard_one, shard_two = call(
        local_shards,
        (
            place, out_one.T, jnp.transpose(qkv_one, (1, 0, 2)), up_one, down_one.T,
            out_two.T, res_two.T, qkv_two, up_two, down_two.T,
        ),
        "s" + "v" * 9,
        (shape((24, 1152), BF16), shape((24, 1536), BF16)),
        [],
        1,
    )
    mine_one, rows_ready, ready, late = gather_one(shard_one)
    mine_two = gather_two(shard_two, ready)
    other_one = tuple(swap(v) for v in mine_one)

    def clip_of(v, at):
        return lax.dynamic_index_in_dim(v, at, 0, keepdims=False)

    near = jnp.where(first_core, 1, 3)
    far = 4 - near
    biases = jnp.concatenate([up_bias_one, up_bias_two])
    biases = jnp.concatenate(thirds(biases)).reshape(12, 288)
    memory = jnp.concatenate([memory_one[:, 0], memory_two[:, 0]], axis=-1)

    memory, biases = after((memory, biases), rows_ready)

    def payload(flip):
        part = clip_of(memory, y ^ flip).reshape(2 * MEMROWS, 288)
        return jnp.concatenate([part, biases], axis=0)

    got = hop(jnp.stack([payload(near), payload(2)]), "y", False)
    more = hop(jnp.stack([payload(far), got[1]]), "y", True)
    parcels = jnp.stack([payload(0), got[0], more[0], more[1]])
    memory = parcels[:, : 2 * MEMROWS].reshape(4, 2, MEMROWS, 288)
    mem_one, mem_two = memory[..., :96], memory[..., 96:]
    biases = parcels[:, 2 * MEMROWS :].astype(F32).reshape(4, 3, 1152)
    biases = biases[:, 0] + biases[:, 1] + biases[:, 2]
    bias_one, bias_two = biases[:, :384], biases[:, 384:]

    pipe, y, x_at, z_at = after((pipe, y, x_at, z_at), late)
    first_core = pipe == 0

    flags = clip_of(token_mask[:, 0], y).reshape(10, 2, 10, 2)[:, 0, :, 0].reshape(WIN)
    key_ok = (flags > 0).astype(F32)
    mem_ok = jnp.repeat((clip_of(memory_valid[:, 0], y) > 0).astype(F32), MEMROWS // 2)
    gap = jnp.zeros((MEM0 - WIN,), F32)
    tail = jnp.zeros((KEYS - MEM0 - MEMROWS,), F32)
    ok = jnp.concatenate([key_ok, gap, mem_ok, tail]).reshape(1, KEYS)
    fill = np.full((1, KEYS), ABSENT, np.float32)
    fill[0, :WIN] = MASKED
    fill[0, MEM0 : MEM0 + MEMROWS] = MASKED
    fill = jnp.asarray(fill)
    key_col = jnp.concatenate([key_ok, jnp.zeros((PW - WIN,), F32)]).reshape(PW, 1)

    def order_of(core, n):
        return jnp.asarray(ORDER[core], jnp.int32)[n]

    def own_order(n):
        return jnp.where(first_core, order_of(0, n), order_of(1, n))

    k = np.arange(384)
    k_outer, k_inner, k_row = k // 96, (k // 24) % 4, k % 24

    def chip(a, b):
        return (x_at ^ a) * 4 + (z_at ^ b)

    piece0 = chip(order_of(0, k_outer), order_of(0, k_inner))
    piece1 = chip(order_of(1, k_outer), order_of(1, k_inner))
    raw0 = piece0 * 24 + k_row
    raw1 = piece1 * 24 + k_row
    raw2 = jnp.concatenate([piece1 * 48 + k_row, piece1 * 48 + 24 + k_row])
    head_raw = (y ^ own_order(k // 96)) * 96 + k % 96
    j = np.arange(192)
    j_outer, j_inner, j_row = own_order(j // 48), own_order((j // 12) % 4), j % 12
    rows_x = pipe * 192 + chip(j_outer, j_inner) * 12 + j_row
    rows_x2 = pipe * 384 + chip(j_outer, j_inner) * 24 + j_row
    rows_z2 = pipe * 384 + chip(j_inner, j_outer) * 24 + j_row
    pair = np.array([[0], [12]])
    rows_x2 = (rows_x2[None, :] + pair).reshape(384)
    rows_z2 = (rows_z2[None, :] + pair).reshape(384)
    index = [raw0, raw1, raw2, head_raw, rows_x, rows_x2, rows_z2, raw0]
    index = jnp.stack([jnp.pad(v, (0, 768 - v.shape[0])) for v in index]).astype(F32)
    turn = turn_matrix(0, 1, "x", "x")
    to_up = turn_matrix(1, 0, "x", "z")
    to_down = turn_matrix(1, 1, "x", "z")

    order = token_order()
    token_perm = jnp.asarray(order, BF16)
    token_back = jnp.asarray(order.T, BF16)
    vec384 = jnp.concatenate([gains_one, shifts_one, gain_two_in[None], shift_two_in[None]], axis=0)
    gains_in = jnp.concatenate([gain_two_in[None], jnp.zeros((7, 384), F32)], axis=0)
    vec768 = jnp.concatenate([gains_two[None], shifts_two, jnp.zeros((4, 768), F32)], axis=0)
    x = clip_of(clips_in[:, 0], y)
    cot = clip_of(cotangent[:, 0], y)

    x, key_col, vec768, gains_in, bias_two, cot, mem_two = lock(
        x, key_col, vec768, gains_in, bias_two, cot, mem_two
    )
    other_two = tuple(swap(v) for v in mine_two)

    dma = pltpu.SemaphoreType.DMA
    saved = call(
        forward,
        (
            place, x, token_perm, index, turn, vec384, ok, fill, mem_one, mem_two, bias_one,
            *mine_one, *other_one,
        ),
        "s" + "v" * 10 + "a" * 8,
        (
            shape((PT, 384), BF16), shape((PT, 384), BF16),
            shape((4, PT, HEAD), BF16), shape((4, KEYS, HEAD), BF16), shape((4, KEYS, HEAD), BF16),
            shape((4, PT, HEAD), BF16), shape((PT, 384), F32),
            shape((4, PT, 384), BF16), shape((4, PT, 384), BF16),
            shape((PW, 384), BF16), shape((8, PW, HEAD), BF16), shape((8, KEYS, HEAD), BF16),
            shape((8, KEYS, HEAD), BF16), shape((4, PW, 384), BF16), shape((PW, 768), F32),
        ),
        [
            pltpu.VMEM((4, 384, 1152), BF16), pltpu.VMEM((4, 384, 1152), BF16), pltpu.VMEM((8, 384), F32),
            dma((4,)), dma((4,)),
        ],
        18,
    )
    passed, x_kept, q1, k1, v1, mix1, mid1, act1, slope1, pn2, q2k, k2, v2, mix2, mid2 = saved

    feed = call(
        feed_two,
        (place, mid2, cot, key_col, index, to_up, to_down, vec768, bias_two, *mine_two, *other_two),
        "s" + "v" * 8 + "a" * 8,
        (
            shape((WIN, 768), BF16), shape((PW, 768), F32), shape((8, 768), F32), shape((4, 768), F32),
            shape((2, 4, 48, 1536), BF16), shape((2, 4, 48, 1536), BF16),
            shape((2, 192, 1536), BF16), shape((2, 192, 1536), BF16),
        ),
        [
            pltpu.VMEM((4, 384, 1536), BF16), pltpu.VMEM((4, 384, 1536), BF16),
            pltpu.VMEM((4, PW, 768), BF16), pltpu.VMEM((4, PW, 768), F32), dma((4,)), dma((4,)),
        ],
        14,
    )
    activation, dmid2, vec_mid, dbias_two, keep_rows, send_rows, keep_y, send_y = feed
    got_a = hop(send_rows, "z", True)
    got_b = hop(send_y, "y", True)

    second = call(
        second_backward,
        (
            place, dmid2, passed, pn2, q2k, k2, v2, mix2, index, gains_in, ok, fill,
            *mine_one, *other_one,
        ),
        "s" + "v" * 11 + "a" * 8,
        (
            shape((PT, 384), BF16), shape((8, 384), F32),
            shape((2, 192, 1152), BF16), shape((2, 192, 1152), BF16),
        ),
        [pltpu.VMEM((4, 384, 1152), BF16), pltpu.VMEM((4, 3, PW, 384), BF16), dma((4,))],
        1,
    )
    dpassed, vec_in, keep_attn, send_attn = second
    attn_got = hop(send_attn, "y", True)

    third = call(
        first_backward,
        (
            place, dpassed, x_kept, q1, k1, v1, mix1, mid1, act1, slope1,
            token_back, index, turn, vec384, ok, fill, vec_mid, vec_in, dbias_two, *mine_one, *other_one,
        ),
        "s" + "v" * 18 + "a" * 8,
        (
            shape((TOK, 384), BF16), shape((12, 768), F32), shape((12, 768), F32),
            shape((2, 4, 48, 1152), BF16), shape((2, 4, 48, 1152), BF16),
        ),
        [
            pltpu.VMEM((4, 384, 1152), BF16), pltpu.VMEM((8, 384), F32), pltpu.VMEM((4, 3, PT, 384), BF16), dma((4,)),
        ],
        1,
    )
    third, got_a, got_b, attn_got, activation = lock(third, got_a, got_b, attn_got, activation)
    xgrad, vec_keep, vec_send, keep_one, send_one = third

    vectors = vec_keep + hop(vec_send, "y", True)
    act_near = spread_near(activation)
    one_sum = ring_begin(keep_one, send_one, "x")
    feed_a = low(ring_end(half_sums(keep_rows, got_a), "z"))
    feed_b = low(ring_end(half_sums(keep_y, got_b), "y"))
    attn_sum = half_sums(keep_attn, attn_got)
    vectors, attn_sum, one_sum, feed_a, feed_b, xgrad, act_near = lock(
        vectors, attn_sum, one_sum, feed_a, feed_b, xgrad, act_near
    )

    vectors = vectors[:10] + hop(jnp.concatenate([vectors[:8], vectors[10:]], axis=0), "y", False)
    feed_a = ring_begin(feed_a[0:2], feed_a[2:4], "y")
    feed_b = ring_begin(*halves(feed_b), "z")
    attn_sum = low(ring_end(attn_sum, "y"))
    one_sum = low(ring_end(one_sum, "x"))
    vectors, feed_a, feed_b, attn_sum, one_sum, xgrad, act_near = lock(
        vectors, feed_a, feed_b, attn_sum, one_sum, xgrad, act_near
    )

    vectors = vectors + hop(vectors, "x", True)
    feed_a = low(ring_end(feed_a, "y"))
    feed_b = low(ring_end(feed_b, "z"))
    attn_sum = ring_begin(*halves(attn_sum), "x")
    one_sum = ring_begin(one_sum[0:2], one_sum[2:4], "y")
    grad_near = spread_near(xgrad)
    vectors, feed_a, feed_b, attn_sum, one_sum, grad_near, act_near = lock(
        vectors, feed_a, feed_b, attn_sum, one_sum, grad_near, act_near
    )

    vectors = vectors + hop(vectors, "x", False)
    feed_sum = ring_begin(*halves(jnp.concatenate([feed_a, feed_b], axis=1)), "x")
    attn_sum = low(ring_end(attn_sum, "x"))
    one_sum = low(ring_end(one_sum, "y"))
    input_grad = spread_far(xgrad, grad_near, pipe, y)
    vectors, feed_sum, attn_sum, one_sum, act_near = lock(vectors, feed_sum, attn_sum, one_sum, act_near)

    feed_part, feed_onward = feed_sum
    feed_got = hop(feed_onward, "x", False)
    activations = spread_far(activation, act_near, pipe, y)
    vectors = vectors + hop(vectors, "z", True)
    rest_sum = ring_begin(*halves(jnp.concatenate([one_sum, attn_sum], axis=1)), "z")
    vectors, rest_sum, input_grad, feed_got = lock(vectors, rest_sum, input_grad, feed_got)
    grad_up_two, grad_down_two = call(
        feed_outputs,
        (feed_part, feed_got),
        "vv",
        (shape((24, 768), F32), shape((24, 768), F32)),
        [],
        2,
    )

    rest_part, rest_onward = rest_sum
    vectors_got = hop(vectors, "z", False)
    rest_got = hop(rest_onward, "z", False)
    outs = call(
        last_outputs,
        (rest_part, rest_got, vectors, vectors_got),
        "vvvv",
        (
            shape((12, 1, 288), F32), shape((12, 96), F32), shape((12, 384), F32), shape((12, 384), F32),
            shape((384,), F32), shape((2, 384), F32), shape((4, 384), F32),
            shape((12, 2, 288), F32), shape((24, 192), F32), shape((24, 96), F32),
            shape((768,), F32), shape((384,), F32), shape((384,), F32), shape((768,), F32),
            shape((3, 768), F32),
        ),
        [],
        2,
    )
    return (
        activations,
        input_grad,
        outs[0],
        outs[1].T,
        outs[2],
        outs[3].T,
        *outs[4:8],
        outs[8].T,
        outs[9].T,
        grad_up_two,
        grad_down_two.T,
        *outs[10:15],
    )


def solution(mesh):
    return jax.shard_map(
        per_device,
        mesh=mesh,
        in_specs=(
            P(None, "dp", None, None), P(None, "dp", None, None), P(None, "dp", None), P(None, "dp", None),
            P(None, "dp", None, None, "head"), P(None, "dp", None, None, "head"),
            P("dp", "head", None), P("head", "dp"), P("dp", "head"), P("head", "dp"), P("head"), P(), P(),
            P("dp", "head", None), P("head", "dp"), P("head", "dp"), P("dp", "head"), P("head", "dp"), P("head"),
            P(), P(), P(), P(),
        ),
        out_specs=(
            P("pipe", "dp", None, None), P("pipe", "dp", None, None),
            P(("pipe", "dp"), "head", None), P("head", ("pipe", "dp")), P(("pipe", "dp"), "head"),
            P("head", ("pipe", "dp")), P("head"), P(), P(),
            P(("pipe", "dp"), "head", None), P("head", ("pipe", "dp")), P("head", ("pipe", "dp")),
            P(("pipe", "dp"), "head"), P("head", ("pipe", "dp")), P("head"), P(), P(), P(), P(),
        ),
        check_vma=False,
    )
```

```python
import functools

import jax
import jax.numpy as jnp
import numpy as np
from jax import lax
from jax.experimental import pallas as pl
from jax.experimental.pallas import tpu as pltpu
from jax.sharding import PartitionSpec as P

F32 = jnp.float32
BF16 = jnp.bfloat16
GRID = 20
TOK = 400
WIN = 100
PW = 104
PT = 4 * PW
KEYS = 256
MEM0 = 112
MEMROWS = 50
HEAD = 96
EPS = 1e-06
MASKED = -1000000000.0
ABSENT = -3e38
SCALE = HEAD ** (-0.5)
VMEM_LIMIT = 56 * 1024 * 1024


def nn(a, b):
    return lax.dot_general(a, b, (((1,), (0,)), ((), ())), preferred_element_type=F32)


def nt(a, b):
    return lax.dot_general(a, b, (((1,), (1,)), ((), ())), preferred_element_type=F32)


def tn(a, b):
    return lax.dot_general(a, b, (((0,), (0,)), ((), ())), preferred_element_type=F32)


def thirds(v):
    high = v.astype(BF16)
    rest = v - high.astype(F32)
    mid = rest.astype(BF16)
    low = (rest - mid.astype(F32)).astype(BF16)
    return high, mid, low


def exact_nn(v, m):
    a, b, c = thirds(v)
    return nn(a, m) + nn(b, m) + nn(c, m)


def exact_nt(v, m):
    a, b, c = thirds(v)
    return nt(a, m) + nt(b, m) + nt(c, m)


def normalise(v):
    average = jnp.mean(v, axis=-1, keepdims=True)
    centred = v - average
    variance = jnp.mean(centred * centred, axis=-1, keepdims=True)
    inverse = lax.rsqrt(variance + EPS)
    return centred * inverse, inverse


def normalise_back(grad, unit, inverse, gain):
    scaled = grad * gain
    mean_one = jnp.mean(scaled, axis=-1, keepdims=True)
    mean_two = jnp.mean(scaled * unit, axis=-1, keepdims=True)
    return inverse * (scaled - mean_one - unit * mean_two)


def column_sum(v):
    return jnp.sum(v, axis=0, keepdims=True)


def gelu_both(h):
    cdf = 0.5 + 0.5 * lax.erf(h * 0.7071067811865476)
    density = 0.3989422804014327 * jnp.exp(-0.5 * h * h)
    return h * cdf, cdf + h * density


def pool_rows(v):
    return 0.25 * (v[0:PW] + v[PW : 2 * PW] + v[2 * PW : 3 * PW] + v[3 * PW : 4 * PW])


def softmax_rows(scores, ok, fill):
    scores = jnp.where(ok > 0, scores * SCALE, fill)
    peak = jnp.max(scores, axis=-1, keepdims=True)
    expos = jnp.exp(scores - peak)
    return expos / jnp.sum(expos, axis=-1, keepdims=True)


def attend_back(q, keys, values, ok, fill, dmix):
    n = range(len(q))
    scores = [nt(q[i], keys[i]) for i in n]
    dshares = [nt(dmix[i], values[i]) for i in n]
    shares = [softmax_rows(v, ok, fill) for v in scores]
    dvalues = [tn(shares[i].astype(BF16), dmix[i]) for i in n]
    inner = [jnp.sum(shares[i] * dshares[i], axis=-1, keepdims=True) for i in n]
    dscores = [(shares[i] * (dshares[i] - inner[i])).astype(BF16) for i in n]
    dq = [nn(dscores[i], keys[i]) * SCALE + dmix[i].astype(F32) for i in n]
    dkeys = [tn(dscores[i], q[i]) * SCALE for i in n]
    return [(dq[i], dkeys[i], dvalues[i]) for i in n]


def index_row(index, row, size):
    return index[row : row + 1, 0:size]


def index_col(index, row, size):
    return jnp.broadcast_to(index[row : row + 1, 0:size], (8, size)).T[:, 0:1]


def natural(index, row, size):
    values = lax.broadcasted_iota(jnp.int32, (size, size), 0).astype(F32)
    return (values == index_row(index, row, size)).astype(F32).astype(BF16)


def matching(index, row, rows, col, cols):
    return (index_col(index, row, rows) == index_row(index, col, cols)).astype(F32).astype(BF16)


def close_nt(v, m):
    high = v.astype(BF16)
    return nt(high, m) + nt((v - high.astype(F32)).astype(BF16), m)


def load_weights(core, owner, mine, other, dst, sem):
    def copies(groups, places):
        at = 0
        for kind, low, high in groups:
            cols = pl.ds(at, low.shape[-1])
            at += low.shape[-1]
            for n in range(4):
                slab = (low if n < 2 else high).at[n % 2]
                if kind == "y":
                    pltpu.make_async_copy(slab, dst.at[places[n], :, cols], sem).start()
                else:
                    for h in range(4):
                        pltpu.make_async_copy(slab.at[h], dst.at[places[h], pl.ds(96 * n, 96), cols], sem).start()

    @pl.when(core == owner)
    def _():
        copies(mine, (0, 1, 2, 3))

    @pl.when(core != owner)
    def _():
        copies(other, (0, 2, 1, 3))


def wait_weights(dst, sem):
    pltpu.make_async_copy(dst, dst, sem).wait()


def groups_one(refs):
    return [("y", refs[0], refs[1]), ("rows", refs[2], refs[3])]


def groups_two(refs):
    return [("rows", refs[0], refs[1]), ("y", refs[2], refs[3])]


def forward(
    place, x, token_perm, index, turn, vec384, ok, fill, mem_one, mem_two, bias_up, *rest
):
    mine, other = groups_one(rest[0:4]), groups_one(rest[4:8])
    (passed, x_out, q_out, k_out, v_out, mix_out, mid_out, act_out, slope_out,
     pn_out, q2_out, k2_out, v2_out, mix2_out, mid2_out) = rest[8:23]
    w1, wa, gains, sem_one, sem_attn = rest[23:28]
    load_weights(place[0], 0, mine, other, w1, sem_one)
    load_weights(place[0], 1, mine, other, wa, sem_attn)
    p1 = natural(index, 0, 384)
    pr = matching(index, 1, 384, 3, 384)
    gains[...] = exact_nn(vec384[...], p1)
    xb = nn(x[...], p1).astype(BF16)
    xb = nn(token_perm[...], xb).astype(BF16)
    x_out[...] = xb
    xf = xb.astype(F32)
    unit, _ = normalise(xf)
    normed = unit * gains[0:1, :] + gains[2:3, :]
    nb = normed.astype(BF16)
    pn = pool_rows(normed).astype(BF16)
    k_out[...] = jnp.zeros_like(k_out)
    v_out[...] = jnp.zeros_like(v_out)
    k2_out[...] = jnp.zeros_like(k2_out)
    v2_out[...] = jnp.zeros_like(v2_out)
    mix2_out[...] = jnp.zeros_like(mix2_out)
    wait_weights(w1, sem_one)
    for r in range(4):
        w = w1[r, :, 0:384]
        q_out[r] = nn(nb, w[:, 0:256])[:, 96:192].astype(BF16)
        kv = nn(pn, w)
        k_out[r, 0:PW, :] = kv[:, 192:288].astype(BF16)
        v_out[r, 0:PW, :] = kv[:, 288:384].astype(BF16)
        k_out[r, MEM0 : MEM0 + MEMROWS, :] = mem_one[r, 0]
        v_out[r, MEM0 : MEM0 + MEMROWS, :] = mem_one[r, 1]
    scores = [nt(q_out[r], k_out[r]) for r in range(4)]
    shares = [softmax_rows(v, ok[...], fill[...]).astype(BF16) for v in scores]
    branch = jnp.zeros((PT, 384), F32)
    for r in range(4):
        mixed = (nn(shares[r], v_out[r]) + q_out[r].astype(F32)).astype(BF16)
        mix_out[r] = mixed
        branch = branch + nt(mixed, w1[r, :, 0:96])
    middle = xf + gains[4:5, :] + branch
    mid_out[...] = middle
    unit, _ = normalise(middle)
    nm = (unit * gains[1:2, :] + gains[3:4, :]).astype(BF16)
    total = middle + gains[5:6, :]
    for r in range(4):
        hidden = nn(nm, w1[r, :, 384:768]) + bias_up[r : r + 1, :]
        active, slope = gelu_both(hidden)
        active = active.astype(BF16)
        act_out[r] = active
        slope_out[r] = slope.astype(BF16)
    for r in range(4):
        total = total + nt(act_out[r], w1[r, :, 768:1152])
    xb = nn(total.astype(BF16), turn[...]).astype(BF16)
    passed[...] = xb

    xf = xb.astype(F32)
    gains[...] = exact_nn(gains[...], turn[...])
    unit, _ = normalise(xf)
    normed = unit * gains[6:7, :] + gains[7:8, :]
    pn = pool_rows(normed).astype(BF16)
    pn_out[...] = pn
    pnr = nn(pn, pr).astype(BF16)
    wait_weights(wa, sem_attn)
    branch = [jnp.zeros((PW, 384), F32), jnp.zeros((PW, 384), F32)]
    for r in range(4):
        kv = nn(pn, wa[r, :, 768:1152])
        mix2_out[r, :, 192:288] = pnr[:, r * 96 : (r + 1) * 96]
        for h in range(2):
            q = nn(pn, wa[r, :, 384 * h + 256 : 384 * h + 384])[:, 32:128].astype(BF16)
            n = 2 * r + h
            q2_out[n] = q
            k2_out[n, 0:PW, :] = kv[:, 192 * h : 192 * h + 96].astype(BF16)
            v2_out[n, 0:PW, :] = kv[:, 192 * h + 96 : 192 * h + 192].astype(BF16)
            k2_out[n, MEM0 : MEM0 + MEMROWS, :] = mem_two[r, 0, :, 96 * h : 96 * h + 96]
            v2_out[n, MEM0 : MEM0 + MEMROWS, :] = mem_two[r, 1, :, 96 * h : 96 * h + 96]
    scores = [nt(q2_out[n], k2_out[n]) for n in range(8)]
    shares = [softmax_rows(v, ok[...], fill[...]).astype(BF16) for v in scores]
    mixed = [nn(shares[n], v2_out[n]) + q2_out[n].astype(F32) for n in range(8)]
    for r in range(4):
        for h in range(2):
            mix2_out[r, :, 96 * h : 96 * h + 96] = mixed[2 * r + h].astype(BF16)
        for s in range(2):
            branch[s] = branch[s] + nt(mix2_out[r], wa[r, :, 384 * s : 384 * s + 384])
    mid2_out[...] = jnp.concatenate(branch, axis=1)


def feed_two(place, middle_in, cot, key_ok, index, to_up, to_down, vec768, bias_up, *rest):
    mine, other = groups_two(rest[0:4]), groups_two(rest[4:8])
    act_out, dmid_out, vec_out, bias_out, keep_rows, send_rows, keep_y, send_y = rest[8:16]
    wu, wd, acts, slopes, sem_u, sem_d = rest[16:22]
    load_weights(place[0], 0, mine, other, wu, sem_u)
    load_weights(place[0], 1, mine, other, wd, sem_d)
    p2 = natural(index, 2, 768)
    s2f = matching(index, 6, 384, 2, 768)
    gains2 = exact_nn(vec768[...], p2)
    middle = middle_in[...] + gains2[2:3, :]
    unit, inverse = normalise(middle)
    nm = (unit * gains2[0:1, :] + gains2[1:2, :]).astype(BF16)
    nm_up = [nn(nm[:, 384 * s : 384 * s + 384], to_up[...]).astype(BF16) for s in range(2)]
    dyb = nn(cot[...], p2).astype(BF16)
    dyb = jnp.concatenate([dyb, jnp.zeros((PW - WIN, 768), BF16)], axis=0)
    dy = dyb.astype(F32) * key_ok[...]
    dyb = dy.astype(BF16)
    dy_down = [nn(dyb[:, 384 * s : 384 * s + 384], to_down[...]).astype(BF16) for s in range(2)]
    dy_sel = nt(s2f, dyb).astype(BF16)
    nm_sel = nt(s2f, nm).astype(BF16)
    wait_weights(wu, sem_u)
    for r in range(4):
        hidden = nn(nm_up[0], wu[r, :, 0:768]) + nn(nm_up[1], wu[r, :, 768:1536])
        active, slope = gelu_both(hidden + bias_up[r : r + 1, :])
        acts[r] = active.astype(BF16)
        slopes[r] = slope
    wait_weights(wd, sem_d)

    def put_rows(r, lo, value):
        value = value.astype(BF16)
        for k in range(4):
            out = keep_rows if k < 2 else send_rows
            out[k % 2, r, :, lo : lo + 768] = value[48 * k : 48 * k + 48]

    def put_head(r, lo, value):
        out = keep_y if r < 2 else send_y
        out[r % 2, :, lo : lo + 768] = value.astype(BF16)

    down = [jnp.zeros((PW, 384), F32), jnp.zeros((PW, 384), F32)]
    dnm = [jnp.zeros((PW, 384), F32), jnp.zeros((PW, 384), F32)]
    dhs = [
        ((nn(dy_down[0], wd[r, :, 0:768]) + nn(dy_down[1], wd[r, :, 768:1536])) * slopes[r]).astype(BF16)
        for r in range(4)
    ]
    for r in range(4):
        active, dh = acts[r], dhs[r]
        bias_out[r : r + 1, :] = column_sum(dh.astype(F32))
        put_rows(r, 0, nn(nm_sel[0:192], dh))
        put_rows(r, 768, nn(dy_sel[0:192], active))
        put_head(r, 0, nn(nm_sel[192:384], dh))
        put_head(r, 768, nn(dy_sel[192:384], active))
        for s in range(2):
            down[s] = down[s] + nt(active, wd[r, :, 768 * s : 768 * s + 768])
            dnm[s] = dnm[s] + nt(dh, wu[r, :, 768 * s : 768 * s + 768])
    down = jnp.concatenate([close_nt(v, to_down[...]) for v in down], axis=1)
    output = (middle + gains2[3:4, :] + down).astype(BF16)
    act_out[...] = nt(output, p2)[0:WIN].astype(BF16)
    dnm = jnp.concatenate([close_nt(v, to_up[...]) for v in dnm], axis=1)
    dmid = dy + normalise_back(dnm, unit, inverse, gains2[0:1, :])
    dmid_out[...] = dmid
    vec = jnp.concatenate(
        [
            column_sum(dnm * unit),
            column_sum(dnm),
            column_sum(dmid),
            column_sum(dy),
            jnp.zeros((4, 768), F32),
        ],
        axis=0,
    )
    vec_out[...] = exact_nt(vec, p2)


def second_backward(
    place, dmid, passed, pn_in, queries, keys, values, mixes, index, gains_in, ok, fill, *rest
):
    mine, other = groups_one(rest[0:4]), groups_one(rest[4:8])
    dpassed, vec_out, keep, send = rest[8:12]
    wa, part, sem = rest[12:15]
    load_weights(place[0], 1, mine, other, wa, sem)
    xf = passed[...].astype(F32)
    unit, inverse = normalise(xf)
    pn = pn_in[...]
    dbr = dmid[...].astype(BF16)
    p1 = natural(index, 1, 384)
    pr = matching(index, 1, 384, 3, 384)
    s1 = matching(index, 4, 192, 1, 384)
    s2 = matching(index, 5, 384, 2, 768)
    dbr_sel = nt(s2, dbr).astype(BF16)
    pn_sel = nt(s1, pn).astype(BF16)
    dpooled = jnp.zeros((PW, 384), F32)
    part[...] = jnp.zeros_like(part)
    wait_weights(wa, sem)

    def put(r, lo, value):
        out = keep if r < 2 else send
        out[r % 2, :, lo : lo + 384] = value.astype(BF16)

    dmm = [nn(dbr[:, 0:384], wa[r, :, 0:384]) + nn(dbr[:, 384:768], wa[r, :, 384:768]) for r in range(4)]
    dres = [v[:, 192:288] for v in dmm]
    dmix = [dmm[n // 2][:, 96 * (n % 2) : 96 * (n % 2) + 96].astype(BF16) for n in range(8)]
    back = attend_back(
        [queries[n] for n in range(8)], [keys[n] for n in range(8)], [values[n] for n in range(8)],
        ok[...], fill[...], dmix,
    )
    for n, (dq, dk, dv) in enumerate(back):
        r, h = n // 2, n % 2
        part[r, h, :, 288:384] = dq.astype(BF16)
        part[r, 2, :, 192 * h : 192 * h + 96] = dk[0:PW].astype(BF16)
        part[r, 2, :, 192 * h + 96 : 192 * h + 192] = dv[0:PW].astype(BF16)
    for r in range(4):
        for s in range(2):
            put(r, 384 * s, nn(dbr_sel[192 * s : 192 * s + 192], mixes[r]) + nn(pn_sel, part[r, s]))
            dpooled = dpooled + nt(part[r, s], wa[r, :, 384 * s : 384 * s + 384])
        put(r, 768, nn(pn_sel, part[r, 2]))
        dpooled = dpooled + nt(part[r, 2], wa[r, :, 768:1152])
    dpooled = dpooled + close_nt(jnp.concatenate(dres, axis=1), pr)
    dpooled = dpooled * 0.25
    dnormed = jnp.concatenate([dpooled, dpooled, dpooled, dpooled], axis=0)
    gain = exact_nn(gains_in[...], p1)[0:1]
    dpassed[...] = normalise_back(dnormed, unit, inverse, gain).astype(BF16)
    vec = jnp.concatenate(
        [column_sum(dnormed * unit), column_sum(dnormed), jnp.zeros((6, 384), F32)], axis=0
    )
    vec_out[...] = exact_nt(vec, p1)


def first_backward(
    place, dpassed, x, q_in, k_in, v_in, mix_in, mid_in, act_in, slope_in,
    token_back, index, turn, vec384, ok, fill, vec_mid, vec_in, dbias_two, *rest
):
    mine, other = groups_one(rest[0:4]), groups_one(rest[4:8])
    xgrad, vec_keep, vec_send, keep, send = rest[8:13]
    weights, gains, part, sem = rest[13:17]
    load_weights(place[0], 0, mine, other, weights, sem)
    p1 = natural(index, 0, 384)
    gains[...] = exact_nn(vec384[...], p1)
    xf = x[...].astype(F32)
    unit_in, inv_in = normalise(xf)
    normed = unit_in * gains[0:1, :] + gains[2:3, :]
    nb = normed.astype(BF16)
    pn = pool_rows(normed).astype(BF16)
    middle = mid_in[...]
    unit_mid, inv_mid = normalise(middle)
    nm = (unit_mid * gains[1:2, :] + gains[3:4, :]).astype(BF16)
    sel = matching(index, 4, 192, 0, 384)
    dyb = nt(dpassed[...], turn[...]).astype(BF16)
    dy = dyb.astype(F32)
    dy_sel = nt(sel, dyb).astype(BF16)
    nm_sel = nt(sel, nm).astype(BF16)
    nb_sel = nt(sel, nb).astype(BF16)
    pn_sel = nt(sel, pn).astype(BF16)
    part[...] = jnp.zeros_like(part)
    wait_weights(weights, sem)

    def put(r, lo, value):
        value = value.astype(BF16)
        for k in range(4):
            out = keep if k < 2 else send
            out[k % 2, r, :, lo : lo + 384] = value[48 * k : 48 * k + 48]

    dnm = jnp.zeros((PT, 384), F32)
    dhs = [
        (nn(dyb, weights[r, :, 768:1152]) * slope_in[r].astype(F32)).astype(BF16) for r in range(4)
    ]
    for r in range(4):
        dh = dhs[r]
        row = 8 + 2 * (r % 2)
        out = vec_keep if r < 2 else vec_send
        out[row : row + 1, :] = dbias_two[r : r + 1, :]
        out[row + 1 : row + 2, 0:384] = column_sum(dh.astype(F32))
        out[row + 1 : row + 2, 384:768] = jnp.zeros((1, 384), F32)
        put(r, 768, nn(dy_sel, act_in[r]))
        put(r, 384, nn(nm_sel, dh))
        dnm = dnm + nt(dh, weights[r, :, 384:768])
    dmid = dy + normalise_back(dnm, unit_mid, inv_mid, gains[1:2, :])
    dbr = dmid.astype(BF16)
    dbr_sel = nt(sel, dbr).astype(BF16)
    dnormed = jnp.zeros((PT, 384), F32)
    dpooled = jnp.zeros((PW, 384), F32)
    dmix = [nn(dbr, weights[r, :, 0:96]).astype(BF16) for r in range(4)]
    back = attend_back(
        [q_in[r] for r in range(4)], [k_in[r] for r in range(4)], [v_in[r] for r in range(4)], ok[...], fill[...], dmix
    )
    for r, (dq, dk, dv) in enumerate(back):
        part[r, 0, :, 0:96] = mix_in[r]
        part[r, 1, :, 96:192] = dq.astype(BF16)
        part[r, 2, 0:PW, 192:288] = (dk[0:PW] * 0.25).astype(BF16)
        part[r, 2, 0:PW, 288:384] = (dv[0:PW] * 0.25).astype(BF16)
    for r in range(4):
        w = weights[r, :, 0:384]
        first = nn(dbr_sel, part[r, 0]) + nn(nb_sel, part[r, 1]) + 4.0 * nn(pn_sel, part[r, 2, 0:PW, :])
        dnormed = dnormed + nt(part[r, 1, :, 0:256], w[:, 0:256])
        dpooled = dpooled + nt(part[r, 2, 0:PW, 128:384], w[:, 128:384])
        put(r, 0, first)
    dnormed = dnormed + jnp.concatenate([dpooled, dpooled, dpooled, dpooled], axis=0)
    dx = normalise_back(dnormed, unit_in, inv_in, gains[0:1, :]) + dmid
    vec = jnp.concatenate(
        [
            column_sum(dnormed * unit_in),
            column_sum(dnm * unit_mid),
            column_sum(dnormed),
            column_sum(dnm),
            column_sum(dmid),
            column_sum(dy),
            jnp.zeros((2, 384), F32),
        ],
        axis=0,
    )
    vec = exact_nt(vec, p1)
    for out in (vec_keep, vec_send):
        out[0:4, :] = vec_mid[0:4, :]
        for k in range(3):
            out[4 + k : 5 + k, 0:384] = vec[2 * k : 2 * k + 1, :]
            out[4 + k : 5 + k, 384:768] = vec[2 * k + 1 : 2 * k + 2, :]
        out[7:8, 0:384] = vec_in[0:1, :]
        out[7:8, 384:768] = vec_in[1:2, :]
    dxb = nt(dx.astype(BF16), p1).astype(BF16)
    xgrad[...] = nn(token_back[...], dxb).astype(BF16)


def local_shards(place, out_one, qkv_one, up_one, down_one, out_two, res_two, qkv_two, up_two, down_two, first, second):
    @pl.when(place[0] == 0)
    def _():
        first[:, 0:96] = out_one[...]
        first[:, 96:384] = qkv_one[0]
        first[:, 384:768] = up_one[...]
        first[:, 768:1152] = down_one[...]
        up = up_two[...].astype(F32)
        second[:, 0:768] = up[0:24].astype(BF16)
        second[:, 768:1536] = up[24:48].astype(BF16)

    @pl.when(place[0] != 0)
    def _():
        out_t, res_t = out_two[...].astype(F32), res_two[...].astype(F32)
        for s in range(2):
            first[:, 384 * s : 384 * s + 192] = out_t[24 * s : 24 * s + 24].astype(BF16)
            first[:, 384 * s + 192 : 384 * s + 288] = res_t[24 * s : 24 * s + 24].astype(BF16)
            first[:, 384 * s + 288 : 384 * s + 384] = qkv_two[:, s, 0:96]
            first[:, 768 + 192 * s : 960 + 192 * s] = qkv_two[:, s, 96:288]
        down = down_two[...].astype(F32)
        second[:, 0:768] = down[0:24].astype(BF16)
        second[:, 768:1536] = down[24:48].astype(BF16)


def feed_outputs(part, got, grad_up, grad_down):
    total = part[...] + got[...].astype(F32)
    grad_up[0:12, :] = total[:, 0:768]
    grad_up[12:24, :] = total[:, 1536:2304]
    grad_down[0:12, :] = total[:, 768:1536]
    grad_down[12:24, :] = total[:, 2304:3072]


def last_outputs(
    part, got, vec_part, vec_got,
    qkv1, out1, up1, down1, bias1, gains1, shifts1, qkv2, out2, res2, bias2, gain_in, shift_in, gain_mid, shifts2,
):
    total = part[...] + got[...].astype(F32)
    vec = vec_part[...] + vec_got[...]
    out1[...] = total[:, 0:96]
    qkv1[:, 0, :] = total[:, 96:384]
    up1[...] = total[:, 384:768]
    down1[...] = total[:, 768:1152]
    for s in range(2):
        at = 1152 + 384 * s
        out2[12 * s : 12 * s + 12, :] = total[:, at : at + 192]
        res2[12 * s : 12 * s + 12, :] = total[:, at + 192 : at + 288]
        qkv2[:, s, 0:96] = total[:, at + 288 : at + 384]
        qkv2[:, s, 96:288] = total[:, 1920 + 192 * s : 2112 + 192 * s]
    gain_mid[...] = vec[0]
    shifts2[...] = vec[1:4, :]
    gains1[0:1, :] = vec[4:5, 0:384]
    gains1[1:2, :] = vec[4:5, 384:768]
    for n in range(2):
        shifts1[2 * n : 2 * n + 1, :] = vec[5 + n : 6 + n, 0:384]
        shifts1[2 * n + 1 : 2 * n + 2, :] = vec[5 + n : 6 + n, 384:768]
    gain_in[...] = vec[7, 0:384]
    shift_in[...] = vec[7, 384:768]
    bias2[...] = vec[8]
    bias1[...] = vec[9, 0:384]


def spec_vmem():
    return pl.BlockSpec(memory_space=pltpu.VMEM)


def spec_any():
    return pl.BlockSpec(memory_space=pltpu.HBM)


def spec_smem():
    return pl.BlockSpec(memory_space=pltpu.SMEM)


def call(body, inputs, kinds, outs, scratch, micros):
    specs = {"v": spec_vmem, "a": spec_any, "s": spec_smem}
    return pl.pallas_call(
        body,
        out_shape=outs,
        in_specs=[specs[k]() for k in kinds],
        out_specs=jax.tree.map(lambda _: spec_vmem(), outs),
        scratch_shapes=scratch,
        compiler_params=pltpu.CompilerParams(vmem_limit_bytes=VMEM_LIMIT),
        cost_estimate=pl.CostEstimate(flops=micros * 1_000_000_000, bytes_accessed=4_000_000, transcendentals=0),
    )(*inputs)


def shape(dims, dtype):
    return jax.ShapeDtypeStruct(dims, dtype)


CUT_ONE = 512
CUT_TWO = 896
ORDER = ((0, 1, 3, 2), (0, 3, 1, 2))


def hop(v, axis, late):
    pairs = []
    for core in range(2):
        flip = 3 if (core == 1) != late else 1
        for xi in range(4):
            for zi in range(4):
                for yi in range(4):
                    tx, tz, ty = xi, zi, yi
                    if axis == "x":
                        tx = xi ^ flip
                    elif axis == "z":
                        tz = zi ^ flip
                    else:
                        ty = yi ^ flip
                    here = ((core * 4 + xi) * 4 + zi) * 4 + yi
                    pairs.append((here, ((core * 4 + tx) * 4 + tz) * 4 + ty))
    return lax.ppermute(v, ("pipe", "dp", "head"), pairs)


def swap(v):
    return lax.ppermute(v, "pipe", [(0, 1), (1, 0)])


def ring_pair(v, axis):
    low = jnp.stack([v, hop(v, axis, False)])
    return low, hop(low, axis, True)


def ring_rows(v, axis):
    low, high = ring_pair(v, axis)
    both = jnp.concatenate([low, high], axis=0)
    return jnp.moveaxis(both, 0, -3).reshape(v.shape[:-2] + (4 * v.shape[-2], v.shape[-1]))


def ring_stack(v, axis):
    low, high = ring_pair(v, axis)
    return jnp.concatenate([low, high], axis=0)


def gather_one(local):
    rows = ring_rows(local, "z")
    first = ring_rows(rows[:, :CUT_ONE], "x")
    last = ring_stack(rows[:, CUT_ONE:], "y")
    first_pair, last_pair = ring_pair(first, "y"), ring_pair(last, "x")
    return first_pair + last_pair, rows, (first, last), (first_pair[0], last_pair[0])


def gather_two(local, ready):
    rows = ring_rows(local, "x")
    first = ring_stack(rows[:, :CUT_TWO], "y")
    last = ring_rows(rows[:, CUT_TWO:], "z")
    first, last = after((first, last), ready)
    return ring_pair(first, "z") + ring_pair(last, "y")


def half_sums(keep, got):
    onward = (keep[1].astype(F32) + got[1].astype(F32)).astype(keep.dtype)
    return keep[0].astype(F32) + got[0].astype(F32), onward


def ring_begin(keep, send, axis):
    return half_sums(keep, hop(send, axis, True))


def ring_end(begun, axis):
    part, onward = begun
    return part + hop(onward, axis, False).astype(F32)


def ring_sum(keep, send, axis):
    return ring_end(ring_begin(keep, send, axis), axis)


def halves(v):
    rows = v.shape[-2] // 4
    parts = [v[..., rows * n : rows * n + rows, :] for n in range(4)]
    return jnp.stack(parts[:2]), jnp.stack(parts[2:])


def low(v):
    return v.astype(BF16)


def after(v, other):
    return lax.optimization_barrier((v, other))[0]


def lock(*values):
    return lax.optimization_barrier(values)


def send_clip(value, rounds):
    pairs = [(p * 4 + source, p * 4 + target) for p, source, target in rounds]
    return lax.ppermute(value, ("pipe", "head"), pairs)


def spread_near(v):
    return send_clip(v, [(0, 0, 1), (0, 1, 0), (1, 2, 3), (1, 3, 2)])


def spread_far(v, near, y):
    even = (y % 2) == 0
    both = jnp.stack([jnp.where(even, v, near), jnp.where(even, near, v)])
    far = send_clip(both, [(0, 0, 3), (0, 1, 2), (1, 2, 1), (1, 3, 0)])
    return both, far


def own_clips(both, far, pipe, y):
    return jnp.where((y // 2) == pipe, both, far)[:, None]


def token_order():
    order = np.zeros((PT, TOK), np.float32)
    for block in range(4):
        for window in range(WIN):
            row = (window // 10) * 2 + block // 2
            col = (window % 10) * 2 + block % 2
            order[block * PW + window, row * GRID + col] = 1
    return order


def turn_matrix(core_from, core_to, rows_from, rows_to):
    def labels(core, outer):
        out = []
        for a in range(4):
            for b in range(4):
                one, two = ORDER[core][a], ORDER[core][b]
                out.append((one, two) if outer == "x" else (two, one))
        return out

    source, target = labels(core_from, rows_from), labels(core_to, rows_to)
    matrix = np.zeros((384, 384), np.float32)
    for n, label in enumerate(source):
        m = target.index(label)
        matrix[n * 24 : n * 24 + 24, m * 24 : m * 24 + 24] = np.eye(24)
    return jnp.asarray(matrix, BF16)


def per_device(
    clips_in, cotangent, token_mask, memory_valid, memory_one, memory_two,
    qkv_one, out_one, up_one, down_one, up_bias_one, gains_one, shifts_one,
    qkv_two, out_two, res_two, up_two, down_two, up_bias_two, gain_two_in, shift_two_in, gains_two, shifts_two,
):
    pipe = lax.axis_index("pipe")
    dp = lax.axis_index("dp")
    y = lax.axis_index("head")
    x_at, z_at = dp // 4, dp % 4
    first_core = pipe == 0

    place = pipe.astype(jnp.int32).reshape(1)
    shard_one, shard_two = call(
        local_shards,
        (
            place, out_one.T, jnp.transpose(qkv_one, (1, 0, 2)), up_one, down_one.T,
            out_two.T, res_two.T, qkv_two, up_two, down_two.T,
        ),
        "s" + "v" * 9,
        (shape((24, 1152), BF16), shape((24, 1536), BF16)),
        [],
        1,
    )
    mine_one, rows_ready, ready, late = gather_one(shard_one)
    mine_two = gather_two(shard_two, ready)
    other_one = tuple(swap(v) for v in mine_one)

    def clip_of(v, at):
        return lax.dynamic_index_in_dim(v, at, 0, keepdims=False)

    near = jnp.where(first_core, 1, 3)
    far = 4 - near
    biases = jnp.concatenate([up_bias_one, up_bias_two])
    biases = jnp.concatenate(thirds(biases)).reshape(12, 288)
    memory = jnp.concatenate([memory_one[:, 0], memory_two[:, 0]], axis=-1)

    memory, biases = after((memory, biases), rows_ready)

    def payload(flip):
        part = clip_of(memory, y ^ flip).reshape(2 * MEMROWS, 288)
        return jnp.concatenate([part, biases], axis=0)

    got = hop(jnp.stack([payload(near), payload(2)]), "y", False)
    more = hop(jnp.stack([payload(far), got[1]]), "y", True)
    parcels = jnp.stack([payload(0), got[0], more[0], more[1]])
    memory = parcels[:, : 2 * MEMROWS].reshape(4, 2, MEMROWS, 288)
    mem_one, mem_two = memory[..., :96], memory[..., 96:]
    biases = parcels[:, 2 * MEMROWS :].astype(F32).reshape(4, 3, 1152)
    biases = biases[:, 0] + biases[:, 1] + biases[:, 2]
    bias_one, bias_two = biases[:, :384], biases[:, 384:]

    pipe, y, x_at, z_at = after((pipe, y, x_at, z_at), late)
    first_core = pipe == 0

    flags = clip_of(token_mask[:, 0], y).reshape(10, 2, 10, 2)[:, 0, :, 0].reshape(WIN)
    key_ok = (flags > 0).astype(F32)
    mem_ok = jnp.repeat((clip_of(memory_valid[:, 0], y) > 0).astype(F32), MEMROWS // 2)
    gap = jnp.zeros((MEM0 - WIN,), F32)
    tail = jnp.zeros((KEYS - MEM0 - MEMROWS,), F32)
    ok = jnp.concatenate([key_ok, gap, mem_ok, tail]).reshape(1, KEYS)
    fill = np.full((1, KEYS), ABSENT, np.float32)
    fill[0, :WIN] = MASKED
    fill[0, MEM0 : MEM0 + MEMROWS] = MASKED
    fill = jnp.asarray(fill)
    key_col = jnp.concatenate([key_ok, jnp.zeros((PW - WIN,), F32)]).reshape(PW, 1)

    def order_of(core, n):
        return jnp.asarray(ORDER[core], jnp.int32)[n]

    def own_order(n):
        return jnp.where(first_core, order_of(0, n), order_of(1, n))

    k = np.arange(384)
    k_outer, k_inner, k_row = k // 96, (k // 24) % 4, k % 24

    def chip(a, b):
        return (x_at ^ a) * 4 + (z_at ^ b)

    piece0 = chip(order_of(0, k_outer), order_of(0, k_inner))
    piece1 = chip(order_of(1, k_outer), order_of(1, k_inner))
    raw0 = piece0 * 24 + k_row
    raw1 = piece1 * 24 + k_row
    raw2 = jnp.concatenate([piece1 * 48 + k_row, piece1 * 48 + 24 + k_row])
    head_raw = (y ^ own_order(k // 96)) * 96 + k % 96
    j = np.arange(192)
    j_outer, j_inner, j_row = own_order(j // 48), own_order((j // 12) % 4), j % 12
    rows_x = pipe * 192 + chip(j_outer, j_inner) * 12 + j_row
    rows_x2 = pipe * 384 + chip(j_outer, j_inner) * 24 + j_row
    rows_z2 = pipe * 384 + chip(j_inner, j_outer) * 24 + j_row
    pair = np.array([[0], [12]])
    rows_x2 = (rows_x2[None, :] + pair).reshape(384)
    rows_z2 = (rows_z2[None, :] + pair).reshape(384)
    index = [raw0, raw1, raw2, head_raw, rows_x, rows_x2, rows_z2, raw0]
    index = jnp.stack([jnp.pad(v, (0, 768 - v.shape[0])) for v in index]).astype(F32)
    turn = turn_matrix(0, 1, "x", "x")
    to_up = turn_matrix(1, 0, "x", "z")
    to_down = turn_matrix(1, 1, "x", "z")

    order = token_order()
    token_perm = jnp.asarray(order, BF16)
    token_back = jnp.asarray(order.T, BF16)
    vec384 = jnp.concatenate([gains_one, shifts_one, gain_two_in[None], shift_two_in[None]], axis=0)
    gains_in = jnp.concatenate([gain_two_in[None], jnp.zeros((7, 384), F32)], axis=0)
    vec768 = jnp.concatenate([gains_two[None], shifts_two, jnp.zeros((4, 768), F32)], axis=0)
    x = clip_of(clips_in[:, 0], y)
    cot = clip_of(cotangent[:, 0], y)

    x, key_col, vec768, gains_in, bias_two, cot, mem_two = lock(
        x, key_col, vec768, gains_in, bias_two, cot, mem_two
    )
    other_two = tuple(swap(v) for v in mine_two)

    dma = pltpu.SemaphoreType.DMA
    saved = call(
        forward,
        (
            place, x, token_perm, index, turn, vec384, ok, fill, mem_one, mem_two, bias_one,
            *mine_one, *other_one,
        ),
        "s" + "v" * 10 + "a" * 8,
        (
            shape((PT, 384), BF16), shape((PT, 384), BF16),
            shape((4, PT, HEAD), BF16), shape((4, KEYS, HEAD), BF16), shape((4, KEYS, HEAD), BF16),
            shape((4, PT, HEAD), BF16), shape((PT, 384), F32),
            shape((4, PT, 384), BF16), shape((4, PT, 384), BF16),
            shape((PW, 384), BF16), shape((8, PW, HEAD), BF16), shape((8, KEYS, HEAD), BF16),
            shape((8, KEYS, HEAD), BF16), shape((4, PW, 384), BF16), shape((PW, 768), F32),
        ),
        [
            pltpu.VMEM((4, 384, 1152), BF16), pltpu.VMEM((4, 384, 1152), BF16), pltpu.VMEM((8, 384), F32),
            dma(()), dma(()),
        ],
        18,
    )
    passed, x_kept, q1, k1, v1, mix1, mid1, act1, slope1, pn2, q2k, k2, v2, mix2, mid2 = saved

    feed = call(
        feed_two,
        (place, mid2, cot, key_col, index, to_up, to_down, vec768, bias_two, *mine_two, *other_two),
        "s" + "v" * 8 + "a" * 8,
        (
            shape((WIN, 768), BF16), shape((PW, 768), F32), shape((8, 768), F32), shape((4, 768), F32),
            shape((2, 4, 48, 1536), BF16), shape((2, 4, 48, 1536), BF16),
            shape((2, 192, 1536), BF16), shape((2, 192, 1536), BF16),
        ),
        [
            pltpu.VMEM((4, 384, 1536), BF16), pltpu.VMEM((4, 384, 1536), BF16),
            pltpu.VMEM((4, PW, 768), BF16), pltpu.VMEM((4, PW, 768), F32), dma(()), dma(()),
        ],
        14,
    )
    activation, dmid2, vec_mid, dbias_two, keep_rows, send_rows, keep_y, send_y = feed
    got_a = hop(send_rows, "z", True)
    got_b = hop(send_y, "y", True)

    second = call(
        second_backward,
        (
            place, dmid2, passed, pn2, q2k, k2, v2, mix2, index, gains_in, ok, fill,
            *mine_one, *other_one,
        ),
        "s" + "v" * 11 + "a" * 8,
        (
            shape((PT, 384), BF16), shape((8, 384), F32),
            shape((2, 192, 1152), BF16), shape((2, 192, 1152), BF16),
        ),
        [pltpu.VMEM((4, 384, 1152), BF16), pltpu.VMEM((4, 3, PW, 384), BF16), dma(())],
        1,
    )
    dpassed, vec_in, keep_attn, send_attn = second
    attn_got = hop(send_attn, "y", True)

    third = call(
        first_backward,
        (
            place, dpassed, x_kept, q1, k1, v1, mix1, mid1, act1, slope1,
            token_back, index, turn, vec384, ok, fill, vec_mid, vec_in, dbias_two, *mine_one, *other_one,
        ),
        "s" + "v" * 18 + "a" * 8,
        (
            shape((TOK, 384), BF16), shape((12, 768), F32), shape((12, 768), F32),
            shape((2, 4, 48, 1152), BF16), shape((2, 4, 48, 1152), BF16),
        ),
        [
            pltpu.VMEM((4, 384, 1152), BF16), pltpu.VMEM((8, 384), F32), pltpu.VMEM((4, 3, PT, 384), BF16), dma(()),
        ],
        1,
    )
    third, got_a, got_b, attn_got, activation = lock(third, got_a, got_b, attn_got, activation)
    xgrad, vec_keep, vec_send, keep_one, send_one = third

    vectors = vec_keep + hop(vec_send, "y", True)
    act_near = spread_near(activation)
    one_sum = ring_begin(keep_one, send_one, "x")
    feed_a = low(ring_end(half_sums(keep_rows, got_a), "z"))
    feed_b = low(ring_end(half_sums(keep_y, got_b), "y"))
    attn_sum = half_sums(keep_attn, attn_got)
    vectors, attn_sum, one_sum, feed_a, feed_b, xgrad, act_near = lock(
        vectors, attn_sum, one_sum, feed_a, feed_b, xgrad, act_near
    )

    vectors = vectors[:10] + hop(jnp.concatenate([vectors[:8], vectors[10:]], axis=0), "y", False)
    feed_a = ring_begin(feed_a[0:2], feed_a[2:4], "y")
    feed_b = ring_begin(*halves(feed_b), "z")
    attn_sum = low(ring_end(attn_sum, "y"))
    one_sum = low(ring_end(one_sum, "x"))
    vectors, feed_a, feed_b, attn_sum, one_sum, xgrad, act_near = lock(
        vectors, feed_a, feed_b, attn_sum, one_sum, xgrad, act_near
    )

    vectors = vectors + hop(vectors, "x", True)
    feed_a = low(ring_end(feed_a, "y"))
    feed_b = low(ring_end(feed_b, "z"))
    attn_sum = ring_begin(*halves(attn_sum), "x")
    one_sum = ring_begin(one_sum[0:2], one_sum[2:4], "y")
    grad_near = spread_near(xgrad)
    vectors, feed_a, feed_b, attn_sum, one_sum, grad_near, act_near = lock(
        vectors, feed_a, feed_b, attn_sum, one_sum, grad_near, act_near
    )

    vectors = vectors + hop(vectors, "x", False)
    feed_sum = ring_begin(*halves(jnp.concatenate([feed_a, feed_b], axis=1)), "x")
    attn_sum = low(ring_end(attn_sum, "x"))
    one_sum = low(ring_end(one_sum, "y"))
    input_grad = spread_far(xgrad, grad_near, y)
    vectors, feed_sum, attn_sum, one_sum, act_near = lock(vectors, feed_sum, attn_sum, one_sum, act_near)

    feed_part, feed_onward = feed_sum
    feed_got = hop(feed_onward, "x", False)
    activations = spread_far(activation, act_near, y)
    vectors = vectors + hop(vectors, "z", True)
    rest_sum = ring_begin(*halves(jnp.concatenate([one_sum, attn_sum], axis=1)), "z")
    vectors, rest_sum, input_grad, activations, feed_got = lock(
        vectors, rest_sum, input_grad, activations, feed_got
    )
    input_grad = own_clips(*input_grad, pipe, y)
    activations = own_clips(*activations, pipe, y)
    grad_up_two, grad_down_two = call(
        feed_outputs,
        (feed_part, feed_got),
        "vv",
        (shape((24, 768), F32), shape((24, 768), F32)),
        [],
        2,
    )

    rest_part, rest_onward = rest_sum
    vectors_got = hop(vectors, "z", False)
    rest_got = hop(rest_onward, "z", False)
    outs = call(
        last_outputs,
        (rest_part, rest_got, vectors, vectors_got),
        "vvvv",
        (
            shape((12, 1, 288), F32), shape((12, 96), F32), shape((12, 384), F32), shape((12, 384), F32),
            shape((384,), F32), shape((2, 384), F32), shape((4, 384), F32),
            shape((12, 2, 288), F32), shape((24, 192), F32), shape((24, 96), F32),
            shape((768,), F32), shape((384,), F32), shape((384,), F32), shape((768,), F32),
            shape((3, 768), F32),
        ),
        [],
        2,
    )
    return (
        activations,
        input_grad,
        outs[0],
        outs[1].T,
        outs[2],
        outs[3].T,
        *outs[4:8],
        outs[8].T,
        outs[9].T,
        grad_up_two,
        grad_down_two.T,
        *outs[10:15],
    )


def solution(mesh):
    return jax.shard_map(
        per_device,
        mesh=mesh,
        in_specs=(
            P(None, "dp", None, None), P(None, "dp", None, None), P(None, "dp", None), P(None, "dp", None),
            P(None, "dp", None, None, "head"), P(None, "dp", None, None, "head"),
            P("dp", "head", None), P("head", "dp"), P("dp", "head"), P("head", "dp"), P("head"), P(), P(),
            P("dp", "head", None), P("head", "dp"), P("head", "dp"), P("dp", "head"), P("head", "dp"), P("head"),
            P(), P(), P(), P(),
        ),
        out_specs=(
            P("pipe", "dp", None, None), P("pipe", "dp", None, None),
            P(("pipe", "dp"), "head", None), P("head", ("pipe", "dp")), P(("pipe", "dp"), "head"),
            P("head", ("pipe", "dp")), P("head"), P(), P(),
            P(("pipe", "dp"), "head", None), P("head", ("pipe", "dp")), P("head", ("pipe", "dp")),
            P(("pipe", "dp"), "head"), P("head", ("pipe", "dp")), P("head"), P(), P(), P(), P(),
        ),
        check_vma=False,
    )
```
